32 devices in a mesh: dp: 2 (over core), expert: 16 (over z, y, x).
Axes of the slice: x: 2, y: 2, z: 4, core: 2. Of those that a mesh axis runs over, the one named last changes fastest.
Arguments:
- hidden_in: bfloat16 [6144, 2048], P(('dp', 'expert')), may hold values from -6 to 6
- cotangent: bfloat16 [6144, 2048], P(('dp', 'expert')), may hold values from -6 to 6
- doc_ids: int32 [32, 192], P(('dp', 'expert')), may hold values from 0 to 3, never falling along the last dimension, each value on 1 to 96 neighbouring positions
- routes: int32 [6144, 8], P(('dp', 'expert')), may hold values from 0 to 15, all different within a row; in each aligned block of 192 rows (0 to 191, 192 to 383, ...) at most 128 rows name the same one
- attn_gain: float32 [2048], replicated, may hold values from 0.5 to 1.5
- w_query: bfloat16 [2048, 2048], P(('dp', 'expert')), may hold values from -0.125 to 0.125
- w_key: bfloat16 [2048, 2048], P(('dp', 'expert')), may hold values from -0.125 to 0.125
- w_value: bfloat16 [2048, 2048], P(('dp', 'expert')), may hold values from -0.125 to 0.125
- query_gain: float32 [2048], replicated, may hold values from 0.5 to 1.5
- key_gain: float32 [2048], replicated, may hold values from 0.5 to 1.5
- w_output: bfloat16 [2048, 2048], P(('dp', 'expert')), may hold values from -0.375 to 0.375
- moe_gain: float32 [2048], replicated, may hold values from 0.5 to 1.5
- w_router: bfloat16 [2048, 16], P(('dp', 'expert')), may hold values from -0.0625 to 0.0625
- w_gate: bfloat16 [16, 2048, 1024], P('expert'), may hold values from -0.125 to 0.125
- w_up: bfloat16 [16, 2048, 1024], P('expert'), may hold values from -0.125 to 0.125
- w_down: bfloat16 [16, 1024, 2048], P('expert'), may hold values from -4 to 4
Outputs:
- block_out: bfloat16 [6144, 2048], P(('dp', 'expert'))
- input_grad: bfloat16 [6144, 2048], P(('dp', 'expert'))
- grad_attn_gain: float32 [2048], P(('dp', 'expert'))
- grad_query: float32 [2048, 2048], P(('dp', 'expert'))
- grad_key: float32 [2048, 2048], P(('dp', 'expert'))
- grad_value: float32 [2048, 2048], P(('dp', 'expert'))
- grad_query_gain: float32 [2048], P(('dp', 'expert'))
- grad_key_gain: float32 [2048], P(('dp', 'expert'))
- grad_output: float32 [2048, 2048], P(('dp', 'expert'))
- grad_moe_gain: float32 [2048], P(('dp', 'expert'))
- grad_router: float32 [2048, 16], P(('dp', 'expert'))
- grad_gate: float32 [16, 2048, 1024], P('expert', None, 'dp')
- grad_up: float32 [16, 2048, 1024], P('expert', None, 'dp')
- grad_down: float32 [16, 1024, 2048], P('expert', 'dp')
The draws below stay inside these ranges and needn't reach their ends.
Inputs may be any that keep to these rules, and one draw needn't show every extreme that they name: `routes`: each row names 8 different experts. Among the rows of one device no expert is named more than 128 times, and in some device's rows one expert is named exactly 128 times. `doc_ids`: along each row of 192 positions the numbers never fall; a document has at most 96 positions, and one has exactly that many.
All inputs are finite; a program needn't handle non-finite values.
Results may differ from the reference program's by a relative error of at most 0.019.
Values may be sent and summed in bfloat16 or wider, within the bound.
No kernel may reach another device: no remote copies, remote signals or barrier semaphores. Data moves between devices by JAX's collectives and lax.ppermute only.
A program may use at most 256 MiB of HBM per device.

```python
import math
import jax
import jax.numpy as jnp
import numpy as np
from jax import lax

D = 2048
HEADS = 16
HD = 128
FF = 1024
TOPK = 8
DOCS = 4
TOK_DEV = 192
EXPERTS = 16
CAP = 128
SEQS = 32
TOKENS = 6144


def level_of(key, dims, pieces, least, high):
    factor_of, own = 1.0, jax.random.fold_in(key, 6)
    for dim, parts in pieces:
        steps = jnp.exp(jax.random.uniform(jax.random.fold_in(own, dim), (parts,), jnp.float32, least / len(pieces), high / len(pieces)))
        factor_of = factor_of * jnp.repeat(steps, dims[dim] // parts).reshape([-1 if axis == dim else 1 for axis in range(len(dims))])
    return factor_of


def split_up(number_of, total, reach, lean):
    portions = [(1 << 20) // math.isqrt(grade ** lean) + 1 for grade in range(2, number_of + 1)]
    rest, given = total - reach - (number_of - 1), [1] * (number_of - 1)
    while rest > 0:
        candidates = [i for i in range(number_of - 1) if given[i] < reach]
        mass, remaining = sum([portions[i] for i in candidates]), rest
        for i in candidates:
            more = min(reach - given[i], max(1, remaining * portions[i] // mass), rest)
            given[i] = given[i] + more
            rest = rest - more
    return np.array([reach] + given)


def ragged(rng, number_of, total, bound, lean):
    if number_of == 2:
        one = jax.random.randint(rng, (), max(1, total - bound), min(bound, total - 1) + 1)
        return jnp.stack([one, total - one])
    lengths = jnp.asarray(split_up(number_of, total, bound, lean), jnp.int32)
    twos = (number_of - 1) // 2
    giver, sink = lengths[1:1 + 2 * twos:2], lengths[2:2 + 2 * twos:2]
    room = jnp.minimum(giver - 1, bound - sink)
    passed = jax.random.randint(jax.random.fold_in(rng, 1), (twos,), 0, 1 << 20) % (room + 1)
    lengths = lengths.at[1:1 + 2 * twos:2].set(giver - passed).at[2:2 + 2 * twos:2].set(sink + passed)
    return lengths[jax.random.permutation(jax.random.fold_in(rng, 2), number_of)]


def shared_out(key, own, number, rows, number_of, top, most, slope):
    ranking = jax.random.permutation(key, number_of)
    heavy_load, usual = shares(number_of, rows * top, most, slope, True), shares(number_of, rows * top, most, slope, False)
    places = jnp.arange(number_of)

    def named(lengths, turn):
        used = int((lengths > 0).sum())
        fixed = max(1, used // 4)
        passed = fixed + (places - fixed + turn * (used - fixed)) % max(1, number_of - fixed)
        return jnp.zeros((number_of,), jnp.int32).at[ranking[jnp.where(places < fixed, places, passed)]].set(jnp.asarray(lengths, jnp.int32))

    lengths = jnp.where(number % 4 == 0, named(heavy_load, number // 4), named(usual, number - number // 4 - 1))
    mixed = jax.random.permutation(jax.random.fold_in(own, 3), number_of)
    source_of, taker = mixed[0:number_of // 2 * 2:2], mixed[1:number_of // 2 * 2:2]
    room = jnp.minimum(lengths[source_of] - 1, most - lengths[taker]) // 2
    room = jnp.where((source_of == ranking[0]) | (taker == ranking[0]) | (lengths[taker] == 0), 0, jnp.maximum(room, 0))
    passed = jax.random.randint(jax.random.fold_in(own, 4), (number_of // 2,), 0, 1 << 20) % (room + 1)
    lengths = lengths.at[source_of].add(-passed).at[taker].add(passed)
    members = jnp.searchsorted(jnp.cumsum(lengths), jnp.arange(rows * top), side="right").astype(jnp.int32)
    grid = members.reshape(top, rows).T
    grid = grid[jax.random.permutation(jax.random.fold_in(own, 1), rows)]
    turn = jax.random.randint(jax.random.fold_in(own, 2), (rows, 1), 0, top)
    return jnp.take_along_axis(grid, (jnp.arange(top)[None, :] + turn) % top, axis=1)


def shares(amount, total, reach, lean, full):
    portions = [(1 << 20) // math.isqrt(grade ** lean) + 1 for grade in range(1, amount + 1)]
    largest = reach if full else min(reach, max(-(-total // amount), total * portions[0] // sum(portions)))
    least = 1 if total - largest >= amount - 1 else 0
    holding, surplus = [largest] + [least] * (amount - 1), total - largest - least * (amount - 1)
    while surplus > 0:
        free = [i for i in range(1, amount) if holding[i] < largest] or [i for i in range(1, amount) if holding[i] < reach]
        whole, left = sum([portions[i] for i in free]), surplus
        for i in free:
            extra = min(reach - holding[i], max(1, left * portions[i] // whole), surplus)
            holding[i] = holding[i] + extra
            surplus = surplus - extra
    return np.array(holding)


def noise(key, extent, scale, limit, split=(), kind=jnp.bfloat16):
    entries = scale * jax.random.normal(key, extent, jnp.float32)
    if split:
        entries = entries * level_of(key, extent, split, -0.22, 0.18)
    return jnp.clip(entries, -limit, limit).astype(kind)


def setup_inputs(seed: int = 0) -> dict:
    keys = jax.random.split(jax.random.key(seed), 17)
    hidden_in = noise(keys[0], (TOKENS, D), 1.0, 6.0, ((0, 32),))
    cotangent = noise(keys[1], (TOKENS, D), 1.0, 6.0, ((0, 32),))
    doc_ids = jax.vmap(lambda own: jnp.searchsorted(jnp.cumsum(ragged(own, DOCS, TOK_DEV, TOK_DEV // 2, 1)), jnp.arange(TOK_DEV), side="right"))(jax.random.split(keys[2], SEQS)).reshape((SEQS, TOK_DEV)).astype(jnp.int32)
    routes_keys = jax.random.split(jax.random.fold_in(keys[3], 1), TOKENS // TOK_DEV)
    routes_turns = jax.random.permutation(jax.random.fold_in(keys[3], 3), TOKENS // TOK_DEV)
    routes = jax.vmap(lambda own, number: shared_out(jax.random.fold_in(keys[3], 2), own, number, TOK_DEV, EXPERTS, TOPK, CAP, 2))(routes_keys, routes_turns).reshape((TOKENS, TOPK))
    attn_gain = jnp.clip(1.0 + 0.1 * jax.random.normal(keys[4], (D,), jnp.float32), 0.5, 1.5)
    w_query = noise(keys[5], (D, D), D ** -0.5, 0.125, ((0, 32),))
    w_key = noise(keys[6], (D, D), D ** -0.5, 0.125, ((0, 32),))
    w_value = noise(keys[7], (D, D), D ** -0.5, 0.125, ((0, 32),))
    query_gain = jnp.clip(1.0 + 0.1 * jax.random.normal(keys[8], (D,), jnp.float32), 0.5, 1.5)
    key_gain = jnp.clip(1.0 + 0.1 * jax.random.normal(keys[9], (D,), jnp.float32), 0.5, 1.5)
    w_output = noise(keys[10], (D, D), (D // 8) ** -0.5, 0.375, ((0, 32),))
    moe_gain = jnp.clip(1.0 + 0.1 * jax.random.normal(keys[11], (D,), jnp.float32), 0.5, 1.5)
    w_router = noise(keys[12], (D, EXPERTS), (4 * D) ** -0.5, 0.0625, ((0, 32),))
    w_gate = noise(keys[13], (EXPERTS, D, FF), D ** -0.5, 0.125, ((0, 16),))
    w_up = noise(keys[14], (EXPERTS, D, FF), D ** -0.5, 0.125, ((0, 16),))
    w_down = noise(keys[15], (EXPERTS, FF, D), (max(FF // 512, 1)) ** -0.5, 4.0, ((0, 16),))
    return dict(hidden_in=hidden_in, cotangent=cotangent, doc_ids=doc_ids, routes=routes, attn_gain=attn_gain, w_query=w_query, w_key=w_key, w_value=w_value, query_gain=query_gain, key_gain=key_gain, w_output=w_output, moe_gain=moe_gain, w_router=w_router, w_gate=w_gate, w_up=w_up, w_down=w_down)


EPSILON = 1e-05
HIGHEST = lax.Precision.HIGHEST

@jax.custom_vjp
def low(v):
    return lax.optimization_barrier(v.astype(jnp.bfloat16)).astype(jnp.float32)

@jax.custom_vjp
def low_back(v):
    return v

def low_keep(v):
    return (low(v), None)

def low_pass(kept, grad):
    return (grad,)

def back_keep(v):
    return (v, None)

def back_low(kept, grad):
    return (low(grad),)
low.defvjp(low_keep, low_pass)
low_back.defvjp(back_keep, back_low)

def matmul_hi(left, right):
    return jnp.dot(left, right, precision=HIGHEST)

def rms_norm(values, gain_vector):
    return values * lax.rsqrt(lax.optimization_barrier(jnp.mean(values * values, axis=-1, keepdims=True)) + EPSILON) * gain_vector

def rotary_tables(length):
    half_dim = HD // 2
    frequency = 10000.0 ** (-jnp.arange(half_dim, dtype=jnp.float32) * 2.0 / HD)
    angles = jnp.arange(length, dtype=jnp.float32)[:, None] * frequency[None, :]
    angles = jnp.concatenate([angles, angles], axis=1)
    return (jnp.cos(angles)[:, None, :], jnp.sin(angles)[:, None, :])

def rotate(values, cosine, sine_table):
    half_dim = values.shape[-1] // 2
    turned = jnp.concatenate([-values[..., half_dim:], values[..., :half_dim]], axis=-1)
    return values * cosine + turned * sine_table

def expert_rows(routes):
    flat_routes = routes.reshape(-1).astype(jnp.int32)
    pair_count = flat_routes.shape[0]
    sorted_pairs = jnp.argsort(flat_routes, stable=True).astype(jnp.int32)
    expert_ids = jnp.arange(EXPERTS, dtype=jnp.int32)
    counts = lax.optimization_barrier(jnp.sum((flat_routes[:, None] == expert_ids[None, :]).astype(jnp.int32), axis=0)).astype(jnp.int32)
    starts = (jnp.cumsum(counts) - counts).astype(jnp.int32)
    most_rows = CAP * (TOKENS // TOK_DEV)
    padded = jnp.concatenate([sorted_pairs, jnp.full((most_rows,), pair_count, jnp.int32)])

    def pick_rows(expert_id):
        row_ids = lax.dynamic_slice_in_dim(padded, starts[expert_id], most_rows)
        is_live = jnp.arange(most_rows, dtype=jnp.int32) < counts[expert_id]
        return jnp.where(is_live, row_ids, pair_count).astype(jnp.int32)
    return jax.vmap(pick_rows)(expert_ids)

def forward_block(hidden, attn_gain, w_query, w_key, w_value, query_gain, key_gain, w_output, moe_gain, w_router, w_gate, w_up, w_down, doc_ids, routes, row_index):
    act_attn = low(rms_norm(hidden, attn_gain))
    query_pre = low_back(matmul_hi(act_attn, w_query))
    key_pre = low_back(matmul_hi(act_attn, w_key))
    value = low(low_back(matmul_hi(act_attn, w_value)))
    seq_count = hidden.shape[0] // TOK_DEV
    head_shape = (seq_count, TOK_DEV, HEADS, HD)
    cosine, sine_table = rotary_tables(TOK_DEV)
    query_rot = low(rotate(rms_norm(query_pre, query_gain).reshape(head_shape), cosine, sine_table))
    key_rot = low(rotate(rms_norm(key_pre, key_gain).reshape(head_shape), cosine, sine_table))
    value_heads = value.reshape(head_shape)
    scores = low_back(jnp.einsum('sqhd,skhd->shqk', query_rot, key_rot, precision=HIGHEST) * HD ** (-0.5))
    position = jnp.arange(TOK_DEV, dtype=jnp.int32)
    allowed = (position[None, :, None] >= position[None, None, :]) & (doc_ids[:, :, None] == doc_ids[:, None, :])
    scores = jnp.where(allowed[:, None], scores, -1e+30)
    probs_low = low(jax.nn.softmax(scores, axis=-1))
    attended = jnp.einsum('shqk,skhd->sqhd', probs_low, value_heads, precision=HIGHEST).reshape(hidden.shape)
    attended = low(low_back(attended))
    middle = hidden + low_back(matmul_hi(attended, w_output))
    act_moe = low(rms_norm(middle, moe_gain))
    logits = low_back(matmul_hi(act_moe, w_router))
    router_probs = jax.nn.softmax(logits, axis=-1)
    gate_values = jnp.take_along_axis(router_probs, routes, axis=1)
    pair_count = routes.shape[0] * routes.shape[1]
    token_of = jnp.minimum(row_index // TOPK, hidden.shape[0] - 1)

    def one_expert(inputs):
        token_rows, weight_gate, weight_up, weight_down = inputs
        expert_in = low_back(act_moe[token_rows])
        gate_pre = low_back(matmul_hi(expert_in, weight_gate))
        up_pre = low_back(matmul_hi(expert_in, weight_up))
        hid = low(jax.nn.silu(gate_pre) * up_pre)
        return low(low_back(matmul_hi(hid, weight_down)))
    expert_out = lax.map(jax.checkpoint(one_expert), (token_of, w_gate, w_up, w_down))
    pair_out = jnp.zeros((pair_count, hidden.shape[1]), hidden.dtype)
    pair_out = pair_out.at[row_index.reshape(-1)].set(expert_out.reshape(-1, hidden.shape[1]), mode='drop')
    moe_term = lax.optimization_barrier(jnp.sum(gate_values[..., None] * pair_out.reshape(hidden.shape[0], TOPK, hidden.shape[1]), axis=1))
    return middle + moe_term

def reference(hidden_in, cotangent, doc_ids, routes, attn_gain, w_query, w_key, w_value, query_gain, key_gain, w_output, moe_gain, w_router, w_gate, w_up, w_down):
    row_index = expert_rows(routes)
    floats = [hidden_in, attn_gain, w_query, w_key, w_value, query_gain, key_gain, w_output, moe_gain, w_router, w_gate, w_up, w_down]
    floats = [entry.astype(jnp.float32) for entry in floats]

    def block_fn(*weights):
        return forward_block(*weights, doc_ids, routes, row_index)
    result, pull_back = jax.vjp(block_fn, *floats)
    grads = pull_back(cotangent.astype(jnp.float32))
    return (result.astype(jnp.bfloat16), grads[0].astype(jnp.bfloat16), grads[1], grads[2], grads[3], grads[4], grads[5], grads[6], grads[7], grads[8], grads[9], grads[10], grads[11], grads[12])
```

```python
import functools

import jax
import jax.numpy as jnp
from jax import lax
from jax.experimental import pallas as pl
from jax.experimental.pallas import tpu as pltpu
from jax.sharding import PartitionSpec as P

HD = 128


EPSILON = 1e-05


def norm_forward(values, gain_vector):
    inverse = lax.rsqrt(jnp.mean(values * values, axis=-1, keepdims=True) + EPSILON)
    return (values * inverse * gain_vector, inverse)


def norm_backward(values, inverse, gain_vector, upstream):
    gain_grad = jnp.sum(upstream * values * inverse, axis=0)
    scaled = upstream * gain_vector
    inner_mean = jnp.mean(scaled * values, axis=-1, keepdims=True)
    return (inverse * (scaled - values * inner_mean * inverse * inverse), gain_grad)


def rotary_tables(length, head_dim):
    half_dim = head_dim // 2
    frequency = 10000.0 ** (-jnp.arange(half_dim, dtype=jnp.float32) * 2.0 / head_dim)
    angles = jnp.arange(length, dtype=jnp.float32)[:, None] * frequency[None, :]
    angles = jnp.concatenate([angles, angles], axis=1)
    return (jnp.cos(angles)[:, None, :], jnp.sin(angles)[:, None, :])


def rotate(values, cosine, sine_table):
    half_dim = values.shape[-1] // 2
    turned = jnp.concatenate([-values[..., half_dim:], values[..., :half_dim]], axis=-1)
    return values * cosine + turned * sine_table


def rotate_back(upstream, cosine, sine_table):
    half_dim = upstream.shape[-1] // 2
    with_sine = upstream * sine_table
    turned = jnp.concatenate([with_sine[..., half_dim:], -with_sine[..., :half_dim]], axis=-1)
    return upstream * cosine + turned


def times_transposed(left, right):
    return jnp.einsum("ta,ba->tb", left, right, preferred_element_type=jnp.float32)


def inner_product(left, right):
    return jnp.einsum("ta,tb->ab", left, right, preferred_element_type=jnp.float32)


def body_routed(
    hidden_in,
    cotangent,
    doc_ids,
    routes,
    attn_gain,
    w_query,
    w_key,
    w_value,
    query_gain,
    key_gain,
    w_output,
    moe_gain,
    w_router,
    w_gate,
    w_up,
    w_down,
):
    f32 = jnp.float32
    bf16 = jnp.bfloat16
    tokens_here = hidden_in.shape[0]
    model_width = hidden_in.shape[1]
    head_dim = HD
    head_count = model_width // head_dim
    top_count = routes.shape[1]
    experts_all = w_router.shape[1]
    capacity = tokens_here * top_count * 4 // (3 * experts_all)
    local_experts = w_gate.shape[0]
    owners = lax.axis_size("expert")
    full_query, full_key, full_value, full_output, full_router = (
        lax.all_gather(w_query, ("dp", "expert"), axis=0, tiled=True),
        lax.all_gather(w_key, ("dp", "expert"), axis=0, tiled=True),
        lax.all_gather(w_value, ("dp", "expert"), axis=0, tiled=True),
        lax.all_gather(w_output, ("dp", "expert"), axis=0, tiled=True),
        lax.all_gather(w_router, ("dp", "expert"), axis=0, tiled=True),
    )
    inputs_f32 = hidden_in.astype(f32)
    normed_attn, inverse_attn = norm_forward(inputs_f32, attn_gain)
    act_attn = normed_attn.astype(bf16)
    query_pre = jnp.dot(act_attn, full_query, preferred_element_type=f32)
    key_pre = jnp.dot(act_attn, full_key, preferred_element_type=f32)
    value_low = jnp.dot(act_attn, full_value, preferred_element_type=f32).astype(bf16)
    query_normed, query_inverse = norm_forward(query_pre, query_gain)
    key_normed, key_inverse = norm_forward(key_pre, key_gain)
    cosine, sine_table = rotary_tables(tokens_here, head_dim)
    head_shape = (tokens_here, head_count, head_dim)
    query_rot = rotate(query_normed.reshape(head_shape), cosine, sine_table).astype(bf16)
    key_rot = rotate(key_normed.reshape(head_shape), cosine, sine_table).astype(bf16)
    value_heads = value_low.reshape(head_shape)
    score_scale = head_dim ** (-0.5)
    position = jnp.arange(tokens_here, dtype=jnp.int32)
    allowed = (position[:, None] >= position[None, :]) & (
        doc_ids[0][:, None] == doc_ids[0][None, :]
    )

    def masked_scores():
        scores = (
            jnp.einsum("qhd,khd->hqk", query_rot, key_rot, preferred_element_type=f32) * score_scale
        )
        return jnp.where(allowed[None], scores, -1e30)

    scores = masked_scores()
    row_max = jnp.max(scores, axis=-1, keepdims=True)
    row_sum = jnp.sum(jnp.exp(scores - row_max), axis=-1, keepdims=True)
    log_total = row_max + jnp.log(row_sum)
    probs_low = jnp.exp(scores - log_total).astype(bf16)
    attended = jnp.einsum("hqk,khd->qhd", probs_low, value_heads, preferred_element_type=f32)
    attended_low = attended.reshape(tokens_here, model_width).astype(bf16)
    middle = inputs_f32 + jnp.dot(attended_low, full_output, preferred_element_type=f32)
    normed_moe, inverse_moe = norm_forward(middle, moe_gain)
    act_moe = normed_moe.astype(bf16)
    logits = jnp.dot(act_moe, full_router, preferred_element_type=f32)
    router_probs = jax.nn.softmax(logits, axis=-1)
    expert_ids = jnp.arange(experts_all, dtype=jnp.int32)
    chosen = routes[:, :, None] == expert_ids[None, None, :]
    gate_values = jnp.sum(jnp.where(chosen, router_probs[:, None, :], 0.0), axis=-1)
    flat_routes = routes.reshape(-1)
    onehot = (flat_routes[:, None] == expert_ids[None, :]).astype(jnp.int32)
    slot_of = jnp.sum((jnp.cumsum(onehot, axis=0) - 1) * onehot, axis=1)
    target_slot = flat_routes * capacity + slot_of
    pair_token = jnp.arange(tokens_here * top_count, dtype=jnp.int32) // top_count

    def to_experts(pair_rows):
        buffer = (
            jnp.zeros((experts_all * capacity, model_width), bf16).at[target_slot].set(pair_rows)
        )
        return buffer.reshape(experts_all, capacity, model_width)

    def from_experts(buffer):
        return buffer.reshape(experts_all * capacity, model_width)[target_slot]

    received = lax.all_to_all(
        to_experts(act_moe[pair_token]), "expert", split_axis=0, concat_axis=0, tiled=True
    )
    owner_rows = received.reshape(owners, local_experts, capacity, model_width)
    gate_pre = jnp.einsum("secd,edf->secf", owner_rows, w_gate, preferred_element_type=f32)
    up_pre = jnp.einsum("secd,edf->secf", owner_rows, w_up, preferred_element_type=f32)
    sigmoid = jax.nn.sigmoid(gate_pre)
    swish = gate_pre * sigmoid
    hidden_low = (swish * up_pre).astype(bf16)
    expert_out = jnp.einsum(
        "secf,efd->secd", hidden_low, w_down, preferred_element_type=f32
    ).astype(bf16)
    returned = lax.all_to_all(
        expert_out.reshape(owners * local_experts, capacity, model_width),
        "expert",
        split_axis=0,
        concat_axis=0,
        tiled=True,
    )
    pair_out = from_experts(returned).reshape(tokens_here, top_count, model_width).astype(f32)
    moe_term = jnp.sum(gate_values[:, :, None] * pair_out, axis=1)
    block_out = (middle + moe_term).astype(bf16)
    upstream = cotangent.astype(f32)
    pair_grad = (gate_values[:, :, None] * upstream[:, None, :]).astype(bf16)
    gate_grad = jnp.sum(upstream[:, None, :] * pair_out, axis=-1)
    out_grad = lax.all_to_all(
        to_experts(pair_grad.reshape(-1, model_width)),
        "expert",
        split_axis=0,
        concat_axis=0,
        tiled=True,
    )
    out_grad = out_grad.reshape(owners, local_experts, capacity, model_width)
    hidden_grad = jnp.einsum("secd,efd->secf", out_grad, w_down, preferred_element_type=f32)
    down_grad = jnp.einsum("secf,secd->efd", hidden_low, out_grad, preferred_element_type=f32)
    slope = sigmoid * (1.0 + gate_pre * (1.0 - sigmoid))
    gate_pre_grad = (hidden_grad * up_pre * slope).astype(bf16)
    up_pre_grad = (hidden_grad * swish).astype(bf16)
    row_grad = jnp.einsum("secf,edf->secd", gate_pre_grad, w_gate, preferred_element_type=f32)
    row_grad = (
        row_grad + jnp.einsum("secf,edf->secd", up_pre_grad, w_up, preferred_element_type=f32)
    ).astype(bf16)
    gate_weight_grad = jnp.einsum(
        "secd,secf->edf", owner_rows, gate_pre_grad, preferred_element_type=f32
    )
    up_weight_grad = jnp.einsum(
        "secd,secf->edf", owner_rows, up_pre_grad, preferred_element_type=f32
    )
    gate_weight_grad, up_weight_grad, down_grad = (
        lax.psum_scatter(
            gate_weight_grad.astype(jnp.bfloat16), "dp", scatter_dimension=2, tiled=True
        ).astype(jnp.float32),
        lax.psum_scatter(
            up_weight_grad.astype(jnp.bfloat16), "dp", scatter_dimension=2, tiled=True
        ).astype(jnp.float32),
        lax.psum_scatter(
            down_grad.astype(jnp.bfloat16), "dp", scatter_dimension=1, tiled=True
        ).astype(jnp.float32),
    )
    back_rows = lax.all_to_all(
        row_grad.reshape(owners * local_experts, capacity, model_width),
        "expert",
        split_axis=0,
        concat_axis=0,
        tiled=True,
    )
    moe_in_grad = jnp.sum(
        from_experts(back_rows).reshape(tokens_here, top_count, model_width).astype(f32), axis=1
    )
    choice_grad = jnp.sum(jnp.where(chosen, gate_grad[:, :, None], 0.0), axis=1)
    logit_grad = router_probs * (
        choice_grad - jnp.sum(router_probs * choice_grad, axis=-1, keepdims=True)
    )
    logit_low = logit_grad.astype(bf16)
    moe_in_grad = moe_in_grad + times_transposed(logit_low, full_router)
    router_grad = inner_product(act_moe, logit_low)
    mid_norm_grad, moe_gain_grad = norm_backward(middle, inverse_moe, moe_gain, moe_in_grad)
    mid_grad = upstream + mid_norm_grad
    mid_low = mid_grad.astype(bf16)
    output_grad = inner_product(attended_low, mid_low)
    attended_grad = times_transposed(mid_low, full_output).astype(bf16).reshape(head_shape)
    probs = jnp.exp(masked_scores() - log_total)
    probs_grad = jnp.einsum("qhd,khd->hqk", attended_grad, value_heads, preferred_element_type=f32)
    row_inner = jnp.sum(probs * probs_grad, axis=-1, keepdims=True)
    scores_grad = (probs * (probs_grad - row_inner)).astype(bf16)
    query_rot_grad = (
        jnp.einsum("hqk,khd->qhd", scores_grad, key_rot, preferred_element_type=f32) * score_scale
    )
    key_rot_grad = (
        jnp.einsum("hqk,qhd->khd", scores_grad, query_rot, preferred_element_type=f32) * score_scale
    )
    value_grad = jnp.einsum("hqk,qhd->khd", probs_low, attended_grad, preferred_element_type=f32)
    value_grad = value_grad.reshape(tokens_here, model_width).astype(bf16)
    query_back = rotate_back(query_rot_grad, cosine, sine_table).reshape(tokens_here, model_width)
    key_back = rotate_back(key_rot_grad, cosine, sine_table).reshape(tokens_here, model_width)
    query_pre_grad, query_gain_grad = norm_backward(
        query_pre, query_inverse, query_gain, query_back
    )
    key_pre_grad, key_gain_grad = norm_backward(key_pre, key_inverse, key_gain, key_back)
    query_low = query_pre_grad.astype(bf16)
    key_low = key_pre_grad.astype(bf16)
    act_grad = (
        times_transposed(query_low, full_query)
        + times_transposed(key_low, full_key)
        + times_transposed(value_grad, full_value)
    )
    query_weight_grad = inner_product(act_attn, query_low)
    key_weight_grad = inner_product(act_attn, key_low)
    value_weight_grad = inner_product(act_attn, value_grad)
    input_norm_grad, attn_gain_grad = norm_backward(inputs_f32, inverse_attn, attn_gain, act_grad)
    input_grad = (mid_grad + input_norm_grad).astype(bf16)
    sharded_grads = (
        lax.psum_scatter(attn_gain_grad, ("dp", "expert"), scatter_dimension=0, tiled=True),
        lax.psum_scatter(query_weight_grad, ("dp", "expert"), scatter_dimension=0, tiled=True),
        lax.psum_scatter(key_weight_grad, ("dp", "expert"), scatter_dimension=0, tiled=True),
        lax.psum_scatter(value_weight_grad, ("dp", "expert"), scatter_dimension=0, tiled=True),
        lax.psum_scatter(query_gain_grad, ("dp", "expert"), scatter_dimension=0, tiled=True),
        lax.psum_scatter(key_gain_grad, ("dp", "expert"), scatter_dimension=0, tiled=True),
        lax.psum_scatter(output_grad, ("dp", "expert"), scatter_dimension=0, tiled=True),
        lax.psum_scatter(moe_gain_grad, ("dp", "expert"), scatter_dimension=0, tiled=True),
        lax.psum_scatter(router_grad, ("dp", "expert"), scatter_dimension=0, tiled=True),
    )
    return (
        block_out,
        input_grad,
        sharded_grads[0],
        sharded_grads[1],
        sharded_grads[2],
        sharded_grads[3],
        sharded_grads[4],
        sharded_grads[5],
        sharded_grads[6],
        sharded_grads[7],
        sharded_grads[8],
        gate_weight_grad,
        up_weight_grad,
        down_grad,
    )


NZ, NY, NX = 4, 2, 2
VMEM_LIMIT = 48 * 1024 * 1024


def chip(z, y, x):
    return (z * NY + y) * NX + x


GRID = [(z, y, x) for z in range(NZ) for y in range(NY) for x in range(NX)]
X_PAIRS = [(chip(z, y, x), chip(z, y, 1 - x)) for z, y, x in GRID]
Y_PAIRS = [(chip(z, y, x), chip(z, 1 - y, x)) for z, y, x in GRID]
Z_PAIRS = [(chip(z, y, x), chip((z + 1) % NZ, y, x)) for z, y, x in GRID]
CORE_PAIRS = [(0, 1), (1, 0)]


def move_x(values):
    return lax.ppermute(values, "expert", X_PAIRS)


def move_y(values):
    return lax.ppermute(values, "expert", Y_PAIRS)


def move_z(values):
    return lax.ppermute(values, "expert", Z_PAIRS)


def move_core(values):
    return lax.ppermute(values, "dp", CORE_PAIRS)


def split_row(rows):
    return (rows // 2 + 15) // 16 * 16


def gather_z(block):
    ring = [block]
    for _ in range(1, NZ):
        ring.append(move_z(ring[-1]))
    return ring


def gather_plane(block):
    cut = split_row(block.shape[0])
    from_x = move_x(block)
    from_y = move_y(block)
    across = jnp.concatenate([move_x(from_y[:cut]), move_y(from_x[cut:])], axis=0)
    return [block, from_x, from_y, across]


def gather_chips(block):
    return [gather_plane(part) for part in gather_z(block)]


def add_f32(left, right):
    return left.astype(jnp.float32) + right.astype(jnp.float32)


def reduce_plane(parts):
    own, for_x, for_y, for_across = parts
    low = own.dtype
    cut = split_row(own.shape[0])
    by_x = move_x(for_across[:cut])
    by_y = move_y(for_across[cut:])
    for_y = jnp.concatenate([add_f32(for_y[:cut], by_x).astype(low), for_y[cut:]], axis=0)
    for_x = jnp.concatenate([for_x[:cut], add_f32(for_x[cut:], by_y).astype(low)], axis=0)
    return add_f32(own, move_x(for_x)) + move_y(for_y).astype(jnp.float32)


def reduce_z(ring):
    total = ring[1].astype(jnp.bfloat16)
    for step in range(2, NZ):
        total = add_f32(move_z(total), ring[step]).astype(jnp.bfloat16)
    return add_f32(move_z(total), ring[0])


def reduce_chips(parts):
    return reduce_z([reduce_plane(part) for part in parts])


def place_of(position, k):
    return (position[2] ^ (k >> 1)) * NX + (position[3] ^ (k & 1))


def chunk_copies(position, pieces, rows, slot, held, sems, chunk):
    out = []
    for k in range(NY * NX):
        place = pl.multiple_of(place_of(position, k) * rows, rows)
        out.append(
            pltpu.make_async_copy(
                pieces[chunk].at[k, pl.ds(slot * rows, rows)],
                held.at[chunk, pl.ds(place, rows)],
                sems.at[chunk, k],
            )
        )
    return out


def chunk_base(position, rows, chunk):
    other, step = chunk // NZ, chunk % NZ
    half = position[0] ^ other
    z_of = (position[1] + NZ - step) % NZ
    span = NY * NX * rows
    return pl.multiple_of((half * NZ + z_of) * span, span)


def apply_kernel(position, acts, *refs, rows, slot, tile):
    pieces, (out, held, sems) = refs[: 2 * NZ], refs[2 * NZ :]
    for chunk in range(2 * NZ):
        for copy in chunk_copies(position, pieces, rows, slot, held, sems, chunk):
            copy.start()
    span = NY * NX * rows
    for chunk in range(2 * NZ):
        for copy in chunk_copies(position, pieces, rows, slot, held, sems, chunk):
            copy.wait()
        left = acts[:, pl.ds(chunk_base(position, rows, chunk), span)]

        @pl.loop(0, out.shape[1] // tile)
        def _(i):
            columns = pl.ds(pl.multiple_of(i * tile, tile), tile)
            part = jnp.dot(left, held[chunk, :, columns], preferred_element_type=jnp.float32)
            if chunk == 0:
                out[:, columns] = part
            else:
                out[:, columns] += part


def apply_back_kernel(position, grads, *refs, rows, slot):
    pieces, (out, held, sems) = refs[: 2 * NZ], refs[2 * NZ :]
    for chunk in range(2 * NZ):
        for copy in chunk_copies(position, pieces, rows, slot, held, sems, chunk):
            copy.start()
    span = NY * NX * rows
    for chunk in range(2 * NZ):
        for copy in chunk_copies(position, pieces, rows, slot, held, sems, chunk):
            copy.wait()
        out[:, pl.ds(chunk_base(position, rows, chunk), span)] = lax.dot_general(
            grads[...], held[chunk], (((1,), (1,)), ((), ())), preferred_element_type=jnp.float32
        )


def apply_weight(position, values, pieces, rows, slot, back=False):
    tokens, width = values.shape
    kernel = (
        functools.partial(apply_back_kernel, rows=rows, slot=slot)
        if back
        else functools.partial(apply_kernel, rows=rows, slot=slot, tile=512)
    )
    return pl.pallas_call(
        kernel,
        out_shape=jax.ShapeDtypeStruct((tokens, width), jnp.float32),
        in_specs=[pl.BlockSpec(memory_space=pltpu.SMEM), pl.BlockSpec(memory_space=pltpu.VMEM)]
        + [pl.BlockSpec(memory_space=pl.ANY)] * len(pieces),
        out_specs=pl.BlockSpec(memory_space=pltpu.VMEM),
        scratch_shapes=[
            pltpu.VMEM((2 * NZ, NY * NX * rows, width), jnp.bfloat16),
            pltpu.SemaphoreType.DMA((2 * NZ, NY * NX)),
        ],
        compiler_params=pltpu.CompilerParams(vmem_limit_bytes=VMEM_LIMIT),
        cost_estimate=pl.CostEstimate(
            flops=2 * tokens * width * width,
            bytes_accessed=2 * width * width + 6 * tokens * width,
            transcendentals=0,
        ),
    )(position, values, *pieces)


def weight_grad_kernel(position, own_left, other_left, *refs, rows, count, tile):
    grads, outs, stage = refs[: 2 * count], refs[2 * count : -1], refs[-1]
    span = NY * NX * rows
    for step in range(NZ):
        z_of = (position[1] + NZ - step) % NZ
        columns = pl.ds(pl.multiple_of(z_of * span, span), span)
        own, other = own_left[:, columns], other_left[:, columns]
        for i in range(count):

            @pl.loop(0, grads[0].shape[1] // tile)
            def _(j):
                part = pl.ds(pl.multiple_of(j * tile, tile), tile)
                product = lax.dot_general(
                    own,
                    grads[2 * i][:, part],
                    (((0,), (0,)), ((), ())),
                    preferred_element_type=jnp.float32,
                ) + lax.dot_general(
                    other,
                    grads[2 * i + 1][:, part],
                    (((0,), (0,)), ((), ())),
                    preferred_element_type=jnp.float32,
                )
                stage[...] = product.astype(stage.dtype)
                for k in range(NY * NX):
                    place = pl.multiple_of(place_of(position, k) * rows, rows)
                    outs[step * NY * NX + k][pl.ds(i * rows, rows), part] = stage[pl.ds(place, rows), :]


def weight_grad_parts(position, own_left, other_left, grads, rows):
    count, width = len(grads) // 2, grads[0].shape[1]
    tokens, tile = own_left.shape[0], 512
    block = jax.ShapeDtypeStruct((count * rows, width), jnp.bfloat16)
    outs = pl.pallas_call(
        functools.partial(weight_grad_kernel, rows=rows, count=count, tile=tile),
        out_shape=[block] * (NZ * NY * NX),
        in_specs=[pl.BlockSpec(memory_space=pltpu.SMEM)]
        + [pl.BlockSpec(memory_space=pltpu.VMEM)] * (2 + len(grads)),
        out_specs=[pl.BlockSpec(memory_space=pltpu.VMEM)] * (NZ * NY * NX),
        scratch_shapes=[pltpu.VMEM((NY * NX * rows, tile), jnp.bfloat16)],
        compiler_params=pltpu.CompilerParams(vmem_limit_bytes=VMEM_LIMIT),
        cost_estimate=pl.CostEstimate(
            flops=4 * count * tokens * NZ * NY * NX * rows * width,
            bytes_accessed=2 * count * NZ * NY * NX * rows * width + 4 * tokens * width * (count + 1),
            transcendentals=0,
        ),
    )(position, own_left, other_left, *grads)
    return [outs[s * NY * NX : (s + 1) * NY * NX] for s in range(NZ)]


def gather_weights(blocks):
    ring = [jnp.stack(part) for part in gather_chips(jnp.concatenate(blocks, axis=0))]
    return ring + [move_core(part) for part in ring]


def after(values, earlier):
    return values + (earlier[(0,) * earlier.ndim] * 0).astype(values.dtype)


def body_dense(
    hidden_in,
    cotangent,
    doc_ids,
    routes,
    attn_gain,
    w_query,
    w_key,
    w_value,
    query_gain,
    key_gain,
    w_output,
    moe_gain,
    w_router,
    w_gate,
    w_up,
    w_down,
):
    f32 = jnp.float32
    bf16 = jnp.bfloat16
    tokens_here, model_width = hidden_in.shape
    head_dim = HD
    head_count = model_width // head_dim
    rows = w_query.shape[0]
    experts_all = w_router.shape[1]
    owners = lax.axis_size("expert")
    core = lax.axis_index("dp")
    here = lax.axis_index("expert")
    z_at, y_at, x_at = here // (NY * NX), here // NX % NY, here % NX
    position = jnp.stack([core, z_at, y_at, x_at]).astype(jnp.int32)
    half_width = model_width // 2
    order = jnp.stack(
        [
            chip((z_at + NZ - s) % NZ, y_at ^ (k >> 1), x_at ^ (k & 1))
            for s in range(NZ)
            for k in range(NY * NX)
        ]
    )

    expert_ids = jnp.arange(experts_all, dtype=jnp.int32)
    chosen = routes[:, :, None] == expert_ids[None, None, :]
    uses = jnp.any(chosen, axis=1).astype(f32)
    router_block = jnp.broadcast_to(w_router.astype(f32).reshape(1, -1), (owners, w_router.size))
    small = lax.all_to_all(
        jnp.concatenate([uses.T, router_block], axis=1), "expert", split_axis=0, concat_axis=0, tiled=True
    )
    used_here = small[:, :tokens_here][order].reshape(NZ, NY * NX * tokens_here, 1)
    own_router = small[:, tokens_here:].reshape(-1, experts_all)
    other_router = move_core(own_router)
    full_router = jnp.where(
        core == 0,
        jnp.concatenate([own_router, other_router], axis=0),
        jnp.concatenate([other_router, own_router], axis=0),
    ).astype(bf16)

    pieces_qk = gather_weights([w_query, w_key])
    pieces_vo = gather_weights([w_value, w_output])

    inputs_f32 = hidden_in.astype(f32)
    normed_attn, inverse_attn = norm_forward(inputs_f32, attn_gain)
    act_attn = normed_attn.astype(bf16)
    own_act = lax.dynamic_slice_in_dim(act_attn, core * half_width, half_width, axis=1)
    other_act = move_core(
        lax.dynamic_slice_in_dim(act_attn, (1 - core) * half_width, half_width, axis=1)
    )
    query_pre = apply_weight(position, act_attn, pieces_qk, rows, 0)
    key_pre = apply_weight(position, act_attn, pieces_qk, rows, 1)
    value_low = apply_weight(position, act_attn, pieces_vo, rows, 0).astype(bf16)
    query_normed, query_inverse = norm_forward(query_pre, query_gain)
    key_normed, key_inverse = norm_forward(key_pre, key_gain)
    cosine, sine_table = rotary_tables(tokens_here, head_dim)
    head_shape = (tokens_here, head_count, head_dim)
    query_rot = rotate(query_normed.reshape(head_shape), cosine, sine_table).astype(bf16)
    key_rot = rotate(key_normed.reshape(head_shape), cosine, sine_table).astype(bf16)
    value_heads = value_low.reshape(head_shape)
    score_scale = head_dim ** (-0.5)
    token_at = jnp.arange(tokens_here, dtype=jnp.int32)
    allowed = (token_at[:, None] >= token_at[None, :]) & (
        doc_ids[0][:, None] == doc_ids[0][None, :]
    )
    scores = (
        jnp.einsum("qhd,khd->hqk", query_rot, key_rot, preferred_element_type=f32) * score_scale
    )
    scores = jnp.where(allowed[None], scores, -1e30)
    row_max = jnp.max(scores, axis=-1, keepdims=True)
    row_sum = jnp.sum(jnp.exp(scores - row_max), axis=-1, keepdims=True)
    log_total = row_max + jnp.log(row_sum)
    probs = jnp.exp(scores - log_total)
    probs_low = probs.astype(bf16)
    attended = jnp.einsum("hqk,khd->qhd", probs_low, value_heads, preferred_element_type=f32)
    attended_low = attended.reshape(tokens_here, model_width).astype(bf16)
    middle = inputs_f32 + apply_weight(position, attended_low, pieces_vo, rows, 1)
    normed_moe, inverse_moe = norm_forward(middle, moe_gain)
    act_moe = normed_moe.astype(bf16)

    acts = gather_chips(act_moe)
    grads_out = gather_chips(after(cotangent, pieces_vo[NZ - 1]))

    logits = jnp.dot(act_moe, full_router, preferred_element_type=f32)
    router_probs = jax.nn.softmax(logits, axis=-1)

    gate_w, up_w, down_w = w_gate[0], w_up[0], w_down[0]
    mine = (expert_ids == here).astype(f32)
    out_parts, row_parts, dots = [], [], []
    all_acts, all_hidden, all_out_grads, all_gate_grads, all_up_grads = [], [], [], [], []
    for s in range(NZ):
        act_rows = jnp.concatenate(acts[s], axis=0)
        probs_rows = jax.nn.softmax(
            jnp.dot(act_rows, full_router, preferred_element_type=f32), axis=-1
        )
        gate_rows = jnp.sum(probs_rows * mine[None, :], axis=-1, keepdims=True) * used_here[s]
        gate_pre = jnp.dot(act_rows, gate_w, preferred_element_type=f32)
        up_pre = jnp.dot(act_rows, up_w, preferred_element_type=f32)
        sigmoid = jax.nn.sigmoid(gate_pre)
        swish = gate_pre * sigmoid
        hidden_low = (swish * up_pre).astype(bf16)
        expert_out = jnp.dot(hidden_low, down_w, preferred_element_type=f32).astype(bf16)
        out_low = (gate_rows * expert_out.astype(f32)).astype(bf16)
        out_parts.append(jnp.split(out_low, NY * NX, axis=0))
        upstream_rows = jnp.concatenate(grads_out[s], axis=0)
        upstream_f32 = upstream_rows.astype(f32)
        dots.append(jnp.sum(upstream_f32 * expert_out.astype(f32), axis=-1, keepdims=True) * used_here[s])
        out_grad = (gate_rows * upstream_f32).astype(bf16)
        hidden_grad = times_transposed(out_grad, down_w)
        slope = sigmoid * (1.0 + gate_pre * (1.0 - sigmoid))
        gate_pre_grad = (hidden_grad * up_pre * slope).astype(bf16)
        up_pre_grad = (hidden_grad * swish).astype(bf16)
        row_grad = (
            times_transposed(gate_pre_grad, gate_w) + times_transposed(up_pre_grad, up_w)
        ).astype(bf16)
        row_parts.append(jnp.split(row_grad, NY * NX, axis=0))
        all_acts.append(act_rows)
        all_hidden.append(hidden_low)
        all_out_grads.append(out_grad)
        all_gate_grads.append(gate_pre_grad)
        all_up_grads.append(up_pre_grad)
    choice_rows = jnp.zeros((owners, tokens_here), f32).at[order].set(
        jnp.concatenate(dots, axis=0).reshape(owners, tokens_here)
    )
    choice_grad = lax.all_to_all(
        choice_rows, "expert", split_axis=0, concat_axis=0, tiled=True
    ).T
    moe_in_grad = reduce_chips(row_parts)

    logit_grad = router_probs * (
        choice_grad - jnp.sum(router_probs * choice_grad, axis=-1, keepdims=True)
    )
    logit_low = logit_grad.astype(bf16)
    moe_in_grad = moe_in_grad + times_transposed(logit_low, full_router)
    router_grad = inner_product(act_moe, logit_low)
    upstream = cotangent.astype(f32)
    mid_norm_grad, moe_gain_grad = norm_backward(middle, inverse_moe, moe_gain, moe_in_grad)
    mid_grad = upstream + mid_norm_grad
    mid_low = mid_grad.astype(bf16)

    own_attended = lax.dynamic_slice_in_dim(attended_low, core * half_width, half_width, axis=1)
    other_attended = move_core(
        lax.dynamic_slice_in_dim(attended_low, (1 - core) * half_width, half_width, axis=1)
    )
    output_grad = reduce_chips(
        weight_grad_parts(
            position, own_attended, other_attended, [mid_low, move_core(mid_low)], rows
        )
    )
    attended_grad = (
        apply_weight(position, mid_low, pieces_vo, rows, 1, back=True)
        .astype(bf16)
        .reshape(head_shape)
    )
    probs_grad = jnp.einsum("qhd,khd->hqk", attended_grad, value_heads, preferred_element_type=f32)
    row_inner = jnp.sum(probs * probs_grad, axis=-1, keepdims=True)
    scores_grad = (probs * (probs_grad - row_inner)).astype(bf16)
    query_rot_grad = (
        jnp.einsum("hqk,khd->qhd", scores_grad, key_rot, preferred_element_type=f32) * score_scale
    )
    key_rot_grad = (
        jnp.einsum("hqk,qhd->khd", scores_grad, query_rot, preferred_element_type=f32) * score_scale
    )
    value_grad = jnp.einsum("hqk,qhd->khd", probs_low, attended_grad, preferred_element_type=f32)
    value_grad = value_grad.reshape(tokens_here, model_width).astype(bf16)
    query_back = rotate_back(query_rot_grad, cosine, sine_table).reshape(tokens_here, model_width)
    key_back = rotate_back(key_rot_grad, cosine, sine_table).reshape(tokens_here, model_width)
    query_pre_grad, query_gain_grad = norm_backward(
        query_pre, query_inverse, query_gain, query_back
    )
    key_pre_grad, key_gain_grad = norm_backward(key_pre, key_inverse, key_gain, key_back)
    query_low = query_pre_grad.astype(bf16)
    key_low = key_pre_grad.astype(bf16)
    attn_weight_grads = reduce_chips(
        weight_grad_parts(
            position,
            own_act,
            other_act,
            [
                query_low,
                move_core(query_low),
                key_low,
                move_core(key_low),
                value_grad,
                move_core(value_grad),
            ],
            rows,
        )
    )
    query_weight_grad, key_weight_grad, value_weight_grad = jnp.split(attn_weight_grads, 3, axis=0)
    act_grad = (
        apply_weight(position, query_low, pieces_qk, rows, 0, back=True)
        + apply_weight(position, key_low, pieces_qk, rows, 1, back=True)
        + apply_weight(position, value_grad, pieces_vo, rows, 0, back=True)
    )
    input_norm_grad, attn_gain_grad = norm_backward(inputs_f32, inverse_attn, attn_gain, act_grad)
    input_grad = (mid_grad + input_norm_grad).astype(bf16)

    devices = 2 * owners
    small_grads = jnp.concatenate(
        [
            part.reshape(devices, -1)
            for part in (attn_gain_grad, query_gain_grad, key_gain_grad, moe_gain_grad, router_grad)
        ],
        axis=1,
    )
    small_grads = jnp.sum(
        lax.all_to_all(
            small_grads, ("dp", "expert"), split_axis=0, concat_axis=0, tiled=True
        ),
        axis=0,
    )
    attn_gain_grad, query_gain_grad, key_gain_grad, moe_gain_grad, router_grad = jnp.split(
        small_grads, [rows, 2 * rows, 3 * rows, 4 * rows]
    )

    moe_term = reduce_chips(out_parts)
    block_out = (middle + moe_term).astype(bf16)
    expert_acts = jnp.concatenate(all_acts, axis=0)
    gate_weight_grad = inner_product(expert_acts, jnp.concatenate(all_gate_grads, axis=0))
    up_weight_grad = inner_product(expert_acts, jnp.concatenate(all_up_grads, axis=0))
    down_grad = inner_product(
        jnp.concatenate(all_hidden, axis=0), jnp.concatenate(all_out_grads, axis=0)
    )
    gate_weight_grad, up_weight_grad, down_grad = (
        lax.psum_scatter(
            gate_weight_grad.astype(bf16)[None], "dp", scatter_dimension=2, tiled=True
        ).astype(f32),
        lax.psum_scatter(
            up_weight_grad.astype(bf16)[None], "dp", scatter_dimension=2, tiled=True
        ).astype(f32),
        lax.psum_scatter(
            down_grad.astype(bf16)[None], "dp", scatter_dimension=1, tiled=True
        ).astype(f32),
    )
    return (
        block_out,
        input_grad,
        attn_gain_grad,
        query_weight_grad,
        key_weight_grad,
        value_weight_grad,
        query_gain_grad,
        key_gain_grad,
        output_grad,
        moe_gain_grad,
        router_grad.reshape(w_router.shape),
        gate_weight_grad,
        up_weight_grad,
        down_grad,
    )


def solution(mesh):
    body = body_dense if mesh.shape["expert"] == NZ * NY * NX else body_routed
    return jax.shard_map(
        body,
        mesh=mesh,
        in_specs=(
            P(("dp", "expert"), None),
            P(("dp", "expert"), None),
            P(("dp", "expert"), None),
            P(("dp", "expert"), None),
            P(),
            P(("dp", "expert"), None),
            P(("dp", "expert"), None),
            P(("dp", "expert"), None),
            P(),
            P(),
            P(("dp", "expert"), None),
            P(),
            P(("dp", "expert"), None),
            P("expert", None, None),
            P("expert", None, None),
            P("expert", None, None),
        ),
        out_specs=(
            P(("dp", "expert"), None),
            P(("dp", "expert"), None),
            P(("dp", "expert")),
            P(("dp", "expert"), None),
            P(("dp", "expert"), None),
            P(("dp", "expert"), None),
            P(("dp", "expert")),
            P(("dp", "expert")),
            P(("dp", "expert"), None),
            P(("dp", "expert")),
            P(("dp", "expert"), None),
            P("expert", None, "dp"),
            P("expert", None, "dp"),
            P("expert", "dp", None),
        ),
        check_vma=False,
    )
```

```python
import functools
import itertools

import jax
import jax.numpy as jnp
from jax import lax
from jax.experimental import pallas as pl
from jax.experimental.pallas import tpu as pltpu
from jax.sharding import PartitionSpec as P

HD = 128


EPSILON = 1e-05


def norm_forward(values, gain_vector):
    inverse = lax.rsqrt(jnp.mean(values * values, axis=-1, keepdims=True) + EPSILON)
    return (values * inverse * gain_vector, inverse)


def norm_backward(values, inverse, gain_vector, upstream):
    gain_grad = jnp.sum(upstream * values * inverse, axis=0)
    scaled = upstream * gain_vector
    inner_mean = jnp.mean(scaled * values, axis=-1, keepdims=True)
    return (inverse * (scaled - values * inner_mean * inverse * inverse), gain_grad)


def rotary_tables(length, head_dim):
    half_dim = head_dim // 2
    frequency = 10000.0 ** (-jnp.arange(half_dim, dtype=jnp.float32) * 2.0 / head_dim)
    angles = jnp.arange(length, dtype=jnp.float32)[:, None] * frequency[None, :]
    angles = jnp.concatenate([angles, angles], axis=1)
    return (jnp.cos(angles)[:, None, :], jnp.sin(angles)[:, None, :])


def rotate(values, cosine, sine_table):
    half_dim = values.shape[-1] // 2
    turned = jnp.concatenate([-values[..., half_dim:], values[..., :half_dim]], axis=-1)
    return values * cosine + turned * sine_table


def rotate_back(upstream, cosine, sine_table):
    half_dim = upstream.shape[-1] // 2
    with_sine = upstream * sine_table
    turned = jnp.concatenate([with_sine[..., half_dim:], -with_sine[..., :half_dim]], axis=-1)
    return upstream * cosine + turned


def times_transposed(left, right):
    return jnp.einsum("ta,ba->tb", left, right, preferred_element_type=jnp.float32)


def inner_product(left, right):
    return jnp.einsum("ta,tb->ab", left, right, preferred_element_type=jnp.float32)


def body_routed(
    hidden_in,
    cotangent,
    doc_ids,
    routes,
    attn_gain,
    w_query,
    w_key,
    w_value,
    query_gain,
    key_gain,
    w_output,
    moe_gain,
    w_router,
    w_gate,
    w_up,
    w_down,
):
    f32 = jnp.float32
    bf16 = jnp.bfloat16
    tokens_here = hidden_in.shape[0]
    model_width = hidden_in.shape[1]
    head_dim = HD
    head_count = model_width // head_dim
    top_count = routes.shape[1]
    experts_all = w_router.shape[1]
    capacity = tokens_here * top_count * 4 // (3 * experts_all)
    local_experts = w_gate.shape[0]
    owners = lax.axis_size("expert")
    full_query, full_key, full_value, full_output, full_router = (
        lax.all_gather(w_query, ("dp", "expert"), axis=0, tiled=True),
        lax.all_gather(w_key, ("dp", "expert"), axis=0, tiled=True),
        lax.all_gather(w_value, ("dp", "expert"), axis=0, tiled=True),
        lax.all_gather(w_output, ("dp", "expert"), axis=0, tiled=True),
        lax.all_gather(w_router, ("dp", "expert"), axis=0, tiled=True),
    )
    inputs_f32 = hidden_in.astype(f32)
    normed_attn, inverse_attn = norm_forward(inputs_f32, attn_gain)
    act_attn = normed_attn.astype(bf16)
    query_pre = jnp.dot(act_attn, full_query, preferred_element_type=f32)
    key_pre = jnp.dot(act_attn, full_key, preferred_element_type=f32)
    value_low = jnp.dot(act_attn, full_value, preferred_element_type=f32).astype(bf16)
    query_normed, query_inverse = norm_forward(query_pre, query_gain)
    key_normed, key_inverse = norm_forward(key_pre, key_gain)
    cosine, sine_table = rotary_tables(tokens_here, head_dim)
    head_shape = (tokens_here, head_count, head_dim)
    query_rot = rotate(query_normed.reshape(head_shape), cosine, sine_table).astype(bf16)
    key_rot = rotate(key_normed.reshape(head_shape), cosine, sine_table).astype(bf16)
    value_heads = value_low.reshape(head_shape)
    score_scale = head_dim ** (-0.5)
    position = jnp.arange(tokens_here, dtype=jnp.int32)
    allowed = (position[:, None] >= position[None, :]) & (
        doc_ids[0][:, None] == doc_ids[0][None, :]
    )

    def masked_scores():
        scores = (
            jnp.einsum("qhd,khd->hqk", query_rot, key_rot, preferred_element_type=f32) * score_scale
        )
        return jnp.where(allowed[None], scores, -1e30)

    scores = masked_scores()
    row_max = jnp.max(scores, axis=-1, keepdims=True)
    row_sum = jnp.sum(jnp.exp(scores - row_max), axis=-1, keepdims=True)
    log_total = row_max + jnp.log(row_sum)
    probs_low = jnp.exp(scores - log_total).astype(bf16)
    attended = jnp.einsum("hqk,khd->qhd", probs_low, value_heads, preferred_element_type=f32)
    attended_low = attended.reshape(tokens_here, model_width).astype(bf16)
    middle = inputs_f32 + jnp.dot(attended_low, full_output, preferred_element_type=f32)
    normed_moe, inverse_moe = norm_forward(middle, moe_gain)
    act_moe = normed_moe.astype(bf16)
    logits = jnp.dot(act_moe, full_router, preferred_element_type=f32)
    router_probs = jax.nn.softmax(logits, axis=-1)
    expert_ids = jnp.arange(experts_all, dtype=jnp.int32)
    chosen = routes[:, :, None] == expert_ids[None, None, :]
    gate_values = jnp.sum(jnp.where(chosen, router_probs[:, None, :], 0.0), axis=-1)
    flat_routes = routes.reshape(-1)
    onehot = (flat_routes[:, None] == expert_ids[None, :]).astype(jnp.int32)
    slot_of = jnp.sum((jnp.cumsum(onehot, axis=0) - 1) * onehot, axis=1)
    target_slot = flat_routes * capacity + slot_of
    pair_token = jnp.arange(tokens_here * top_count, dtype=jnp.int32) // top_count

    def to_experts(pair_rows):
        buffer = (
            jnp.zeros((experts_all * capacity, model_width), bf16).at[target_slot].set(pair_rows)
        )
        return buffer.reshape(experts_all, capacity, model_width)

    def from_experts(buffer):
        return buffer.reshape(experts_all * capacity, model_width)[target_slot]

    received = lax.all_to_all(
        to_experts(act_moe[pair_token]), "expert", split_axis=0, concat_axis=0, tiled=True
    )
    owner_rows = received.reshape(owners, local_experts, capacity, model_width)
    gate_pre = jnp.einsum("secd,edf->secf", owner_rows, w_gate, preferred_element_type=f32)
    up_pre = jnp.einsum("secd,edf->secf", owner_rows, w_up, preferred_element_type=f32)
    sigmoid = jax.nn.sigmoid(gate_pre)
    swish = gate_pre * sigmoid
    hidden_low = (swish * up_pre).astype(bf16)
    expert_out = jnp.einsum(
        "secf,efd->secd", hidden_low, w_down, preferred_element_type=f32
    ).astype(bf16)
    returned = lax.all_to_all(
        expert_out.reshape(owners * local_experts, capacity, model_width),
        "expert",
        split_axis=0,
        concat_axis=0,
        tiled=True,
    )
    pair_out = from_experts(returned).reshape(tokens_here, top_count, model_width).astype(f32)
    moe_term = jnp.sum(gate_values[:, :, None] * pair_out, axis=1)
    block_out = (middle + moe_term).astype(bf16)
    upstream = cotangent.astype(f32)
    pair_grad = (gate_values[:, :, None] * upstream[:, None, :]).astype(bf16)
    gate_grad = jnp.sum(upstream[:, None, :] * pair_out, axis=-1)
    out_grad = lax.all_to_all(
        to_experts(pair_grad.reshape(-1, model_width)),
        "expert",
        split_axis=0,
        concat_axis=0,
        tiled=True,
    )
    out_grad = out_grad.reshape(owners, local_experts, capacity, model_width)
    hidden_grad = jnp.einsum("secd,efd->secf", out_grad, w_down, preferred_element_type=f32)
    down_grad = jnp.einsum("secf,secd->efd", hidden_low, out_grad, preferred_element_type=f32)
    slope = sigmoid * (1.0 + gate_pre * (1.0 - sigmoid))
    gate_pre_grad = (hidden_grad * up_pre * slope).astype(bf16)
    up_pre_grad = (hidden_grad * swish).astype(bf16)
    row_grad = jnp.einsum("secf,edf->secd", gate_pre_grad, w_gate, preferred_element_type=f32)
    row_grad = (
        row_grad + jnp.einsum("secf,edf->secd", up_pre_grad, w_up, preferred_element_type=f32)
    ).astype(bf16)
    gate_weight_grad = jnp.einsum(
        "secd,secf->edf", owner_rows, gate_pre_grad, preferred_element_type=f32
    )
    up_weight_grad = jnp.einsum(
        "secd,secf->edf", owner_rows, up_pre_grad, preferred_element_type=f32
    )
    gate_weight_grad, up_weight_grad, down_grad = (
        lax.psum_scatter(
            gate_weight_grad.astype(jnp.bfloat16), "dp", scatter_dimension=2, tiled=True
        ).astype(jnp.float32),
        lax.psum_scatter(
            up_weight_grad.astype(jnp.bfloat16), "dp", scatter_dimension=2, tiled=True
        ).astype(jnp.float32),
        lax.psum_scatter(
            down_grad.astype(jnp.bfloat16), "dp", scatter_dimension=1, tiled=True
        ).astype(jnp.float32),
    )
    back_rows = lax.all_to_all(
        row_grad.reshape(owners * local_experts, capacity, model_width),
        "expert",
        split_axis=0,
        concat_axis=0,
        tiled=True,
    )
    moe_in_grad = jnp.sum(
        from_experts(back_rows).reshape(tokens_here, top_count, model_width).astype(f32), axis=1
    )
    choice_grad = jnp.sum(jnp.where(chosen, gate_grad[:, :, None], 0.0), axis=1)
    logit_grad = router_probs * (
        choice_grad - jnp.sum(router_probs * choice_grad, axis=-1, keepdims=True)
    )
    logit_low = logit_grad.astype(bf16)
    moe_in_grad = moe_in_grad + times_transposed(logit_low, full_router)
    router_grad = inner_product(act_moe, logit_low)
    mid_norm_grad, moe_gain_grad = norm_backward(middle, inverse_moe, moe_gain, moe_in_grad)
    mid_grad = upstream + mid_norm_grad
    mid_low = mid_grad.astype(bf16)
    output_grad = inner_product(attended_low, mid_low)
    attended_grad = times_transposed(mid_low, full_output).astype(bf16).reshape(head_shape)
    probs = jnp.exp(masked_scores() - log_total)
    probs_grad = jnp.einsum("qhd,khd->hqk", attended_grad, value_heads, preferred_element_type=f32)
    row_inner = jnp.sum(probs * probs_grad, axis=-1, keepdims=True)
    scores_grad = (probs * (probs_grad - row_inner)).astype(bf16)
    query_rot_grad = (
        jnp.einsum("hqk,khd->qhd", scores_grad, key_rot, preferred_element_type=f32) * score_scale
    )
    key_rot_grad = (
        jnp.einsum("hqk,qhd->khd", scores_grad, query_rot, preferred_element_type=f32) * score_scale
    )
    value_grad = jnp.einsum("hqk,qhd->khd", probs_low, attended_grad, preferred_element_type=f32)
    value_grad = value_grad.reshape(tokens_here, model_width).astype(bf16)
    query_back = rotate_back(query_rot_grad, cosine, sine_table).reshape(tokens_here, model_width)
    key_back = rotate_back(key_rot_grad, cosine, sine_table).reshape(tokens_here, model_width)
    query_pre_grad, query_gain_grad = norm_backward(
        query_pre, query_inverse, query_gain, query_back
    )
    key_pre_grad, key_gain_grad = norm_backward(key_pre, key_inverse, key_gain, key_back)
    query_low = query_pre_grad.astype(bf16)
    key_low = key_pre_grad.astype(bf16)
    act_grad = (
        times_transposed(query_low, full_query)
        + times_transposed(key_low, full_key)
        + times_transposed(value_grad, full_value)
    )
    query_weight_grad = inner_product(act_attn, query_low)
    key_weight_grad = inner_product(act_attn, key_low)
    value_weight_grad = inner_product(act_attn, value_grad)
    input_norm_grad, attn_gain_grad = norm_backward(inputs_f32, inverse_attn, attn_gain, act_grad)
    input_grad = (mid_grad + input_norm_grad).astype(bf16)
    sharded_grads = (
        lax.psum_scatter(attn_gain_grad, ("dp", "expert"), scatter_dimension=0, tiled=True),
        lax.psum_scatter(query_weight_grad, ("dp", "expert"), scatter_dimension=0, tiled=True),
        lax.psum_scatter(key_weight_grad, ("dp", "expert"), scatter_dimension=0, tiled=True),
        lax.psum_scatter(value_weight_grad, ("dp", "expert"), scatter_dimension=0, tiled=True),
        lax.psum_scatter(query_gain_grad, ("dp", "expert"), scatter_dimension=0, tiled=True),
        lax.psum_scatter(key_gain_grad, ("dp", "expert"), scatter_dimension=0, tiled=True),
        lax.psum_scatter(output_grad, ("dp", "expert"), scatter_dimension=0, tiled=True),
        lax.psum_scatter(moe_gain_grad, ("dp", "expert"), scatter_dimension=0, tiled=True),
        lax.psum_scatter(router_grad, ("dp", "expert"), scatter_dimension=0, tiled=True),
    )
    return (
        block_out,
        input_grad,
        sharded_grads[0],
        sharded_grads[1],
        sharded_grads[2],
        sharded_grads[3],
        sharded_grads[4],
        sharded_grads[5],
        sharded_grads[6],
        sharded_grads[7],
        sharded_grads[8],
        gate_weight_grad,
        up_weight_grad,
        down_grad,
    )


NZ, NY, NX = 4, 2, 2
VMEM_LIMIT = 48 * 1024 * 1024
EXPERT_VMEM = 60 * 1024 * 1024
WINDOW = 5
UPSTREAM_AT = 1


def chip(z, y, x):
    return (z * NY + y) * NX + x


GRID = [(z, y, x) for z in range(NZ) for y in range(NY) for x in range(NX)]
X_PAIRS = [(chip(z, y, x), chip(z, y, 1 - x)) for z, y, x in GRID]
Y_PAIRS = [(chip(z, y, x), chip(z, 1 - y, x)) for z, y, x in GRID]
Z_PAIRS = [(chip(z, y, x), chip((z + 1) % NZ, y, x)) for z, y, x in GRID]
CORE_PAIRS = [(0, 1), (1, 0)]


def move_x(values):
    return lax.ppermute(values, "expert", X_PAIRS)


def move_y(values):
    return lax.ppermute(values, "expert", Y_PAIRS)


def move_z(values):
    return lax.ppermute(values, "expert", Z_PAIRS)


def move_core(values):
    return lax.ppermute(values, "dp", CORE_PAIRS)


def split_row(rows):
    return (rows // 2 + 15) // 16 * 16


def after(values, *earlier):
    return lax.optimization_barrier((values, *earlier))[0]


class Line:
    def __init__(self):
        self.sent, self.held = [], []

    def hold(self, *earlier):
        self.held += earlier

    def send(self, move, values):
        if len(self.sent) >= WINDOW:
            self.held.append(self.sent[-WINDOW])
        if self.held:
            values = after(values, *self.held)
            self.held = []
        self.sent.append(move(values))
        return self.sent[-1]


def gather_z(block):
    ring = [block]
    for _ in range(1, NZ):
        ring.append(move_z(ring[-1]))
    return ring


def gather_plane(block):
    cut = split_row(block.shape[0])
    from_x = move_x(block)
    from_y = move_y(block)
    across = jnp.concatenate([move_x(from_y[:cut]), move_y(from_x[cut:])], axis=0)
    return [block, from_x, from_y, across]


def gather_chips(block):
    return [gather_plane(part) for part in gather_z(block)]


def add_f32(left, right):
    return left.astype(jnp.float32) + right.astype(jnp.float32)


class Reduce:
    def __init__(self, line):
        self.line, self.planes, self.open, self.steps = line, {}, None, 0
        self.total = None

    def add(self, step, parts):
        by_x = self.line.send(move_x, parts[3])
        by_y = self.line.send(move_y, parts[4])
        self.finish_plane()
        self.open = (step, parts, by_x, by_y)
        self.push()

    def ways(self):
        return self.open[2:]

    def finish_plane(self):
        if self.open is None:
            return
        step, (own, for_x, for_y, *_), by_x, by_y = self.open
        low = own.dtype
        cut = by_x.shape[0]
        for_y = jnp.concatenate([add_f32(for_y[:cut], by_x).astype(low), for_y[cut:]], axis=0)
        for_x = jnp.concatenate([for_x[:cut], add_f32(for_x[cut:], by_y).astype(low)], axis=0)
        from_x = self.line.send(move_x, for_x)
        from_y = self.line.send(move_y, for_y)
        self.planes[step] = add_f32(own, from_x) + from_y.astype(jnp.float32)
        self.open = None

    def push(self):
        while self.steps + 1 < NZ and self.steps + 1 in self.planes:
            self.steps += 1
            total = self.planes[self.steps]
            if self.total is not None:
                total = add_f32(self.total, total)
            self.total = self.line.send(move_z, total.astype(jnp.bfloat16))

    def result(self):
        self.finish_plane()
        self.push()
        return add_f32(self.total, self.planes[0])


def place_of(position, k):
    return (position[2] ^ (k >> 1)) * NX + (position[3] ^ (k & 1))


def weight_copies(position, pieces, rows, slot, held, sems, other):
    out = []
    for step in range(NZ):
        z_of = (position[1] + NZ - step) % NZ
        for k in range(NY * NX):
            place = pl.multiple_of((z_of * NY * NX + place_of(position, k)) * rows, rows)
            out.append(
                pltpu.make_async_copy(
                    pieces[other * NZ + step].at[k, pl.ds(slot * rows, rows)],
                    held.at[other, pl.ds(place, rows)],
                    sems.at[other * NZ + step, k],
                )
            )
    return out


def apply_kernel(position, acts, *refs, rows, slot, tile):
    pieces, (out, held, sems) = refs[: 2 * NZ], refs[2 * NZ :]
    for other in range(2):
        for copy in weight_copies(position, pieces, rows, slot, held, sems, other):
            copy.start()
    span = held.shape[1]
    for other in range(2):
        for copy in weight_copies(position, pieces, rows, slot, held, sems, other):
            copy.wait()
        left = acts[:, pl.ds(pl.multiple_of((position[0] ^ other) * span, span), span)]

        @pl.loop(0, out.shape[1] // tile)
        def _(i):
            columns = pl.ds(pl.multiple_of(i * tile, tile), tile)
            part = jnp.dot(left, held[other, :, columns], preferred_element_type=jnp.float32)
            if other == 0:
                out[:, columns] = part
            else:
                out[:, columns] += part


def apply_back_kernel(position, grads, *refs, rows, slot, tile):
    pieces, (out, held, sems) = refs[: 2 * NZ], refs[2 * NZ :]
    for other in range(2):
        for copy in weight_copies(position, pieces, rows, slot, held, sems, other):
            copy.start()
    span = held.shape[1]
    for other in range(2):
        for copy in weight_copies(position, pieces, rows, slot, held, sems, other):
            copy.wait()

        @pl.loop(0, span // tile)
        def _(i):
            lines = pl.ds(pl.multiple_of(i * tile, tile), tile)
            low = pl.multiple_of((position[0] ^ other) * span + i * tile, tile)
            out[:, pl.ds(low, tile)] = lax.dot_general(
                grads[...],
                held[other, lines, :],
                (((1,), (1,)), ((), ())),
                preferred_element_type=jnp.float32,
            )


def apply_weight(position, values, pieces, rows, slot, back=False):
    tokens, width = values.shape
    return pl.pallas_call(
        functools.partial(
            apply_back_kernel if back else apply_kernel, rows=rows, slot=slot, tile=512
        ),
        out_shape=jax.ShapeDtypeStruct((tokens, width), jnp.float32),
        in_specs=[pl.BlockSpec(memory_space=pltpu.SMEM), pl.BlockSpec(memory_space=pltpu.VMEM)]
        + [pl.BlockSpec(memory_space=pl.ANY)] * len(pieces),
        out_specs=pl.BlockSpec(memory_space=pltpu.VMEM),
        scratch_shapes=[
            pltpu.VMEM((2, width // 2, width), jnp.bfloat16),
            pltpu.SemaphoreType.DMA((2 * NZ, NY * NX)),
        ],
        compiler_params=pltpu.CompilerParams(vmem_limit_bytes=VMEM_LIMIT),
        cost_estimate=pl.CostEstimate(
            flops=2 * tokens * width * width,
            bytes_accessed=2 * width * width + 6 * tokens * width,
            transcendentals=0,
        ),
    )(position, values, *pieces)


def weight_grad_kernel(position, own_left, other_left, *refs, rows, count, tile, step):
    grads, outs, stage = refs[: 2 * count], refs[2 * count : -1], refs[-1]
    span = NY * NX * rows
    z_of = (position[1] + NZ - step) % NZ
    lines = pl.ds(pl.multiple_of(z_of * span, span), span)
    own, other = own_left[lines, :], other_left[lines, :]
    for i in range(count):

        @pl.loop(0, grads[0].shape[1] // tile)
        def _(j):
            part = pl.ds(pl.multiple_of(j * tile, tile), tile)
            product = jnp.dot(
                own, grads[2 * i][:, part], preferred_element_type=jnp.float32
            ) + jnp.dot(other, grads[2 * i + 1][:, part], preferred_element_type=jnp.float32)
            stage[...] = product.astype(stage.dtype)
            for k in range(NY * NX):
                place = pl.multiple_of(place_of(position, k) * rows, rows)
                outs[k][pl.ds(i * rows, rows), part] = stage[pl.ds(place, rows), :]


def weight_grad_parts(position, own_left, other_left, grads, rows, step):
    count, width = len(grads) // 2, grads[0].shape[1]
    tokens, tile = own_left.shape[1], 512
    block = jax.ShapeDtypeStruct((count * rows, width), jnp.bfloat16)
    return pl.pallas_call(
        functools.partial(weight_grad_kernel, rows=rows, count=count, tile=tile, step=step),
        out_shape=[block] * (NY * NX),
        in_specs=[pl.BlockSpec(memory_space=pltpu.SMEM)]
        + [pl.BlockSpec(memory_space=pltpu.VMEM)] * (2 + len(grads)),
        out_specs=[pl.BlockSpec(memory_space=pltpu.VMEM)] * (NY * NX),
        scratch_shapes=[pltpu.VMEM((NY * NX * rows, tile), jnp.bfloat16)],
        compiler_params=pltpu.CompilerParams(vmem_limit_bytes=VMEM_LIMIT),
        cost_estimate=pl.CostEstimate(
            flops=4 * count * tokens * NY * NX * rows * width,
            bytes_accessed=2 * count * NY * NX * rows * width + 4 * tokens * width * (count + 1),
            transcendentals=0,
        ),
    )(position, own_left, other_left, *grads)


def column_grad_kernel(position, *refs):
    parts = (len(refs) - 2) // 2
    acts, grads, outs = refs[:parts], refs[parts:-2], refs[-2:]
    half = outs[0].shape[1]
    turned = [act[...].T for act in acts]
    for side, out in enumerate(outs):
        columns = pl.ds(pl.multiple_of((position[0] ^ side) * half, half), half)
        total = None
        for act, grad in zip(turned, grads, strict=True):
            more = jnp.dot(act, grad[:, columns], preferred_element_type=jnp.float32)
            total = more if total is None else total + more
        out[...] = total.astype(out.dtype)


def column_grads(position, acts, grads):
    parts = len(acts)
    count, width = acts[0].shape
    units = grads[0].shape[1]
    tile = 256
    whole = pl.BlockSpec((count, units), lambda i: (0, 0), pipeline_mode=pl.Buffered(1))
    out = pl.BlockSpec((tile, units // 2), lambda i: (i, 0))
    return pl.pallas_call(
        column_grad_kernel,
        grid=(width // tile,),
        out_shape=[jax.ShapeDtypeStruct((width, units // 2), t) for t in (jnp.float32, jnp.bfloat16)],
        in_specs=[pl.BlockSpec(memory_space=pltpu.SMEM)]
        + [pl.BlockSpec((count, tile), lambda i: (0, i))] * parts
        + [whole] * parts,
        out_specs=[out] * 2,
        compiler_params=pltpu.CompilerParams(vmem_limit_bytes=EXPERT_VMEM),
        cost_estimate=pl.CostEstimate(
            flops=2 * parts * count * width * units,
            bytes_accessed=2 * parts * count * (width + units) + 3 * width * units,
            transcendentals=0,
        ),
    )(position, *acts, *grads)


def down_grad_kernel(position, *refs):
    parts = (len(refs) - 3) // 2
    hiddens, grads, (own, other, turned) = refs[:parts], refs[parts:-3], refs[-3:]
    tile = 512
    for s, hidden in enumerate(hiddens):
        turned[s] = hidden[...].T

    def part_of(j):
        columns = pl.ds(pl.multiple_of(j * tile, tile), tile)
        total = None
        for s, grad in enumerate(grads):
            more = jnp.dot(turned[s], grad[:, columns], preferred_element_type=jnp.float32)
            total = more if total is None else total + more
        return columns, total

    steps = grads[0].shape[1] // tile

    @pl.when(pl.program_id(0) < pl.num_programs(0) // 2)
    def _():
        @pl.loop(0, steps)
        def _(j):
            columns, total = part_of(j)
            own[:, columns] = total

    @pl.when(pl.program_id(0) >= pl.num_programs(0) // 2)
    def _():
        @pl.loop(0, steps)
        def _(j):
            columns, total = part_of(j)
            other[:, columns] = total.astype(other.dtype)


def down_grads(position, hiddens, grads):
    parts = len(hiddens)
    count, units = hiddens[0].shape
    width = grads[0].shape[1]
    tile = 256
    half = units // 2 // tile
    whole = pl.BlockSpec((count, width), lambda i, at: (0, 0), pipeline_mode=pl.Buffered(1))
    return pl.pallas_call(
        down_grad_kernel,
        grid_spec=pltpu.PrefetchScalarGridSpec(
            num_scalar_prefetch=1,
            grid=(2 * half,),
            in_specs=[
                pl.BlockSpec((count, tile), lambda i, at: (0, (i + at[0] * half) % (2 * half)))
            ]
            * parts
            + [whole] * parts,
            out_specs=[
                pl.BlockSpec((tile, width), lambda i, at: (jnp.minimum(i, half - 1), 0)),
                pl.BlockSpec((tile, width), lambda i, at: (jnp.maximum(i - half, 0), 0)),
            ],
            scratch_shapes=[pltpu.VMEM((parts, tile, count), jnp.bfloat16)],
        ),
        out_shape=[
            jax.ShapeDtypeStruct((units // 2, width), jnp.float32),
            jax.ShapeDtypeStruct((units // 2, width), jnp.bfloat16),
        ],
        compiler_params=pltpu.CompilerParams(vmem_limit_bytes=EXPERT_VMEM),
        cost_estimate=pl.CostEstimate(
            flops=2 * parts * count * width * units,
            bytes_accessed=2 * parts * count * (width + units) + 3 * width * units,
            transcendentals=0,
        ),
    )(position, *hiddens, *grads)


def gather_weights(blocks):
    ring = [jnp.stack(part) for part in gather_chips(jnp.concatenate(blocks, axis=0))]
    return ring + [move_core(part) for part in ring]


def body_dense(
    hidden_in,
    cotangent,
    doc_ids,
    routes,
    attn_gain,
    w_query,
    w_key,
    w_value,
    query_gain,
    key_gain,
    w_output,
    moe_gain,
    w_router,
    w_gate,
    w_up,
    w_down,
):
    f32 = jnp.float32
    bf16 = jnp.bfloat16
    tokens_here, model_width = hidden_in.shape
    head_dim = HD
    head_count = model_width // head_dim
    rows = w_query.shape[0]
    experts_all = w_router.shape[1]
    owners = lax.axis_size("expert")
    core = lax.axis_index("dp")
    here = lax.axis_index("expert")
    z_at, y_at, x_at = here // (NY * NX), here // NX % NY, here % NX
    position = jnp.stack([core, z_at, y_at, x_at, here]).astype(jnp.int32)
    half_width = model_width // 2
    plane = NY * NX
    places = [(y_at ^ (k >> 1)) * NX + (x_at ^ (k & 1)) for k in range(plane)]
    planes = [(z_at + NZ - s) % NZ for s in range(NZ)]

    line = Line()
    pieces_qk = gather_weights([w_query, w_key])
    pieces_vo = gather_weights([w_value, w_output])
    upstream_all = lax.all_gather(
        after(cotangent, pieces_vo[UPSTREAM_AT]), "expert", axis=0, tiled=True
    ).reshape(NZ, plane * tokens_here, model_width)

    expert_ids = jnp.arange(experts_all, dtype=jnp.int32)
    chosen = routes[:, :, None] == expert_ids[None, None, :]
    uses = jnp.any(chosen, axis=1).astype(f32)
    router_block = jnp.broadcast_to(w_router.astype(f32).reshape(1, -1), (owners, w_router.size))
    small = jnp.concatenate([uses.T, router_block], axis=1)
    small = lax.all_to_all(
        small, "expert", split_axis=0, concat_axis=0, tiled=True
    )
    used_here = small[:, :tokens_here].reshape(NZ, plane * tokens_here, 1)
    own_router = small[:, tokens_here:].reshape(-1, experts_all)
    other_router = move_core(own_router)
    full_router = jnp.where(
        core == 0,
        jnp.concatenate([own_router, other_router], axis=0),
        jnp.concatenate([other_router, own_router], axis=0),
    ).astype(bf16)

    inputs_f32 = hidden_in.astype(f32)
    normed_attn, inverse_attn = norm_forward(inputs_f32, attn_gain)
    act_attn = normed_attn.astype(bf16)
    own_act = lax.dynamic_slice_in_dim(act_attn, core * half_width, half_width, axis=1).T
    other_act = move_core(
        lax.dynamic_slice_in_dim(act_attn, (1 - core) * half_width, half_width, axis=1)
    ).T
    query_pre = apply_weight(position, act_attn, pieces_qk, rows, 0)
    key_pre = apply_weight(position, act_attn, pieces_qk, rows, 1)
    value_low = apply_weight(after(position, small), act_attn, pieces_vo, rows, 0).astype(bf16)
    query_normed, query_inverse = norm_forward(query_pre, query_gain)
    key_normed, key_inverse = norm_forward(key_pre, key_gain)
    cosine, sine_table = rotary_tables(tokens_here, head_dim)
    head_shape = (tokens_here, head_count, head_dim)
    query_rot = rotate(query_normed.reshape(head_shape), cosine, sine_table).astype(bf16)
    key_rot = rotate(key_normed.reshape(head_shape), cosine, sine_table).astype(bf16)
    value_heads = value_low.reshape(head_shape)
    score_scale = head_dim ** (-0.5)
    token_at = jnp.arange(tokens_here, dtype=jnp.int32)
    allowed = (token_at[:, None] >= token_at[None, :]) & (
        doc_ids[0][:, None] == doc_ids[0][None, :]
    )
    scores = (
        jnp.einsum("qhd,khd->hqk", query_rot, key_rot, preferred_element_type=f32) * score_scale
    )
    scores = jnp.where(allowed[None], scores, -1e30)
    row_max = jnp.max(scores, axis=-1, keepdims=True)
    row_sum = jnp.sum(jnp.exp(scores - row_max), axis=-1, keepdims=True)
    log_total = row_max + jnp.log(row_sum)
    probs = jnp.exp(scores - log_total)
    probs_low = probs.astype(bf16)
    attended = jnp.einsum("hqk,khd->qhd", probs_low, value_heads, preferred_element_type=f32)
    attended_low = attended.reshape(tokens_here, model_width).astype(bf16)
    middle = inputs_f32 + apply_weight(position, attended_low, pieces_vo, rows, 1)
    normed_moe, inverse_moe = norm_forward(middle, moe_gain)
    act_moe = normed_moe.astype(bf16)

    logits = jnp.dot(act_moe, full_router, preferred_element_type=f32)
    router_probs = jax.nn.softmax(logits, axis=-1)

    gate_w, up_w, down_w = w_gate[0], w_up[0], w_down[0]
    mine = (expert_ids == here).astype(f32)
    forward, backward, ways = [], [], []
    all_outs = jnp.zeros((NZ, plane * tokens_here, model_width), bf16)
    for s, pieces in enumerate(gather_chips(act_moe)):
        act_rows = jnp.zeros((plane, tokens_here, model_width), bf16)
        for k in range(plane):
            act_rows = lax.dynamic_update_slice(act_rows, pieces[k][None], (places[k], 0, 0))
        act_rows = act_rows.reshape(plane * tokens_here, model_width)
        if s:
            act_rows = after(act_rows, expert_out)
        used = lax.dynamic_index_in_dim(used_here, planes[s], axis=0, keepdims=False)
        probs_rows = jax.nn.softmax(
            jnp.dot(act_rows, full_router, preferred_element_type=f32), axis=-1
        )
        gate_rows = jnp.sum(probs_rows * mine[None, :], axis=-1, keepdims=True) * used
        gate_pre = jnp.dot(act_rows, gate_w, preferred_element_type=f32)
        up_pre = jnp.dot(act_rows, up_w, preferred_element_type=f32)
        sigmoid = jax.nn.sigmoid(gate_pre)
        swish = gate_pre * sigmoid
        hidden_low = (swish * up_pre).astype(bf16)
        expert_out = jnp.dot(hidden_low, down_w, preferred_element_type=f32).astype(bf16)
        out_low = (gate_rows * expert_out.astype(f32)).astype(bf16)
        all_outs = lax.dynamic_update_slice(all_outs, out_low[None], (planes[s], 0, 0))
        forward.append((act_rows, used, gate_rows, gate_pre, up_pre, hidden_low, expert_out))
    rows_reduce = Reduce(line)
    choice_rows = jnp.zeros((NZ, plane * tokens_here, 1), f32)
    for s in range(NZ):
        act_rows, used, gate_rows, gate_pre, up_pre, hidden_low, expert_out = forward[s]
        upstream_rows = lax.dynamic_index_in_dim(upstream_all, planes[s], axis=0, keepdims=False)
        if s:
            upstream_rows = after(upstream_rows, row_grad)
        upstream_f32 = upstream_rows.astype(f32)
        dots = jnp.sum(upstream_f32 * expert_out.astype(f32), axis=-1, keepdims=True) * used
        choice_rows = lax.dynamic_update_slice(choice_rows, dots[None], (planes[s], 0, 0))
        out_grad = (gate_rows * upstream_f32).astype(bf16)
        hidden_grad = times_transposed(out_grad, down_w)
        sigmoid = jax.nn.sigmoid(gate_pre)
        slope = sigmoid * (1.0 + gate_pre * (1.0 - sigmoid))
        gate_pre_grad = (hidden_grad * up_pre * slope).astype(bf16)
        up_pre_grad = (hidden_grad * (gate_pre * sigmoid)).astype(bf16)
        row_grad = (
            times_transposed(gate_pre_grad, gate_w) + times_transposed(up_pre_grad, up_w)
        ).astype(bf16)
        blocks = row_grad.reshape(plane, tokens_here, model_width)
        own, for_x, for_y, across = [
            lax.dynamic_index_in_dim(blocks, places[k], axis=0, keepdims=False)
            for k in range(plane)
        ]
        cut = split_row(tokens_here)
        backward.append((out_grad, gate_pre_grad, up_pre_grad))
        rows_reduce.add(s, [own, for_x, for_y, across[:cut], across[cut:]])
        ways.append(rows_reduce.ways())
    choice_grad = lax.all_to_all(
        choice_rows.reshape(owners, tokens_here), "expert", split_axis=0, concat_axis=0, tiled=True
    ).T
    own_down, other_down = down_grads(
        after(position, *ways[3]), [chunk[5] for chunk in forward], [chunk[0] for chunk in backward]
    )
    moe_in_grad = after(rows_reduce.result(), own_down, other_down)

    logit_grad = router_probs * (
        choice_grad - jnp.sum(router_probs * choice_grad, axis=-1, keepdims=True)
    )
    logit_low = logit_grad.astype(bf16)
    moe_in_grad = moe_in_grad + times_transposed(logit_low, full_router)
    router_grad = inner_product(act_moe, logit_low)
    upstream = cotangent.astype(f32)
    mid_norm_grad, moe_gain_grad = norm_backward(middle, inverse_moe, moe_gain, moe_in_grad)
    mid_grad = upstream + mid_norm_grad
    mid_low = mid_grad.astype(bf16)
    moe_term = lax.psum_scatter(
        after(all_outs, moe_in_grad).reshape(-1, model_width), "expert", scatter_dimension=0, tiled=True
    ).astype(f32)
    own_attended = lax.dynamic_slice_in_dim(attended_low, core * half_width, half_width, axis=1).T
    other_attended = move_core(
        lax.dynamic_slice_in_dim(attended_low, (1 - core) * half_width, half_width, axis=1)
    ).T
    attended_grad = (
        apply_weight(position, mid_low, pieces_vo, rows, 1, back=True)
        .astype(bf16)
        .reshape(head_shape)
    )
    probs_grad = jnp.einsum("qhd,khd->hqk", attended_grad, value_heads, preferred_element_type=f32)
    row_inner = jnp.sum(probs * probs_grad, axis=-1, keepdims=True)
    scores_grad = (probs * (probs_grad - row_inner)).astype(bf16)
    query_rot_grad = (
        jnp.einsum("hqk,khd->qhd", scores_grad, key_rot, preferred_element_type=f32) * score_scale
    )
    key_rot_grad = (
        jnp.einsum("hqk,qhd->khd", scores_grad, query_rot, preferred_element_type=f32) * score_scale
    )
    value_grad = jnp.einsum("hqk,qhd->khd", probs_low, attended_grad, preferred_element_type=f32)
    value_grad = value_grad.reshape(tokens_here, model_width).astype(bf16)
    query_back = rotate_back(query_rot_grad, cosine, sine_table).reshape(tokens_here, model_width)
    key_back = rotate_back(key_rot_grad, cosine, sine_table).reshape(tokens_here, model_width)
    query_pre_grad, query_gain_grad = norm_backward(
        query_pre, query_inverse, query_gain, query_back
    )
    key_pre_grad, key_gain_grad = norm_backward(key_pre, key_inverse, key_gain, key_back)
    query_low = query_pre_grad.astype(bf16)
    key_low = key_pre_grad.astype(bf16)
    attn_grads = []
    for low in (query_low, key_low, value_grad):
        attn_grads += [low, move_core(low)]
    output_grads = [mid_low, move_core(mid_low)]
    weights_reduce = Reduce(line)
    ways = []
    for s in (1, 2, 3, 0):
        at = after(position, *ways[-2]) if len(ways) > 1 else position
        attn_parts = weight_grad_parts(at, own_act, other_act, attn_grads, rows, s)
        output_parts = weight_grad_parts(at, own_attended, other_attended, output_grads, rows, s)
        own_part, for_x, for_y, across = [
            jnp.concatenate(pair, axis=0) for pair in zip(attn_parts, output_parts, strict=True)
        ]
        weights_reduce.add(s, [own_part, for_x, for_y, *jnp.split(across, 2, axis=0)])
        ways.append(weights_reduce.ways())
    query_weight_grad, key_weight_grad, value_weight_grad, output_grad = jnp.split(
        weights_reduce.result(), 4, axis=0
    )
    sums = weights_reduce.planes
    later = after(position, *attn_parts, *output_parts, sums[1])
    act_grad = (
        apply_weight(later, query_low, pieces_qk, rows, 0, back=True)
        + apply_weight(later, key_low, pieces_qk, rows, 1, back=True)
        + apply_weight(later, value_grad, pieces_vo, rows, 0, back=True)
    )
    expert_acts = [chunk[0] for chunk in forward]
    own_gate, other_gate = column_grads(
        after(later, act_grad, sums[2]), expert_acts, [chunk[1] for chunk in backward]
    )
    own_up, other_up = column_grads(
        after(later, own_gate, sums[3]), expert_acts, [chunk[2] for chunk in backward]
    )
    input_norm_grad, attn_gain_grad = norm_backward(inputs_f32, inverse_attn, attn_gain, act_grad)
    input_grad = (mid_grad + input_norm_grad).astype(bf16)

    devices = 2 * owners
    small_grads = jnp.concatenate(
        [
            part.reshape(devices, -1)
            for part in (attn_gain_grad, query_gain_grad, key_gain_grad, moe_gain_grad, router_grad)
        ],
        axis=1,
    )
    small_grads = jnp.sum(
        lax.all_to_all(
            small_grads, ("dp", "expert"), split_axis=0, concat_axis=0, tiled=True
        ),
        axis=0,
    )
    attn_gain_grad, query_gain_grad, key_gain_grad, moe_gain_grad, router_grad = jnp.split(
        small_grads, [rows, 2 * rows, 3 * rows, 4 * rows]
    )

    block_out = (middle + moe_term).astype(bf16)
    down_grad = after(own_down, sums[2]) + move_core(after(other_down, sums[1])).astype(f32)
    gate_weight_grad = own_gate + move_core(other_gate).astype(f32)
    up_weight_grad = own_up + move_core(other_up).astype(f32)
    return (
        block_out,
        input_grad,
        attn_gain_grad,
        query_weight_grad,
        key_weight_grad,
        value_weight_grad,
        query_gain_grad,
        key_gain_grad,
        output_grad,
        moe_gain_grad,
        router_grad.reshape(w_router.shape),
        gate_weight_grad[None],
        up_weight_grad[None],
        down_grad[None],
    )


def solution(mesh):
    body = body_dense if mesh.shape["expert"] == NZ * NY * NX else body_routed
    return jax.shard_map(
        body,
        mesh=mesh,
        in_specs=(
            P(("dp", "expert"), None),
            P(("dp", "expert"), None),
            P(("dp", "expert"), None),
            P(("dp", "expert"), None),
            P(),
            P(("dp", "expert"), None),
            P(("dp", "expert"), None),
            P(("dp", "expert"), None),
            P(),
            P(),
            P(("dp", "expert"), None),
            P(),
            P(("dp", "expert"), None),
            P("expert", None, None),
            P("expert", None, None),
            P("expert", None, None),
        ),
        out_specs=(
            P(("dp", "expert"), None),
            P(("dp", "expert"), None),
            P(("dp", "expert")),
            P(("dp", "expert"), None),
            P(("dp", "expert"), None),
            P(("dp", "expert"), None),
            P(("dp", "expert")),
            P(("dp", "expert")),
            P(("dp", "expert"), None),
            P(("dp", "expert")),
            P(("dp", "expert"), None),
            P("expert", None, "dp"),
            P("expert", None, "dp"),
            P("expert", "dp", None),
        ),
        check_vma=False,
    )
```

```python
import functools
import itertools

import jax
import jax.numpy as jnp
from jax import lax
from jax.experimental import pallas as pl
from jax.experimental.pallas import tpu as pltpu
from jax.sharding import PartitionSpec as P

HD = 128


EPSILON = 1e-05


def norm_forward(values, gain_vector):
    inverse = lax.rsqrt(jnp.mean(values * values, axis=-1, keepdims=True) + EPSILON)
    return (values * inverse * gain_vector, inverse)


def norm_backward(values, inverse, gain_vector, upstream):
    gain_grad = jnp.sum(upstream * values * inverse, axis=0)
    scaled = upstream * gain_vector
    inner_mean = jnp.mean(scaled * values, axis=-1, keepdims=True)
    return (inverse * (scaled - values * inner_mean * inverse * inverse), gain_grad)


def rotary_tables(length, head_dim):
    half_dim = head_dim // 2
    frequency = 10000.0 ** (-jnp.arange(half_dim, dtype=jnp.float32) * 2.0 / head_dim)
    angles = jnp.arange(length, dtype=jnp.float32)[:, None] * frequency[None, :]
    angles = jnp.concatenate([angles, angles], axis=1)
    return (jnp.cos(angles)[:, None, :], jnp.sin(angles)[:, None, :])


def rotate(values, cosine, sine_table):
    half_dim = values.shape[-1] // 2
    turned = jnp.concatenate([-values[..., half_dim:], values[..., :half_dim]], axis=-1)
    return values * cosine + turned * sine_table


def rotate_back(upstream, cosine, sine_table):
    half_dim = upstream.shape[-1] // 2
    with_sine = upstream * sine_table
    turned = jnp.concatenate([with_sine[..., half_dim:], -with_sine[..., :half_dim]], axis=-1)
    return upstream * cosine + turned


def times_transposed(left, right):
    return jnp.einsum("ta,ba->tb", left, right, preferred_element_type=jnp.float32)


def inner_product(left, right):
    return jnp.einsum("ta,tb->ab", left, right, preferred_element_type=jnp.float32)


def body_routed(
    hidden_in,
    cotangent,
    doc_ids,
    routes,
    attn_gain,
    w_query,
    w_key,
    w_value,
    query_gain,
    key_gain,
    w_output,
    moe_gain,
    w_router,
    w_gate,
    w_up,
    w_down,
):
    f32 = jnp.float32
    bf16 = jnp.bfloat16
    tokens_here = hidden_in.shape[0]
    model_width = hidden_in.shape[1]
    head_dim = HD
    head_count = model_width // head_dim
    top_count = routes.shape[1]
    experts_all = w_router.shape[1]
    capacity = tokens_here * top_count * 4 // (3 * experts_all)
    local_experts = w_gate.shape[0]
    owners = lax.axis_size("expert")
    full_query, full_key, full_value, full_output, full_router = (
        lax.all_gather(w_query, ("dp", "expert"), axis=0, tiled=True),
        lax.all_gather(w_key, ("dp", "expert"), axis=0, tiled=True),
        lax.all_gather(w_value, ("dp", "expert"), axis=0, tiled=True),
        lax.all_gather(w_output, ("dp", "expert"), axis=0, tiled=True),
        lax.all_gather(w_router, ("dp", "expert"), axis=0, tiled=True),
    )
    inputs_f32 = hidden_in.astype(f32)
    normed_attn, inverse_attn = norm_forward(inputs_f32, attn_gain)
    act_attn = normed_attn.astype(bf16)
    query_pre = jnp.dot(act_attn, full_query, preferred_element_type=f32)
    key_pre = jnp.dot(act_attn, full_key, preferred_element_type=f32)
    value_low = jnp.dot(act_attn, full_value, preferred_element_type=f32).astype(bf16)
    query_normed, query_inverse = norm_forward(query_pre, query_gain)
    key_normed, key_inverse = norm_forward(key_pre, key_gain)
    cosine, sine_table = rotary_tables(tokens_here, head_dim)
    head_shape = (tokens_here, head_count, head_dim)
    query_rot = rotate(query_normed.reshape(head_shape), cosine, sine_table).astype(bf16)
    key_rot = rotate(key_normed.reshape(head_shape), cosine, sine_table).astype(bf16)
    value_heads = value_low.reshape(head_shape)
    score_scale = head_dim ** (-0.5)
    position = jnp.arange(tokens_here, dtype=jnp.int32)
    allowed = (position[:, None] >= position[None, :]) & (
        doc_ids[0][:, None] == doc_ids[0][None, :]
    )

    def masked_scores():
        scores = (
            jnp.einsum("qhd,khd->hqk", query_rot, key_rot, preferred_element_type=f32) * score_scale
        )
        return jnp.where(allowed[None], scores, -1e30)

    scores = masked_scores()
    row_max = jnp.max(scores, axis=-1, keepdims=True)
    row_sum = jnp.sum(jnp.exp(scores - row_max), axis=-1, keepdims=True)
    log_total = row_max + jnp.log(row_sum)
    probs_low = jnp.exp(scores - log_total).astype(bf16)
    attended = jnp.einsum("hqk,khd->qhd", probs_low, value_heads, preferred_element_type=f32)
    attended_low = attended.reshape(tokens_here, model_width).astype(bf16)
    middle = inputs_f32 + jnp.dot(attended_low, full_output, preferred_element_type=f32)
    normed_moe, inverse_moe = norm_forward(middle, moe_gain)
    act_moe = normed_moe.astype(bf16)
    logits = jnp.dot(act_moe, full_router, preferred_element_type=f32)
    router_probs = jax.nn.softmax(logits, axis=-1)
    expert_ids = jnp.arange(experts_all, dtype=jnp.int32)
    chosen = routes[:, :, None] == expert_ids[None, None, :]
    gate_values = jnp.sum(jnp.where(chosen, router_probs[:, None, :], 0.0), axis=-1)
    flat_routes = routes.reshape(-1)
    onehot = (flat_routes[:, None] == expert_ids[None, :]).astype(jnp.int32)
    slot_of = jnp.sum((jnp.cumsum(onehot, axis=0) - 1) * onehot, axis=1)
    target_slot = flat_routes * capacity + slot_of
    pair_token = jnp.arange(tokens_here * top_count, dtype=jnp.int32) // top_count

    def to_experts(pair_rows):
        buffer = (
            jnp.zeros((experts_all * capacity, model_width), bf16).at[target_slot].set(pair_rows)
        )
        return buffer.reshape(experts_all, capacity, model_width)

    def from_experts(buffer):
        return buffer.reshape(experts_all * capacity, model_width)[target_slot]

    received = lax.all_to_all(
        to_experts(act_moe[pair_token]), "expert", split_axis=0, concat_axis=0, tiled=True
    )
    owner_rows = received.reshape(owners, local_experts, capacity, model_width)
    gate_pre = jnp.einsum("secd,edf->secf", owner_rows, w_gate, preferred_element_type=f32)
    up_pre = jnp.einsum("secd,edf->secf", owner_rows, w_up, preferred_element_type=f32)
    sigmoid = jax.nn.sigmoid(gate_pre)
    swish = gate_pre * sigmoid
    hidden_low = (swish * up_pre).astype(bf16)
    expert_out = jnp.einsum(
        "secf,efd->secd", hidden_low, w_down, preferred_element_type=f32
    ).astype(bf16)
    returned = lax.all_to_all(
        expert_out.reshape(owners * local_experts, capacity, model_width),
        "expert",
        split_axis=0,
        concat_axis=0,
        tiled=True,
    )
    pair_out = from_experts(returned).reshape(tokens_here, top_count, model_width).astype(f32)
    moe_term = jnp.sum(gate_values[:, :, None] * pair_out, axis=1)
    block_out = (middle + moe_term).astype(bf16)
    upstream = cotangent.astype(f32)
    pair_grad = (gate_values[:, :, None] * upstream[:, None, :]).astype(bf16)
    gate_grad = jnp.sum(upstream[:, None, :] * pair_out, axis=-1)
    out_grad = lax.all_to_all(
        to_experts(pair_grad.reshape(-1, model_width)),
        "expert",
        split_axis=0,
        concat_axis=0,
        tiled=True,
    )
    out_grad = out_grad.reshape(owners, local_experts, capacity, model_width)
    hidden_grad = jnp.einsum("secd,efd->secf", out_grad, w_down, preferred_element_type=f32)
    down_grad = jnp.einsum("secf,secd->efd", hidden_low, out_grad, preferred_element_type=f32)
    slope = sigmoid * (1.0 + gate_pre * (1.0 - sigmoid))
    gate_pre_grad = (hidden_grad * up_pre * slope).astype(bf16)
    up_pre_grad = (hidden_grad * swish).astype(bf16)
    row_grad = jnp.einsum("secf,edf->secd", gate_pre_grad, w_gate, preferred_element_type=f32)
    row_grad = (
        row_grad + jnp.einsum("secf,edf->secd", up_pre_grad, w_up, preferred_element_type=f32)
    ).astype(bf16)
    gate_weight_grad = jnp.einsum(
        "secd,secf->edf", owner_rows, gate_pre_grad, preferred_element_type=f32
    )
    up_weight_grad = jnp.einsum(
        "secd,secf->edf", owner_rows, up_pre_grad, preferred_element_type=f32
    )
    gate_weight_grad, up_weight_grad, down_grad = (
        lax.psum_scatter(
            gate_weight_grad.astype(jnp.bfloat16), "dp", scatter_dimension=2, tiled=True
        ).astype(jnp.float32),
        lax.psum_scatter(
            up_weight_grad.astype(jnp.bfloat16), "dp", scatter_dimension=2, tiled=True
        ).astype(jnp.float32),
        lax.psum_scatter(
            down_grad.astype(jnp.bfloat16), "dp", scatter_dimension=1, tiled=True
        ).astype(jnp.float32),
    )
    back_rows = lax.all_to_all(
        row_grad.reshape(owners * local_experts, capacity, model_width),
        "expert",
        split_axis=0,
        concat_axis=0,
        tiled=True,
    )
    moe_in_grad = jnp.sum(
        from_experts(back_rows).reshape(tokens_here, top_count, model_width).astype(f32), axis=1
    )
    choice_grad = jnp.sum(jnp.where(chosen, gate_grad[:, :, None], 0.0), axis=1)
    logit_grad = router_probs * (
        choice_grad - jnp.sum(router_probs * choice_grad, axis=-1, keepdims=True)
    )
    logit_low = logit_grad.astype(bf16)
    moe_in_grad = moe_in_grad + times_transposed(logit_low, full_router)
    router_grad = inner_product(act_moe, logit_low)
    mid_norm_grad, moe_gain_grad = norm_backward(middle, inverse_moe, moe_gain, moe_in_grad)
    mid_grad = upstream + mid_norm_grad
    mid_low = mid_grad.astype(bf16)
    output_grad = inner_product(attended_low, mid_low)
    attended_grad = times_transposed(mid_low, full_output).astype(bf16).reshape(head_shape)
    probs = jnp.exp(masked_scores() - log_total)
    probs_grad = jnp.einsum("qhd,khd->hqk", attended_grad, value_heads, preferred_element_type=f32)
    row_inner = jnp.sum(probs * probs_grad, axis=-1, keepdims=True)
    scores_grad = (probs * (probs_grad - row_inner)).astype(bf16)
    query_rot_grad = (
        jnp.einsum("hqk,khd->qhd", scores_grad, key_rot, preferred_element_type=f32) * score_scale
    )
    key_rot_grad = (
        jnp.einsum("hqk,qhd->khd", scores_grad, query_rot, preferred_element_type=f32) * score_scale
    )
    value_grad = jnp.einsum("hqk,qhd->khd", probs_low, attended_grad, preferred_element_type=f32)
    value_grad = value_grad.reshape(tokens_here, model_width).astype(bf16)
    query_back = rotate_back(query_rot_grad, cosine, sine_table).reshape(tokens_here, model_width)
    key_back = rotate_back(key_rot_grad, cosine, sine_table).reshape(tokens_here, model_width)
    query_pre_grad, query_gain_grad = norm_backward(
        query_pre, query_inverse, query_gain, query_back
    )
    key_pre_grad, key_gain_grad = norm_backward(key_pre, key_inverse, key_gain, key_back)
    query_low = query_pre_grad.astype(bf16)
    key_low = key_pre_grad.astype(bf16)
    act_grad = (
        times_transposed(query_low, full_query)
        + times_transposed(key_low, full_key)
        + times_transposed(value_grad, full_value)
    )
    query_weight_grad = inner_product(act_attn, query_low)
    key_weight_grad = inner_product(act_attn, key_low)
    value_weight_grad = inner_product(act_attn, value_grad)
    input_norm_grad, attn_gain_grad = norm_backward(inputs_f32, inverse_attn, attn_gain, act_grad)
    input_grad = (mid_grad + input_norm_grad).astype(bf16)
    sharded_grads = (
        lax.psum_scatter(attn_gain_grad, ("dp", "expert"), scatter_dimension=0, tiled=True),
        lax.psum_scatter(query_weight_grad, ("dp", "expert"), scatter_dimension=0, tiled=True),
        lax.psum_scatter(key_weight_grad, ("dp", "expert"), scatter_dimension=0, tiled=True),
        lax.psum_scatter(value_weight_grad, ("dp", "expert"), scatter_dimension=0, tiled=True),
        lax.psum_scatter(query_gain_grad, ("dp", "expert"), scatter_dimension=0, tiled=True),
        lax.psum_scatter(key_gain_grad, ("dp", "expert"), scatter_dimension=0, tiled=True),
        lax.psum_scatter(output_grad, ("dp", "expert"), scatter_dimension=0, tiled=True),
        lax.psum_scatter(moe_gain_grad, ("dp", "expert"), scatter_dimension=0, tiled=True),
        lax.psum_scatter(router_grad, ("dp", "expert"), scatter_dimension=0, tiled=True),
    )
    return (
        block_out,
        input_grad,
        sharded_grads[0],
        sharded_grads[1],
        sharded_grads[2],
        sharded_grads[3],
        sharded_grads[4],
        sharded_grads[5],
        sharded_grads[6],
        sharded_grads[7],
        sharded_grads[8],
        gate_weight_grad,
        up_weight_grad,
        down_grad,
    )


NZ, NY, NX = 4, 2, 2
VMEM_LIMIT = 48 * 1024 * 1024
EXPERT_VMEM = 60 * 1024 * 1024


def chip(z, y, x):
    return (z * NY + y) * NX + x


GRID = [(z, y, x) for z in range(NZ) for y in range(NY) for x in range(NX)]
X_PAIRS = [(chip(z, y, x), chip(z, y, 1 - x)) for z, y, x in GRID]
Y_PAIRS = [(chip(z, y, x), chip(z, 1 - y, x)) for z, y, x in GRID]
Z_PAIRS = [(chip(z, y, x), chip((z + 1) % NZ, y, x)) for z, y, x in GRID]
CORE_PAIRS = [(0, 1), (1, 0)]


def move_x(values):
    return lax.ppermute(values, "expert", X_PAIRS)


def move_y(values):
    return lax.ppermute(values, "expert", Y_PAIRS)


def move_z(values):
    return lax.ppermute(values, "expert", Z_PAIRS)


def move_core(values):
    return lax.ppermute(values, "dp", CORE_PAIRS)


def split_row(rows):
    return (rows // 2 + 15) // 16 * 16


def tie(*values):
    return lax.optimization_barrier(values)


def without(kernel, start, count):
    return lambda *refs: kernel(*refs[:start], *refs[start + count :])


def gather_z(block):
    ring = [block]
    for _ in range(1, NZ):
        ring.append(move_z(ring[-1]))
    return ring


def gather_plane(block):
    cut = split_row(block.shape[0])
    from_x = move_x(block)
    from_y = move_y(block)
    across = jnp.concatenate([move_x(from_y[:cut]), move_y(from_x[cut:])], axis=0)
    return [block, from_x, from_y, across]


def gather_chips(block):
    return [gather_plane(part) for part in gather_z(block)]


def add_f32(left, right):
    return left.astype(jnp.float32) + right.astype(jnp.float32)


class Reduce:
    def __init__(self):
        self.planes, self.steps, self.total = {}, 0, None

    def across(self, low, high):
        return move_x(low), move_y(high)

    def finish(self, steps, own, for_x, for_y, by_x, by_y):
        low = own.dtype
        cut = by_x.shape[0]
        for_y = jnp.concatenate([add_f32(for_y[:cut], by_x).astype(low), for_y[cut:]], axis=0)
        for_x = jnp.concatenate([for_x[:cut], add_f32(for_x[cut:], by_y).astype(low)], axis=0)
        total = add_f32(own, move_x(for_x)) + move_y(for_y).astype(jnp.float32)
        for step, part in zip(steps, jnp.split(total, len(steps), axis=0), strict=True):
            self.planes[step] = part

    def push(self):
        while self.steps + 1 < NZ and self.steps + 1 in self.planes:
            self.steps += 1
            total = self.planes[self.steps]
            if self.total is not None:
                total = add_f32(self.total, total)
            self.total = move_z(total.astype(jnp.bfloat16))

    def result(self):
        self.push()
        return add_f32(self.total, self.planes[0])


def place_of(position, k):
    return (position[2] ^ (k >> 1)) * NX + (position[3] ^ (k & 1))


def weight_copies(position, pieces, rows, slot, held, sems, other):
    out = []
    for step in range(NZ):
        z_of = (position[1] + NZ - step) % NZ
        for k in range(NY * NX):
            place = pl.multiple_of((z_of * NY * NX + place_of(position, k)) * rows, rows)
            out.append(
                pltpu.make_async_copy(
                    pieces[other * NZ + step].at[k, pl.ds(slot * rows, rows)],
                    held.at[other, pl.ds(place, rows)],
                    sems.at[other * NZ + step, k],
                )
            )
    return out


def apply_kernel(position, acts, *refs, rows, slot, tile):
    pieces, (out, held, sems) = refs[: 2 * NZ], refs[2 * NZ :]
    for other in range(2):
        for copy in weight_copies(position, pieces, rows, slot, held, sems, other):
            copy.start()
    span = held.shape[1]
    for other in range(2):
        for copy in weight_copies(position, pieces, rows, slot, held, sems, other):
            copy.wait()
        left = acts[:, pl.ds(pl.multiple_of((position[0] ^ other) * span, span), span)]

        @pl.loop(0, out.shape[1] // tile)
        def _(i):
            columns = pl.ds(pl.multiple_of(i * tile, tile), tile)
            part = jnp.dot(left, held[other, :, columns], preferred_element_type=jnp.float32)
            if other == 0:
                out[:, columns] = part
            else:
                out[:, columns] += part


def apply_back_kernel(position, grads, *refs, rows, slot, tile):
    pieces, (out, held, sems) = refs[: 2 * NZ], refs[2 * NZ :]
    for other in range(2):
        for copy in weight_copies(position, pieces, rows, slot, held, sems, other):
            copy.start()
    span = held.shape[1]
    for other in range(2):
        for copy in weight_copies(position, pieces, rows, slot, held, sems, other):
            copy.wait()

        @pl.loop(0, span // tile)
        def _(i):
            lines = pl.ds(pl.multiple_of(i * tile, tile), tile)
            low = pl.multiple_of((position[0] ^ other) * span + i * tile, tile)
            out[:, pl.ds(low, tile)] = lax.dot_general(
                grads[...],
                held[other, lines, :],
                (((1,), (1,)), ((), ())),
                preferred_element_type=jnp.float32,
            )


def apply_weight(position, values, pieces, rows, slot, back=False, waits=()):
    tokens, width = values.shape
    return pl.pallas_call(
        without(
            functools.partial(
                apply_back_kernel if back else apply_kernel, rows=rows, slot=slot, tile=512
            ),
            2 + len(pieces),
            len(waits),
        ),
        out_shape=jax.ShapeDtypeStruct((tokens, width), jnp.float32),
        in_specs=[pl.BlockSpec(memory_space=pltpu.SMEM), pl.BlockSpec(memory_space=pltpu.VMEM)]
        + [pl.BlockSpec(memory_space=pl.ANY)] * (len(pieces) + len(waits)),
        out_specs=pl.BlockSpec(memory_space=pltpu.VMEM),
        scratch_shapes=[
            pltpu.VMEM((2, width // 2, width), jnp.bfloat16),
            pltpu.SemaphoreType.DMA((2 * NZ, NY * NX)),
        ],
        compiler_params=pltpu.CompilerParams(vmem_limit_bytes=VMEM_LIMIT),
        cost_estimate=pl.CostEstimate(
            flops=2 * tokens * width * width,
            bytes_accessed=2 * width * width + 6 * tokens * width,
            transcendentals=0,
        ),
    )(position, values, *pieces, *waits)


def weight_grad_kernel(position, *refs, rows, lefts, steps, tile):
    count = len(lefts)
    turned, grads = refs[: 2 * max(lefts) + 2], refs[2 * max(lefts) + 2 :]
    grads, (own, for_x, for_y, *across, stage) = grads[: 2 * count], grads[2 * count :]
    span = NY * NX * rows
    for p, step in enumerate(steps):
        z_of = (position[1] + NZ - step) % NZ
        lines = pl.ds(pl.multiple_of(z_of * span, span), span)
        for i, left in enumerate(lefts):
            low = p * count * rows + i * rows
            targets = [(own, low), (for_x, low), (for_y, low), (across[p], i * rows)]

            @pl.loop(0, grads[0].shape[1] // tile)
            def _(j):
                part = pl.ds(pl.multiple_of(j * tile, tile), tile)
                product = jnp.dot(
                    turned[2 * left][lines, :],
                    grads[2 * i][:, part],
                    preferred_element_type=jnp.float32,
                ) + jnp.dot(
                    turned[2 * left + 1][lines, :],
                    grads[2 * i + 1][:, part],
                    preferred_element_type=jnp.float32,
                )
                stage[...] = product.astype(stage.dtype)
                for k, (target, at) in enumerate(targets):
                    place = pl.multiple_of(place_of(position, k) * rows, rows)
                    target[pl.ds(at, rows), part] = stage[pl.ds(place, rows), :]


def weight_grad_parts(position, turned, grads, lefts, rows, steps, waits=()):
    count, width = len(lefts), grads[0].shape[1]
    tokens, tile = turned[0].shape[1], 512
    vmem_spec = pl.BlockSpec(memory_space=pltpu.VMEM)
    both = jax.ShapeDtypeStruct((2 * count * rows, width), jnp.bfloat16)
    one = jax.ShapeDtypeStruct((count * rows, width), jnp.bfloat16)
    operands = [*turned, *grads]
    return pl.pallas_call(
        without(
            functools.partial(weight_grad_kernel, rows=rows, lefts=lefts, steps=steps, tile=tile),
            1 + len(operands),
            len(waits),
        ),
        out_shape=[both] * 3 + [one] * 2,
        in_specs=[pl.BlockSpec(memory_space=pltpu.SMEM)]
        + [vmem_spec] * len(operands)
        + [pl.BlockSpec(memory_space=pl.ANY)] * len(waits),
        out_specs=[vmem_spec] * 5,
        scratch_shapes=[pltpu.VMEM((NY * NX * rows, tile), jnp.bfloat16)],
        compiler_params=pltpu.CompilerParams(vmem_limit_bytes=VMEM_LIMIT),
        cost_estimate=pl.CostEstimate(
            flops=8 * count * tokens * NY * NX * rows * width,
            bytes_accessed=4 * count * NY * NX * rows * width + 4 * tokens * width * (count + 1),
            transcendentals=0,
        ),
    )(position, *operands, *waits)


def column_grad_kernel(position, *refs):
    parts = (len(refs) - 2) // 2
    acts, grads, outs = refs[:parts], refs[parts:-2], refs[-2:]
    half = outs[0].shape[1]
    turned = [act[...].T for act in acts]
    for side, out in enumerate(outs):
        columns = pl.ds(pl.multiple_of((position[0] ^ side) * half, half), half)
        total = None
        for act, grad in zip(turned, grads, strict=True):
            more = jnp.dot(act, grad[:, columns], preferred_element_type=jnp.float32)
            total = more if total is None else total + more
        out[...] = total.astype(out.dtype)


def column_grads(position, acts, grads, waits=()):
    parts = len(acts)
    count, width = acts[0].shape
    units = grads[0].shape[1]
    tile = 256
    whole = pl.BlockSpec((count, units), lambda i: (0, 0), pipeline_mode=pl.Buffered(1))
    out = pl.BlockSpec((tile, units // 2), lambda i: (i, 0))
    return pl.pallas_call(
        without(column_grad_kernel, 1 + 2 * parts, len(waits)),
        grid=(width // tile,),
        out_shape=[jax.ShapeDtypeStruct((width, units // 2), t) for t in (jnp.float32, jnp.bfloat16)],
        in_specs=[pl.BlockSpec(memory_space=pltpu.SMEM)]
        + [pl.BlockSpec((count, tile), lambda i: (0, i))] * parts
        + [whole] * parts
        + [pl.BlockSpec(memory_space=pl.ANY)] * len(waits),
        out_specs=[out] * 2,
        compiler_params=pltpu.CompilerParams(vmem_limit_bytes=EXPERT_VMEM),
        cost_estimate=pl.CostEstimate(
            flops=2 * parts * count * width * units,
            bytes_accessed=2 * parts * count * (width + units) + 3 * width * units,
            transcendentals=0,
        ),
    )(position, *acts, *grads, *waits)


def down_grad_kernel(position, *refs):
    parts = (len(refs) - 3) // 2
    hiddens, grads, (own, other, turned) = refs[:parts], refs[parts:-3], refs[-3:]
    tile = 512
    for s, hidden in enumerate(hiddens):
        turned[s] = hidden[...].T

    def part_of(j):
        columns = pl.ds(pl.multiple_of(j * tile, tile), tile)
        total = None
        for s, grad in enumerate(grads):
            more = jnp.dot(turned[s], grad[:, columns], preferred_element_type=jnp.float32)
            total = more if total is None else total + more
        return columns, total

    steps = grads[0].shape[1] // tile

    @pl.when(pl.program_id(0) < pl.num_programs(0) // 2)
    def _():
        @pl.loop(0, steps)
        def _(j):
            columns, total = part_of(j)
            own[:, columns] = total

    @pl.when(pl.program_id(0) >= pl.num_programs(0) // 2)
    def _():
        @pl.loop(0, steps)
        def _(j):
            columns, total = part_of(j)
            other[:, columns] = total.astype(other.dtype)


def down_grads(position, hiddens, grads, waits=()):
    parts = len(hiddens)
    count, units = hiddens[0].shape
    width = grads[0].shape[1]
    tile = 256
    half = units // 2 // tile
    whole = pl.BlockSpec((count, width), lambda i, at: (0, 0), pipeline_mode=pl.Buffered(1))
    return pl.pallas_call(
        without(down_grad_kernel, 1 + 2 * parts, len(waits)),
        grid_spec=pltpu.PrefetchScalarGridSpec(
            num_scalar_prefetch=1,
            grid=(2 * half,),
            in_specs=[
                pl.BlockSpec((count, tile), lambda i, at: (0, (i + at[0] * half) % (2 * half)))
            ]
            * parts
            + [whole] * parts
            + [pl.BlockSpec(memory_space=pl.ANY)] * len(waits),
            out_specs=[
                pl.BlockSpec((tile, width), lambda i, at: (jnp.minimum(i, half - 1), 0)),
                pl.BlockSpec((tile, width), lambda i, at: (jnp.maximum(i - half, 0), 0)),
            ],
            scratch_shapes=[pltpu.VMEM((parts, tile, count), jnp.bfloat16)],
        ),
        out_shape=[
            jax.ShapeDtypeStruct((units // 2, width), jnp.float32),
            jax.ShapeDtypeStruct((units // 2, width), jnp.bfloat16),
        ],
        compiler_params=pltpu.CompilerParams(vmem_limit_bytes=EXPERT_VMEM),
        cost_estimate=pl.CostEstimate(
            flops=2 * parts * count * width * units,
            bytes_accessed=2 * parts * count * (width + units) + 3 * width * units,
            transcendentals=0,
        ),
    )(position, *hiddens, *grads, *waits)


def gather_weights(blocks):
    ring = [jnp.stack(part) for part in gather_chips(jnp.concatenate(blocks, axis=0))]
    return ring + [move_core(part) for part in ring]


def body_dense(
    hidden_in,
    cotangent,
    doc_ids,
    routes,
    attn_gain,
    w_query,
    w_key,
    w_value,
    query_gain,
    key_gain,
    w_output,
    moe_gain,
    w_router,
    w_gate,
    w_up,
    w_down,
):
    f32 = jnp.float32
    bf16 = jnp.bfloat16
    tokens_here, model_width = hidden_in.shape
    head_dim = HD
    head_count = model_width // head_dim
    rows = w_query.shape[0]
    experts_all = w_router.shape[1]
    owners = lax.axis_size("expert")
    core = lax.axis_index("dp")
    here = lax.axis_index("expert")
    z_at, y_at, x_at = here // (NY * NX), here // NX % NY, here % NX
    position = jnp.stack([core, z_at, y_at, x_at, here]).astype(jnp.int32)
    half_width = model_width // 2
    plane = NY * NX
    places = [(y_at ^ (k >> 1)) * NX + (x_at ^ (k & 1)) for k in range(plane)]
    planes = [(z_at + NZ - s) % NZ for s in range(NZ)]

    pieces_qk = gather_weights([w_query, w_key])
    pieces_vo = gather_weights([w_value, w_output])
    upstream, pieces_vo[0] = tie(cotangent, pieces_vo[0])
    upstream_all = lax.all_gather(
        upstream, "expert", axis=0, tiled=True
    ).reshape(NZ, plane * tokens_here, model_width)

    expert_ids = jnp.arange(experts_all, dtype=jnp.int32)
    chosen = routes[:, :, None] == expert_ids[None, None, :]
    uses = jnp.any(chosen, axis=1).astype(f32)
    router_block = jnp.broadcast_to(w_router.astype(f32).reshape(1, -1), (owners, w_router.size))
    small = jnp.concatenate([uses.T, router_block], axis=1)
    small = lax.all_to_all(
        small, "expert", split_axis=0, concat_axis=0, tiled=True
    )
    used_here = small[:, :tokens_here].reshape(NZ, plane * tokens_here, 1)
    own_router = small[:, tokens_here:].reshape(-1, experts_all)
    other_router = move_core(own_router)
    full_router = jnp.where(
        core == 0,
        jnp.concatenate([own_router, other_router], axis=0),
        jnp.concatenate([other_router, own_router], axis=0),
    ).astype(bf16)

    inputs_f32 = hidden_in.astype(f32)
    normed_attn, inverse_attn = norm_forward(inputs_f32, attn_gain)
    act_attn = normed_attn.astype(bf16)
    own_act = lax.dynamic_slice_in_dim(act_attn, core * half_width, half_width, axis=1).T
    other_act = move_core(
        lax.dynamic_slice_in_dim(act_attn, (1 - core) * half_width, half_width, axis=1)
    ).T
    query_pre = apply_weight(position, act_attn, pieces_qk, rows, 0)
    key_pre = apply_weight(position, act_attn, pieces_qk, rows, 1)
    value_low = apply_weight(
        position, act_attn, pieces_vo, rows, 0, waits=(small,)
    ).astype(bf16)
    query_normed, query_inverse = norm_forward(query_pre, query_gain)
    key_normed, key_inverse = norm_forward(key_pre, key_gain)
    cosine, sine_table = rotary_tables(tokens_here, head_dim)
    head_shape = (tokens_here, head_count, head_dim)
    query_rot = rotate(query_normed.reshape(head_shape), cosine, sine_table).astype(bf16)
    key_rot = rotate(key_normed.reshape(head_shape), cosine, sine_table).astype(bf16)
    value_heads = value_low.reshape(head_shape)
    score_scale = head_dim ** (-0.5)
    token_at = jnp.arange(tokens_here, dtype=jnp.int32)
    allowed = (token_at[:, None] >= token_at[None, :]) & (
        doc_ids[0][:, None] == doc_ids[0][None, :]
    )
    scores = (
        jnp.einsum("qhd,khd->hqk", query_rot, key_rot, preferred_element_type=f32) * score_scale
    )
    scores = jnp.where(allowed[None], scores, -1e30)
    row_max = jnp.max(scores, axis=-1, keepdims=True)
    row_sum = jnp.sum(jnp.exp(scores - row_max), axis=-1, keepdims=True)
    log_total = row_max + jnp.log(row_sum)
    probs = jnp.exp(scores - log_total)
    probs_low = probs.astype(bf16)
    attended = jnp.einsum("hqk,khd->qhd", probs_low, value_heads, preferred_element_type=f32)
    attended_low = attended.reshape(tokens_here, model_width).astype(bf16)
    middle = inputs_f32 + apply_weight(position, attended_low, pieces_vo, rows, 1)
    normed_moe, inverse_moe = norm_forward(middle, moe_gain)
    act_moe = normed_moe.astype(bf16)

    logits = jnp.dot(act_moe, full_router, preferred_element_type=f32)
    router_probs = jax.nn.softmax(logits, axis=-1)

    gate_w, up_w, down_w = w_gate[0], w_up[0], w_down[0]
    mine = (expert_ids == here).astype(f32)
    forward, backward = [], []
    for s, pieces in enumerate(gather_chips(act_moe)):
        act_rows = jnp.zeros((plane, tokens_here, model_width), bf16)
        for k in range(plane):
            act_rows = lax.dynamic_update_slice(act_rows, pieces[k][None], (places[k], 0, 0))
        act_rows = act_rows.reshape(plane * tokens_here, model_width)
        used = lax.dynamic_index_in_dim(used_here, planes[s], axis=0, keepdims=False)
        probs_rows = jax.nn.softmax(
            jnp.dot(act_rows, full_router, preferred_element_type=f32), axis=-1
        )
        gate_rows = jnp.sum(probs_rows * mine[None, :], axis=-1, keepdims=True) * used
        gate_pre = jnp.dot(act_rows, gate_w, preferred_element_type=f32)
        up_pre = jnp.dot(act_rows, up_w, preferred_element_type=f32)
        sigmoid = jax.nn.sigmoid(gate_pre)
        swish = gate_pre * sigmoid
        hidden_low = (swish * up_pre).astype(bf16)
        expert_out = jnp.dot(hidden_low, down_w, preferred_element_type=f32).astype(bf16)
        out_low = (gate_rows * expert_out.astype(f32)).astype(bf16)
        forward.append((act_rows, used, gate_rows, gate_pre, up_pre, hidden_low, expert_out, out_low))
    rows_reduce = Reduce()
    choice_rows = jnp.zeros((NZ, plane * tokens_here, 1), f32)
    for s in range(NZ):
        act_rows, used, gate_rows, gate_pre, up_pre, hidden_low, expert_out, _ = forward[s]
        upstream_rows = lax.dynamic_index_in_dim(upstream_all, planes[s], axis=0, keepdims=False)
        if s == NZ - 1:
            upstream_rows, rows_reduce.planes[0] = tie(upstream_rows, rows_reduce.planes[0])
        upstream_f32 = upstream_rows.astype(f32)
        dots = jnp.sum(upstream_f32 * expert_out.astype(f32), axis=-1, keepdims=True) * used
        choice_rows = lax.dynamic_update_slice(choice_rows, dots[None], (planes[s], 0, 0))
        out_grad = (gate_rows * upstream_f32).astype(bf16)
        hidden_grad = times_transposed(out_grad, down_w)
        sigmoid = jax.nn.sigmoid(gate_pre)
        slope = sigmoid * (1.0 + gate_pre * (1.0 - sigmoid))
        gate_pre_grad = (hidden_grad * up_pre * slope).astype(bf16)
        up_pre_grad = (hidden_grad * (gate_pre * sigmoid)).astype(bf16)
        row_grad = (
            times_transposed(gate_pre_grad, gate_w) + times_transposed(up_pre_grad, up_w)
        ).astype(bf16)
        if s == NZ - 1:
            tied = tie(row_grad, *[chunk[7] for chunk in forward])
            row_grad, out_lows = tied[0], tied[1:]
        blocks = row_grad.reshape(plane, tokens_here, model_width)
        own, for_x, for_y, across = [
            lax.dynamic_index_in_dim(blocks, places[k], axis=0, keepdims=False)
            for k in range(plane)
        ]
        cut = split_row(tokens_here)
        backward.append((out_grad, gate_pre_grad, up_pre_grad))
        ways = rows_reduce.across(across[:cut], across[cut:])
        if s:
            rows_reduce.finish([s - 1], *opened)
        opened = (own, for_x, for_y, *ways)
    rows_reduce.finish([NZ - 1], *opened)
    choice_grad = lax.all_to_all(
        choice_rows.reshape(owners, tokens_here), "expert", split_axis=0, concat_axis=0, tiled=True
    ).T
    all_outs = jnp.zeros((NZ, plane * tokens_here, model_width), bf16)
    for s in range(NZ):
        all_outs = lax.dynamic_update_slice(all_outs, out_lows[s][None], (planes[s], 0, 0))
    expert_acts = [chunk[0] for chunk in forward]
    gate_grads = [chunk[1] for chunk in backward]
    moe_in_grad = rows_reduce.result()
    own_gate, other_gate = column_grads(
        position, expert_acts, gate_grads, waits=(rows_reduce.planes[3],)
    )
    moe_in_grad, own_gate, all_outs = tie(moe_in_grad, own_gate, all_outs)

    logit_grad = router_probs * (
        choice_grad - jnp.sum(router_probs * choice_grad, axis=-1, keepdims=True)
    )
    logit_low = logit_grad.astype(bf16)
    moe_in_grad = moe_in_grad + times_transposed(logit_low, full_router)
    router_grad = inner_product(act_moe, logit_low)
    upstream = cotangent.astype(f32)
    mid_norm_grad, moe_gain_grad = norm_backward(middle, inverse_moe, moe_gain, moe_in_grad)
    mid_grad = upstream + mid_norm_grad
    mid_low = mid_grad.astype(bf16)
    moe_term = lax.psum_scatter(
        all_outs.reshape(-1, model_width), "expert", scatter_dimension=0, tiled=True
    ).astype(f32)
    own_attended = lax.dynamic_slice_in_dim(attended_low, core * half_width, half_width, axis=1).T
    other_attended = move_core(
        lax.dynamic_slice_in_dim(attended_low, (1 - core) * half_width, half_width, axis=1)
    ).T
    attended_grad = (
        apply_weight(position, mid_low, pieces_vo, rows, 1, back=True)
        .astype(bf16)
        .reshape(head_shape)
    )
    probs_grad = jnp.einsum("qhd,khd->hqk", attended_grad, value_heads, preferred_element_type=f32)
    row_inner = jnp.sum(probs * probs_grad, axis=-1, keepdims=True)
    scores_grad = (probs * (probs_grad - row_inner)).astype(bf16)
    query_rot_grad = (
        jnp.einsum("hqk,khd->qhd", scores_grad, key_rot, preferred_element_type=f32) * score_scale
    )
    key_rot_grad = (
        jnp.einsum("hqk,qhd->khd", scores_grad, query_rot, preferred_element_type=f32) * score_scale
    )
    value_grad = jnp.einsum("hqk,qhd->khd", probs_low, attended_grad, preferred_element_type=f32)
    value_grad = value_grad.reshape(tokens_here, model_width).astype(bf16)
    query_back = rotate_back(query_rot_grad, cosine, sine_table).reshape(tokens_here, model_width)
    key_back = rotate_back(key_rot_grad, cosine, sine_table).reshape(tokens_here, model_width)
    query_pre_grad, query_gain_grad = norm_backward(
        query_pre, query_inverse, query_gain, query_back
    )
    key_pre_grad, key_gain_grad = norm_backward(key_pre, key_inverse, key_gain, key_back)
    query_low = query_pre_grad.astype(bf16)
    key_low = key_pre_grad.astype(bf16)
    attn_grads = []
    for low in (query_low, key_low, value_grad):
        attn_grads += [low, move_core(low)]
    weights_reduce = Reduce()
    turned = [own_act, other_act, own_attended, other_attended]
    attn_grads += [mid_low, move_core(mid_low)]
    lefts = (0, 0, 0, 1)
    first = weight_grad_parts(position, turned, attn_grads, lefts, rows, (1, 2))
    first_ways = weights_reduce.across(*first[3:])
    last = weight_grad_parts(position, turned, attn_grads, lefts, rows, (3, 0))
    last_ways = weights_reduce.across(*last[3:])
    weights_reduce.finish([1, 2], *first[:3], *first_ways)
    act_grad = (
        apply_weight(position, query_low, pieces_qk, rows, 0, back=True, waits=first_ways)
        + apply_weight(position, key_low, pieces_qk, rows, 1, back=True, waits=first_ways)
        + apply_weight(position, value_grad, pieces_vo, rows, 0, back=True, waits=first_ways)
    )
    up_grads = [chunk[2] for chunk in backward]
    own_up, other_up = column_grads(position, expert_acts, up_grads, waits=(act_grad,))
    weights_reduce.push()
    weights_reduce.finish([3, 0], *last[:3], *last_ways)
    own_down, other_down = down_grads(
        position,
        [chunk[5] for chunk in forward],
        [chunk[0] for chunk in backward],
        waits=(weights_reduce.planes[1], own_up),
    )
    weight_sums, moe_term = tie(weights_reduce.result(), moe_term)
    query_weight_grad, key_weight_grad, value_weight_grad, output_grad = jnp.split(
        weight_sums, 4, axis=0
    )
    input_norm_grad, attn_gain_grad = norm_backward(inputs_f32, inverse_attn, attn_gain, act_grad)
    input_grad = (mid_grad + input_norm_grad).astype(bf16)

    devices = 2 * owners
    small_grads = jnp.concatenate(
        [
            part.reshape(devices, -1)
            for part in (attn_gain_grad, query_gain_grad, key_gain_grad, moe_gain_grad, router_grad)
        ],
        axis=1,
    )
    small_grads = jnp.sum(
        lax.all_to_all(
            small_grads, ("dp", "expert"), split_axis=0, concat_axis=0, tiled=True
        ),
        axis=0,
    )
    attn_gain_grad, query_gain_grad, key_gain_grad, moe_gain_grad, router_grad = jnp.split(
        small_grads, [rows, 2 * rows, 3 * rows, 4 * rows]
    )

    block_out = (middle + moe_term).astype(bf16)
    down_grad = own_down + move_core(other_down).astype(f32)
    gate_weight_grad = own_gate + move_core(other_gate).astype(f32)
    up_weight_grad = own_up + move_core(other_up).astype(f32)
    return (
        block_out,
        input_grad,
        attn_gain_grad,
        query_weight_grad,
        key_weight_grad,
        value_weight_grad,
        query_gain_grad,
        key_gain_grad,
        output_grad,
        moe_gain_grad,
        router_grad.reshape(w_router.shape),
        gate_weight_grad[None],
        up_weight_grad[None],
        down_grad[None],
    )


def solution(mesh):
    body = body_dense if mesh.shape["expert"] == NZ * NY * NX else body_routed
    return jax.shard_map(
        body,
        mesh=mesh,
        in_specs=(
            P(("dp", "expert"), None),
            P(("dp", "expert"), None),
            P(("dp", "expert"), None),
            P(("dp", "expert"), None),
            P(),
            P(("dp", "expert"), None),
            P(("dp", "expert"), None),
            P(("dp", "expert"), None),
            P(),
            P(),
            P(("dp", "expert"), None),
            P(),
            P(("dp", "expert"), None),
            P("expert", None, None),
            P("expert", None, None),
            P("expert", None, None),
        ),
        out_specs=(
            P(("dp", "expert"), None),
            P(("dp", "expert"), None),
            P(("dp", "expert")),
            P(("dp", "expert"), None),
            P(("dp", "expert"), None),
            P(("dp", "expert"), None),
            P(("dp", "expert")),
            P(("dp", "expert")),
            P(("dp", "expert"), None),
            P(("dp", "expert")),
            P(("dp", "expert"), None),
            P("expert", None, "dp"),
            P("expert", None, "dp"),
            P("expert", "dp", None),
        ),
        check_vma=False,
    )
```

```python
import functools
import itertools

import jax
import jax.numpy as jnp
from jax import lax
from jax.experimental import pallas as pl
from jax.experimental.pallas import tpu as pltpu
from jax.sharding import PartitionSpec as P

HD = 128


EPSILON = 1e-05


def norm_forward(values, gain_vector):
    inverse = lax.rsqrt(jnp.mean(values * values, axis=-1, keepdims=True) + EPSILON)
    return (values * inverse * gain_vector, inverse)


def norm_backward(values, inverse, gain_vector, upstream):
    gain_grad = jnp.sum(upstream * values * inverse, axis=0)
    scaled = upstream * gain_vector
    inner_mean = jnp.mean(scaled * values, axis=-1, keepdims=True)
    return (inverse * (scaled - values * inner_mean * inverse * inverse), gain_grad)


def rotary_tables(length, head_dim):
    half_dim = head_dim // 2
    frequency = 10000.0 ** (-jnp.arange(half_dim, dtype=jnp.float32) * 2.0 / head_dim)
    angles = jnp.arange(length, dtype=jnp.float32)[:, None] * frequency[None, :]
    angles = jnp.concatenate([angles, angles], axis=1)
    return (jnp.cos(angles)[:, None, :], jnp.sin(angles)[:, None, :])


def rotate(values, cosine, sine_table):
    half_dim = values.shape[-1] // 2
    turned = jnp.concatenate([-values[..., half_dim:], values[..., :half_dim]], axis=-1)
    return values * cosine + turned * sine_table


def rotate_back(upstream, cosine, sine_table):
    half_dim = upstream.shape[-1] // 2
    with_sine = upstream * sine_table
    turned = jnp.concatenate([with_sine[..., half_dim:], -with_sine[..., :half_dim]], axis=-1)
    return upstream * cosine + turned


def times_transposed(left, right):
    return jnp.einsum("ta,ba->tb", left, right, preferred_element_type=jnp.float32)


def inner_product(left, right):
    return jnp.einsum("ta,tb->ab", left, right, preferred_element_type=jnp.float32)


def body_routed(
    hidden_in,
    cotangent,
    doc_ids,
    routes,
    attn_gain,
    w_query,
    w_key,
    w_value,
    query_gain,
    key_gain,
    w_output,
    moe_gain,
    w_router,
    w_gate,
    w_up,
    w_down,
):
    f32 = jnp.float32
    bf16 = jnp.bfloat16
    tokens_here = hidden_in.shape[0]
    model_width = hidden_in.shape[1]
    head_dim = HD
    head_count = model_width // head_dim
    top_count = routes.shape[1]
    experts_all = w_router.shape[1]
    capacity = tokens_here * top_count * 4 // (3 * experts_all)
    local_experts = w_gate.shape[0]
    owners = lax.axis_size("expert")
    full_query, full_key, full_value, full_output, full_router = (
        lax.all_gather(w_query, ("dp", "expert"), axis=0, tiled=True),
        lax.all_gather(w_key, ("dp", "expert"), axis=0, tiled=True),
        lax.all_gather(w_value, ("dp", "expert"), axis=0, tiled=True),
        lax.all_gather(w_output, ("dp", "expert"), axis=0, tiled=True),
        lax.all_gather(w_router, ("dp", "expert"), axis=0, tiled=True),
    )
    inputs_f32 = hidden_in.astype(f32)
    normed_attn, inverse_attn = norm_forward(inputs_f32, attn_gain)
    act_attn = normed_attn.astype(bf16)
    query_pre = jnp.dot(act_attn, full_query, preferred_element_type=f32)
    key_pre = jnp.dot(act_attn, full_key, preferred_element_type=f32)
    value_low = jnp.dot(act_attn, full_value, preferred_element_type=f32).astype(bf16)
    query_normed, query_inverse = norm_forward(query_pre, query_gain)
    key_normed, key_inverse = norm_forward(key_pre, key_gain)
    cosine, sine_table = rotary_tables(tokens_here, head_dim)
    head_shape = (tokens_here, head_count, head_dim)
    query_rot = rotate(query_normed.reshape(head_shape), cosine, sine_table).astype(bf16)
    key_rot = rotate(key_normed.reshape(head_shape), cosine, sine_table).astype(bf16)
    value_heads = value_low.reshape(head_shape)
    score_scale = head_dim ** (-0.5)
    position = jnp.arange(tokens_here, dtype=jnp.int32)
    allowed = (position[:, None] >= position[None, :]) & (
        doc_ids[0][:, None] == doc_ids[0][None, :]
    )

    def masked_scores():
        scores = (
            jnp.einsum("qhd,khd->hqk", query_rot, key_rot, preferred_element_type=f32) * score_scale
        )
        return jnp.where(allowed[None], scores, -1e30)

    scores = masked_scores()
    row_max = jnp.max(scores, axis=-1, keepdims=True)
    row_sum = jnp.sum(jnp.exp(scores - row_max), axis=-1, keepdims=True)
    log_total = row_max + jnp.log(row_sum)
    probs_low = jnp.exp(scores - log_total).astype(bf16)
    attended = jnp.einsum("hqk,khd->qhd", probs_low, value_heads, preferred_element_type=f32)
    attended_low = attended.reshape(tokens_here, model_width).astype(bf16)
    middle = inputs_f32 + jnp.dot(attended_low, full_output, preferred_element_type=f32)
    normed_moe, inverse_moe = norm_forward(middle, moe_gain)
    act_moe = normed_moe.astype(bf16)
    logits = jnp.dot(act_moe, full_router, preferred_element_type=f32)
    router_probs = jax.nn.softmax(logits, axis=-1)
    expert_ids = jnp.arange(experts_all, dtype=jnp.int32)
    chosen = routes[:, :, None] == expert_ids[None, None, :]
    gate_values = jnp.sum(jnp.where(chosen, router_probs[:, None, :], 0.0), axis=-1)
    flat_routes = routes.reshape(-1)
    onehot = (flat_routes[:, None] == expert_ids[None, :]).astype(jnp.int32)
    slot_of = jnp.sum((jnp.cumsum(onehot, axis=0) - 1) * onehot, axis=1)
    target_slot = flat_routes * capacity + slot_of
    pair_token = jnp.arange(tokens_here * top_count, dtype=jnp.int32) // top_count

    def to_experts(pair_rows):
        buffer = (
            jnp.zeros((experts_all * capacity, model_width), bf16).at[target_slot].set(pair_rows)
        )
        return buffer.reshape(experts_all, capacity, model_width)

    def from_experts(buffer):
        return buffer.reshape(experts_all * capacity, model_width)[target_slot]

    received = lax.all_to_all(
        to_experts(act_moe[pair_token]), "expert", split_axis=0, concat_axis=0, tiled=True
    )
    owner_rows = received.reshape(owners, local_experts, capacity, model_width)
    gate_pre = jnp.einsum("secd,edf->secf", owner_rows, w_gate, preferred_element_type=f32)
    up_pre = jnp.einsum("secd,edf->secf", owner_rows, w_up, preferred_element_type=f32)
    sigmoid = jax.nn.sigmoid(gate_pre)
    swish = gate_pre * sigmoid
    hidden_low = (swish * up_pre).astype(bf16)
    expert_out = jnp.einsum(
        "secf,efd->secd", hidden_low, w_down, preferred_element_type=f32
    ).astype(bf16)
    returned = lax.all_to_all(
        expert_out.reshape(owners * local_experts, capacity, model_width),
        "expert",
        split_axis=0,
        concat_axis=0,
        tiled=True,
    )
    pair_out = from_experts(returned).reshape(tokens_here, top_count, model_width).astype(f32)
    moe_term = jnp.sum(gate_values[:, :, None] * pair_out, axis=1)
    block_out = (middle + moe_term).astype(bf16)
    upstream = cotangent.astype(f32)
    pair_grad = (gate_values[:, :, None] * upstream[:, None, :]).astype(bf16)
    gate_grad = jnp.sum(upstream[:, None, :] * pair_out, axis=-1)
    out_grad = lax.all_to_all(
        to_experts(pair_grad.reshape(-1, model_width)),
        "expert",
        split_axis=0,
        concat_axis=0,
        tiled=True,
    )
    out_grad = out_grad.reshape(owners, local_experts, capacity, model_width)
    hidden_grad = jnp.einsum("secd,efd->secf", out_grad, w_down, preferred_element_type=f32)
    down_grad = jnp.einsum("secf,secd->efd", hidden_low, out_grad, preferred_element_type=f32)
    slope = sigmoid * (1.0 + gate_pre * (1.0 - sigmoid))
    gate_pre_grad = (hidden_grad * up_pre * slope).astype(bf16)
    up_pre_grad = (hidden_grad * swish).astype(bf16)
    row_grad = jnp.einsum("secf,edf->secd", gate_pre_grad, w_gate, preferred_element_type=f32)
    row_grad = (
        row_grad + jnp.einsum("secf,edf->secd", up_pre_grad, w_up, preferred_element_type=f32)
    ).astype(bf16)
    gate_weight_grad = jnp.einsum(
        "secd,secf->edf", owner_rows, gate_pre_grad, preferred_element_type=f32
    )
    up_weight_grad = jnp.einsum(
        "secd,secf->edf", owner_rows, up_pre_grad, preferred_element_type=f32
    )
    gate_weight_grad, up_weight_grad, down_grad = (
        lax.psum_scatter(
            gate_weight_grad.astype(jnp.bfloat16), "dp", scatter_dimension=2, tiled=True
        ).astype(jnp.float32),
        lax.psum_scatter(
            up_weight_grad.astype(jnp.bfloat16), "dp", scatter_dimension=2, tiled=True
        ).astype(jnp.float32),
        lax.psum_scatter(
            down_grad.astype(jnp.bfloat16), "dp", scatter_dimension=1, tiled=True
        ).astype(jnp.float32),
    )
    back_rows = lax.all_to_all(
        row_grad.reshape(owners * local_experts, capacity, model_width),
        "expert",
        split_axis=0,
        concat_axis=0,
        tiled=True,
    )
    moe_in_grad = jnp.sum(
        from_experts(back_rows).reshape(tokens_here, top_count, model_width).astype(f32), axis=1
    )
    choice_grad = jnp.sum(jnp.where(chosen, gate_grad[:, :, None], 0.0), axis=1)
    logit_grad = router_probs * (
        choice_grad - jnp.sum(router_probs * choice_grad, axis=-1, keepdims=True)
    )
    logit_low = logit_grad.astype(bf16)
    moe_in_grad = moe_in_grad + times_transposed(logit_low, full_router)
    router_grad = inner_product(act_moe, logit_low)
    mid_norm_grad, moe_gain_grad = norm_backward(middle, inverse_moe, moe_gain, moe_in_grad)
    mid_grad = upstream + mid_norm_grad
    mid_low = mid_grad.astype(bf16)
    output_grad = inner_product(attended_low, mid_low)
    attended_grad = times_transposed(mid_low, full_output).astype(bf16).reshape(head_shape)
    probs = jnp.exp(masked_scores() - log_total)
    probs_grad = jnp.einsum("qhd,khd->hqk", attended_grad, value_heads, preferred_element_type=f32)
    row_inner = jnp.sum(probs * probs_grad, axis=-1, keepdims=True)
    scores_grad = (probs * (probs_grad - row_inner)).astype(bf16)
    query_rot_grad = (
        jnp.einsum("hqk,khd->qhd", scores_grad, key_rot, preferred_element_type=f32) * score_scale
    )
    key_rot_grad = (
        jnp.einsum("hqk,qhd->khd", scores_grad, query_rot, preferred_element_type=f32) * score_scale
    )
    value_grad = jnp.einsum("hqk,qhd->khd", probs_low, attended_grad, preferred_element_type=f32)
    value_grad = value_grad.reshape(tokens_here, model_width).astype(bf16)
    query_back = rotate_back(query_rot_grad, cosine, sine_table).reshape(tokens_here, model_width)
    key_back = rotate_back(key_rot_grad, cosine, sine_table).reshape(tokens_here, model_width)
    query_pre_grad, query_gain_grad = norm_backward(
        query_pre, query_inverse, query_gain, query_back
    )
    key_pre_grad, key_gain_grad = norm_backward(key_pre, key_inverse, key_gain, key_back)
    query_low = query_pre_grad.astype(bf16)
    key_low = key_pre_grad.astype(bf16)
    act_grad = (
        times_transposed(query_low, full_query)
        + times_transposed(key_low, full_key)
        + times_transposed(value_grad, full_value)
    )
    query_weight_grad = inner_product(act_attn, query_low)
    key_weight_grad = inner_product(act_attn, key_low)
    value_weight_grad = inner_product(act_attn, value_grad)
    input_norm_grad, attn_gain_grad = norm_backward(inputs_f32, inverse_attn, attn_gain, act_grad)
    input_grad = (mid_grad + input_norm_grad).astype(bf16)
    sharded_grads = (
        lax.psum_scatter(attn_gain_grad, ("dp", "expert"), scatter_dimension=0, tiled=True),
        lax.psum_scatter(query_weight_grad, ("dp", "expert"), scatter_dimension=0, tiled=True),
        lax.psum_scatter(key_weight_grad, ("dp", "expert"), scatter_dimension=0, tiled=True),
        lax.psum_scatter(value_weight_grad, ("dp", "expert"), scatter_dimension=0, tiled=True),
        lax.psum_scatter(query_gain_grad, ("dp", "expert"), scatter_dimension=0, tiled=True),
        lax.psum_scatter(key_gain_grad, ("dp", "expert"), scatter_dimension=0, tiled=True),
        lax.psum_scatter(output_grad, ("dp", "expert"), scatter_dimension=0, tiled=True),
        lax.psum_scatter(moe_gain_grad, ("dp", "expert"), scatter_dimension=0, tiled=True),
        lax.psum_scatter(router_grad, ("dp", "expert"), scatter_dimension=0, tiled=True),
    )
    return (
        block_out,
        input_grad,
        sharded_grads[0],
        sharded_grads[1],
        sharded_grads[2],
        sharded_grads[3],
        sharded_grads[4],
        sharded_grads[5],
        sharded_grads[6],
        sharded_grads[7],
        sharded_grads[8],
        gate_weight_grad,
        up_weight_grad,
        down_grad,
    )


NZ, NY, NX = 4, 2, 2
VMEM_LIMIT = 48 * 1024 * 1024
EXPERT_VMEM = 60 * 1024 * 1024


def chip(z, y, x):
    return (z * NY + y) * NX + x


GRID = [(z, y, x) for z in range(NZ) for y in range(NY) for x in range(NX)]
X_PAIRS = [(chip(z, y, x), chip(z, y, 1 - x)) for z, y, x in GRID]
Y_PAIRS = [(chip(z, y, x), chip(z, 1 - y, x)) for z, y, x in GRID]
Z_PAIRS = [(chip(z, y, x), chip((z + 1) % NZ, y, x)) for z, y, x in GRID]
CORE_PAIRS = [(0, 1), (1, 0)]


def move_x(values):
    return lax.ppermute(values, "expert", X_PAIRS)


def move_y(values):
    return lax.ppermute(values, "expert", Y_PAIRS)


def move_z(values):
    return lax.ppermute(values, "expert", Z_PAIRS)


def move_core(values):
    return lax.ppermute(values, "dp", CORE_PAIRS)


def split_row(rows):
    return (rows // 2 + 15) // 16 * 16


def tie(*values):
    return lax.optimization_barrier(values)


def without(kernel, start, count):
    return lambda *refs: kernel(*refs[:start], *refs[start + count :])


def gather_z(block):
    ring = [block]
    for _ in range(1, NZ):
        ring.append(move_z(ring[-1]))
    return ring


def gather_plane(block):
    cut = split_row(block.shape[0])
    from_x = move_x(block)
    from_y = move_y(block)
    across = jnp.concatenate([move_x(from_y[:cut]), move_y(from_x[cut:])], axis=0)
    return [block, from_x, from_y, across]


def gather_chips(block):
    return [gather_plane(part) for part in gather_z(block)]


def add_f32(left, right):
    return left.astype(jnp.float32) + right.astype(jnp.float32)


class Reduce:
    def __init__(self):
        self.planes, self.steps, self.total = {}, 0, None

    def across(self, low, high):
        return move_x(low), move_y(high)

    def finish(self, steps, own, for_x, for_y, by_x, by_y):
        low = own.dtype
        cut = by_x.shape[0]
        for_y = jnp.concatenate([add_f32(for_y[:cut], by_x).astype(low), for_y[cut:]], axis=0)
        for_x = jnp.concatenate([for_x[:cut], add_f32(for_x[cut:], by_y).astype(low)], axis=0)
        total = add_f32(own, move_x(for_x)) + move_y(for_y).astype(jnp.float32)
        for step, part in zip(steps, jnp.split(total, len(steps), axis=0), strict=True):
            self.planes[step] = part

    def push(self):
        while self.steps + 1 < NZ and self.steps + 1 in self.planes:
            self.steps += 1
            total = self.planes[self.steps]
            if self.total is not None:
                total = add_f32(self.total, total)
            self.total = move_z(total.astype(jnp.bfloat16))

    def result(self):
        self.push()
        return add_f32(self.total, self.planes[0])


def place_of(position, k):
    return (position[2] ^ (k >> 1)) * NX + (position[3] ^ (k & 1))


def weight_copies(position, pieces, rows, slot, held, sems, other):
    out = []
    for step in range(NZ):
        z_of = (position[1] + NZ - step) % NZ
        for k in range(NY * NX):
            place = pl.multiple_of((z_of * NY * NX + place_of(position, k)) * rows, rows)
            out.append(
                pltpu.make_async_copy(
                    pieces[other * NZ + step].at[k, pl.ds(slot * rows, rows)],
                    held.at[other, pl.ds(place, rows)],
                    sems.at[other * NZ + step, k],
                )
            )
    return out


def apply_kernel(position, acts, *refs, rows, slot, tile):
    pieces, (out, held, sems) = refs[: 2 * NZ], refs[2 * NZ :]
    for other in range(2):
        for copy in weight_copies(position, pieces, rows, slot, held, sems, other):
            copy.start()
    span = held.shape[1]
    for other in range(2):
        for copy in weight_copies(position, pieces, rows, slot, held, sems, other):
            copy.wait()
        left = acts[:, pl.ds(pl.multiple_of((position[0] ^ other) * span, span), span)]

        @pl.loop(0, out.shape[1] // tile)
        def _(i):
            columns = pl.ds(pl.multiple_of(i * tile, tile), tile)
            part = jnp.dot(left, held[other, :, columns], preferred_element_type=jnp.float32)
            if other == 0:
                out[:, columns] = part
            else:
                out[:, columns] += part


def apply_back_kernel(position, grads, *refs, rows, slot, tile):
    pieces, (out, held, sems) = refs[: 2 * NZ], refs[2 * NZ :]
    for other in range(2):
        for copy in weight_copies(position, pieces, rows, slot, held, sems, other):
            copy.start()
    span = held.shape[1]
    for other in range(2):
        for copy in weight_copies(position, pieces, rows, slot, held, sems, other):
            copy.wait()

        @pl.loop(0, span // tile)
        def _(i):
            lines = pl.ds(pl.multiple_of(i * tile, tile), tile)
            low = pl.multiple_of((position[0] ^ other) * span + i * tile, tile)
            out[:, pl.ds(low, tile)] = lax.dot_general(
                grads[...],
                held[other, lines, :],
                (((1,), (1,)), ((), ())),
                preferred_element_type=jnp.float32,
            )


def apply_weight(position, values, pieces, rows, slot, back=False, waits=()):
    tokens, width = values.shape
    return pl.pallas_call(
        without(
            functools.partial(
                apply_back_kernel if back else apply_kernel, rows=rows, slot=slot, tile=512
            ),
            2 + len(pieces),
            len(waits),
        ),
        out_shape=jax.ShapeDtypeStruct((tokens, width), jnp.float32),
        in_specs=[pl.BlockSpec(memory_space=pltpu.SMEM), pl.BlockSpec(memory_space=pltpu.VMEM)]
        + [pl.BlockSpec(memory_space=pl.ANY)] * (len(pieces) + len(waits)),
        out_specs=pl.BlockSpec(memory_space=pltpu.VMEM),
        scratch_shapes=[
            pltpu.VMEM((2, width // 2, width), jnp.bfloat16),
            pltpu.SemaphoreType.DMA((2 * NZ, NY * NX)),
        ],
        compiler_params=pltpu.CompilerParams(vmem_limit_bytes=VMEM_LIMIT),
        cost_estimate=pl.CostEstimate(
            flops=2 * tokens * width * width,
            bytes_accessed=2 * width * width + 6 * tokens * width,
            transcendentals=0,
        ),
    )(position, values, *pieces, *waits)


def weight_grad_kernel(position, *refs, rows, lefts, steps, tile):
    count = len(lefts)
    turned, grads = refs[: 2 * max(lefts) + 2], refs[2 * max(lefts) + 2 :]
    grads, (own, for_x, for_y, *across, stage) = grads[: 2 * count], grads[2 * count :]
    span = NY * NX * rows
    for p, step in enumerate(steps):
        z_of = (position[1] + NZ - step) % NZ
        lines = pl.ds(pl.multiple_of(z_of * span, span), span)
        for i, left in enumerate(lefts):
            low = p * count * rows + i * rows
            targets = [(own, low), (for_x, low), (for_y, low), (across[p], i * rows)]

            @pl.loop(0, grads[0].shape[1] // tile)
            def _(j):
                part = pl.ds(pl.multiple_of(j * tile, tile), tile)
                product = jnp.dot(
                    turned[2 * left][lines, :],
                    grads[2 * i][:, part],
                    preferred_element_type=jnp.float32,
                ) + jnp.dot(
                    turned[2 * left + 1][lines, :],
                    grads[2 * i + 1][:, part],
                    preferred_element_type=jnp.float32,
                )
                stage[...] = product.astype(stage.dtype)
                for k, (target, at) in enumerate(targets):
                    place = pl.multiple_of(place_of(position, k) * rows, rows)
                    target[pl.ds(at, rows), part] = stage[pl.ds(place, rows), :]


def weight_grad_parts(position, turned, grads, lefts, rows, steps, waits=()):
    count, width = len(lefts), grads[0].shape[1]
    tokens, tile = turned[0].shape[1], 512
    vmem_spec = pl.BlockSpec(memory_space=pltpu.VMEM)
    both = jax.ShapeDtypeStruct((2 * count * rows, width), jnp.bfloat16)
    one = jax.ShapeDtypeStruct((count * rows, width), jnp.bfloat16)
    operands = [*turned, *grads]
    return pl.pallas_call(
        without(
            functools.partial(weight_grad_kernel, rows=rows, lefts=lefts, steps=steps, tile=tile),
            1 + len(operands),
            len(waits),
        ),
        out_shape=[both] * 3 + [one] * 2,
        in_specs=[pl.BlockSpec(memory_space=pltpu.SMEM)]
        + [vmem_spec] * len(operands)
        + [pl.BlockSpec(memory_space=pl.ANY)] * len(waits),
        out_specs=[vmem_spec] * 5,
        scratch_shapes=[pltpu.VMEM((NY * NX * rows, tile), jnp.bfloat16)],
        compiler_params=pltpu.CompilerParams(vmem_limit_bytes=VMEM_LIMIT),
        cost_estimate=pl.CostEstimate(
            flops=8 * count * tokens * NY * NX * rows * width,
            bytes_accessed=4 * count * NY * NX * rows * width + 4 * tokens * width * (count + 1),
            transcendentals=0,
        ),
    )(position, *operands, *waits)


def column_grad_kernel(position, *refs):
    parts = (len(refs) - 2) // 2
    acts, grads, outs = refs[:parts], refs[parts:-2], refs[-2:]
    half = outs[0].shape[1]
    turned = [act[...].T for act in acts]
    for side, out in enumerate(outs):
        columns = pl.ds(pl.multiple_of((position[0] ^ side) * half, half), half)
        total = None
        for act, grad in zip(turned, grads, strict=True):
            more = jnp.dot(act, grad[:, columns], preferred_element_type=jnp.float32)
            total = more if total is None else total + more
        out[...] = total.astype(out.dtype)


def column_grads(position, acts, grads, waits=()):
    parts = len(acts)
    count, width = acts[0].shape
    units = grads[0].shape[1]
    tile = 256
    whole = pl.BlockSpec((count, units), lambda i: (0, 0), pipeline_mode=pl.Buffered(1))
    out = pl.BlockSpec((tile, units // 2), lambda i: (i, 0))
    return pl.pallas_call(
        without(column_grad_kernel, 1 + 2 * parts, len(waits)),
        grid=(width // tile,),
        out_shape=[jax.ShapeDtypeStruct((width, units // 2), t) for t in (jnp.float32, jnp.bfloat16)],
        in_specs=[pl.BlockSpec(memory_space=pltpu.SMEM)]
        + [pl.BlockSpec((count, tile), lambda i: (0, i))] * parts
        + [whole] * parts
        + [pl.BlockSpec(memory_space=pl.ANY)] * len(waits),
        out_specs=[out] * 2,
        compiler_params=pltpu.CompilerParams(vmem_limit_bytes=EXPERT_VMEM),
        cost_estimate=pl.CostEstimate(
            flops=2 * parts * count * width * units,
            bytes_accessed=2 * parts * count * (width + units) + 3 * width * units,
            transcendentals=0,
        ),
    )(position, *acts, *grads, *waits)


def down_grad_kernel(position, *refs):
    parts = (len(refs) - 3) // 2
    hiddens, grads, (own, other, turned) = refs[:parts], refs[parts:-3], refs[-3:]
    tile = 512
    for s, hidden in enumerate(hiddens):
        turned[s] = hidden[...].T

    def part_of(j):
        columns = pl.ds(pl.multiple_of(j * tile, tile), tile)
        total = None
        for s, grad in enumerate(grads):
            more = jnp.dot(turned[s], grad[:, columns], preferred_element_type=jnp.float32)
            total = more if total is None else total + more
        return columns, total

    steps = grads[0].shape[1] // tile

    @pl.when(pl.program_id(0) < pl.num_programs(0) // 2)
    def _():
        @pl.loop(0, steps)
        def _(j):
            columns, total = part_of(j)
            own[:, columns] = total

    @pl.when(pl.program_id(0) >= pl.num_programs(0) // 2)
    def _():
        @pl.loop(0, steps)
        def _(j):
            columns, total = part_of(j)
            other[:, columns] = total.astype(other.dtype)


def down_grads(position, hiddens, grads, waits=()):
    parts = len(hiddens)
    count, units = hiddens[0].shape
    width = grads[0].shape[1]
    tile = 256
    half = units // 2 // tile
    whole = pl.BlockSpec((count, width), lambda i, at: (0, 0), pipeline_mode=pl.Buffered(1))
    return pl.pallas_call(
        without(down_grad_kernel, 1 + 2 * parts, len(waits)),
        grid_spec=pltpu.PrefetchScalarGridSpec(
            num_scalar_prefetch=1,
            grid=(2 * half,),
            in_specs=[
                pl.BlockSpec((count, tile), lambda i, at: (0, (i + at[0] * half) % (2 * half)))
            ]
            * parts
            + [whole] * parts
            + [pl.BlockSpec(memory_space=pl.ANY)] * len(waits),
            out_specs=[
                pl.BlockSpec((tile, width), lambda i, at: (jnp.minimum(i, half - 1), 0)),
                pl.BlockSpec((tile, width), lambda i, at: (jnp.maximum(i - half, 0), 0)),
            ],
            scratch_shapes=[pltpu.VMEM((parts, tile, count), jnp.bfloat16)],
        ),
        out_shape=[
            jax.ShapeDtypeStruct((units // 2, width), jnp.float32),
            jax.ShapeDtypeStruct((units // 2, width), jnp.bfloat16),
        ],
        compiler_params=pltpu.CompilerParams(vmem_limit_bytes=EXPERT_VMEM),
        cost_estimate=pl.CostEstimate(
            flops=2 * parts * count * width * units,
            bytes_accessed=2 * parts * count * (width + units) + 3 * width * units,
            transcendentals=0,
        ),
    )(position, *hiddens, *grads, *waits)


def gather_weights(blocks):
    ring = [jnp.stack(part) for part in gather_chips(jnp.concatenate(blocks, axis=0))]
    return ring + [move_core(part) for part in ring]


def body_dense(
    hidden_in,
    cotangent,
    doc_ids,
    routes,
    attn_gain,
    w_query,
    w_key,
    w_value,
    query_gain,
    key_gain,
    w_output,
    moe_gain,
    w_router,
    w_gate,
    w_up,
    w_down,
):
    f32 = jnp.float32
    bf16 = jnp.bfloat16
    tokens_here, model_width = hidden_in.shape
    head_dim = HD
    head_count = model_width // head_dim
    rows = w_query.shape[0]
    experts_all = w_router.shape[1]
    owners = lax.axis_size("expert")
    core = lax.axis_index("dp")
    here = lax.axis_index("expert")
    z_at, y_at, x_at = here // (NY * NX), here // NX % NY, here % NX
    position = jnp.stack([core, z_at, y_at, x_at, here]).astype(jnp.int32)
    half_width = model_width // 2
    plane = NY * NX
    places = [(y_at ^ (k >> 1)) * NX + (x_at ^ (k & 1)) for k in range(plane)]
    planes = [(z_at + NZ - s) % NZ for s in range(NZ)]

    pieces_qk = gather_weights([w_query, w_key])
    pieces_vo = gather_weights([w_value, w_output])
    upstream, pieces_vo[0] = tie(cotangent, pieces_vo[0])
    upstream_all = lax.all_gather(
        upstream, "expert", axis=0, tiled=True
    ).reshape(NZ, plane * tokens_here, model_width)

    expert_ids = jnp.arange(experts_all, dtype=jnp.int32)
    chosen = routes[:, :, None] == expert_ids[None, None, :]
    uses = jnp.any(chosen, axis=1).astype(f32)
    router_block = jnp.broadcast_to(w_router.astype(f32).reshape(1, -1), (owners, w_router.size))
    small = jnp.concatenate([uses.T, router_block], axis=1)
    small = lax.all_to_all(
        small, "expert", split_axis=0, concat_axis=0, tiled=True
    )
    used_here = small[:, :tokens_here].reshape(NZ, plane * tokens_here, 1)
    own_router = small[:, tokens_here:].reshape(-1, experts_all)
    other_router = move_core(own_router)
    full_router = jnp.where(
        core == 0,
        jnp.concatenate([own_router, other_router], axis=0),
        jnp.concatenate([other_router, own_router], axis=0),
    ).astype(bf16)

    inputs_f32 = hidden_in.astype(f32)
    normed_attn, inverse_attn = norm_forward(inputs_f32, attn_gain)
    act_attn = normed_attn.astype(bf16)
    own_act = lax.dynamic_slice_in_dim(act_attn, core * half_width, half_width, axis=1).T
    other_act = move_core(
        lax.dynamic_slice_in_dim(act_attn, (1 - core) * half_width, half_width, axis=1)
    ).T
    query_pre = apply_weight(position, act_attn, pieces_qk, rows, 0)
    key_pre = apply_weight(position, act_attn, pieces_qk, rows, 1)
    value_low = apply_weight(
        position, act_attn, pieces_vo, rows, 0, waits=(small,)
    ).astype(bf16)
    query_normed, query_inverse = norm_forward(query_pre, query_gain)
    key_normed, key_inverse = norm_forward(key_pre, key_gain)
    cosine, sine_table = rotary_tables(tokens_here, head_dim)
    head_shape = (tokens_here, head_count, head_dim)
    query_rot = rotate(query_normed.reshape(head_shape), cosine, sine_table).astype(bf16)
    key_rot = rotate(key_normed.reshape(head_shape), cosine, sine_table).astype(bf16)
    value_heads = value_low.reshape(head_shape)
    score_scale = head_dim ** (-0.5)
    token_at = jnp.arange(tokens_here, dtype=jnp.int32)
    allowed = (token_at[:, None] >= token_at[None, :]) & (
        doc_ids[0][:, None] == doc_ids[0][None, :]
    )
    scores = (
        jnp.einsum("qhd,khd->hqk", query_rot, key_rot, preferred_element_type=f32) * score_scale
    )
    scores = jnp.where(allowed[None], scores, -1e30)
    row_max = jnp.max(scores, axis=-1, keepdims=True)
    row_sum = jnp.sum(jnp.exp(scores - row_max), axis=-1, keepdims=True)
    log_total = row_max + jnp.log(row_sum)
    probs = jnp.exp(scores - log_total)
    probs_low = probs.astype(bf16)
    attended = jnp.einsum("hqk,khd->qhd", probs_low, value_heads, preferred_element_type=f32)
    attended_low = attended.reshape(tokens_here, model_width).astype(bf16)
    middle = inputs_f32 + apply_weight(position, attended_low, pieces_vo, rows, 1)
    normed_moe, inverse_moe = norm_forward(middle, moe_gain)
    act_moe = normed_moe.astype(bf16)

    logits = jnp.dot(act_moe, full_router, preferred_element_type=f32)
    router_probs = jax.nn.softmax(logits, axis=-1)

    gate_w, up_w, down_w = w_gate[0], w_up[0], w_down[0]
    mine = (expert_ids == here).astype(f32)
    forward, backward = [], []
    for s, pieces in enumerate(gather_chips(act_moe)):
        act_rows = jnp.zeros((plane, tokens_here, model_width), bf16)
        for k in range(plane):
            act_rows = lax.dynamic_update_slice(act_rows, pieces[k][None], (places[k], 0, 0))
        act_rows = act_rows.reshape(plane * tokens_here, model_width)
        used = lax.dynamic_index_in_dim(used_here, planes[s], axis=0, keepdims=False)
        probs_rows = jax.nn.softmax(
            jnp.dot(act_rows, full_router, preferred_element_type=f32), axis=-1
        )
        gate_rows = jnp.sum(probs_rows * mine[None, :], axis=-1, keepdims=True) * used
        gate_pre = jnp.dot(act_rows, gate_w, preferred_element_type=f32)
        up_pre = jnp.dot(act_rows, up_w, preferred_element_type=f32)
        sigmoid = jax.nn.sigmoid(gate_pre)
        swish = gate_pre * sigmoid
        hidden_low = (swish * up_pre).astype(bf16)
        expert_out = jnp.dot(hidden_low, down_w, preferred_element_type=f32).astype(bf16)
        out_low = (gate_rows * expert_out.astype(f32)).astype(bf16)
        forward.append((act_rows, used, gate_rows, gate_pre, up_pre, hidden_low, expert_out, out_low))
    rows_reduce = Reduce()
    choice_rows = jnp.zeros((NZ, plane * tokens_here, 1), f32)
    for s in range(NZ):
        act_rows, used, gate_rows, gate_pre, up_pre, hidden_low, expert_out, _ = forward[s]
        upstream_rows = lax.dynamic_index_in_dim(upstream_all, planes[s], axis=0, keepdims=False)
        if s == NZ - 1:
            upstream_rows, rows_reduce.planes[0] = tie(upstream_rows, rows_reduce.planes[0])
        upstream_f32 = upstream_rows.astype(f32)
        dots = jnp.sum(upstream_f32 * expert_out.astype(f32), axis=-1, keepdims=True) * used
        choice_rows = lax.dynamic_update_slice(choice_rows, dots[None], (planes[s], 0, 0))
        out_grad = (gate_rows * upstream_f32).astype(bf16)
        hidden_grad = times_transposed(out_grad, down_w)
        sigmoid = jax.nn.sigmoid(gate_pre)
        slope = sigmoid * (1.0 + gate_pre * (1.0 - sigmoid))
        gate_pre_grad = (hidden_grad * up_pre * slope).astype(bf16)
        up_pre_grad = (hidden_grad * (gate_pre * sigmoid)).astype(bf16)
        row_grad = (
            times_transposed(gate_pre_grad, gate_w) + times_transposed(up_pre_grad, up_w)
        ).astype(bf16)
        blocks = row_grad.reshape(plane, tokens_here, model_width)
        own, for_x, for_y, across = [
            lax.dynamic_index_in_dim(blocks, places[k], axis=0, keepdims=False)
            for k in range(plane)
        ]
        cut = split_row(tokens_here)
        backward.append((out_grad, gate_pre_grad, up_pre_grad))
        ways = rows_reduce.across(across[:cut], across[cut:])
        if s:
            rows_reduce.finish([s - 1], *opened)
        opened = (own, for_x, for_y, *ways)
    rows_reduce.finish([NZ - 1], *opened)
    choice_grad = lax.all_to_all(
        choice_rows.reshape(owners, tokens_here), "expert", split_axis=0, concat_axis=0, tiled=True
    ).T
    all_outs = jnp.zeros((NZ, plane * tokens_here, model_width), bf16)
    for s in range(NZ):
        all_outs = lax.dynamic_update_slice(all_outs, forward[s][7][None], (planes[s], 0, 0))
    expert_acts = [chunk[0] for chunk in forward]
    gate_grads = [chunk[1] for chunk in backward]
    moe_in_grad = rows_reduce.result()
    own_gate, other_gate = column_grads(
        position, expert_acts, gate_grads, waits=(rows_reduce.planes[3],)
    )
    moe_in_grad, own_gate, all_outs = tie(moe_in_grad, own_gate, all_outs)

    logit_grad = router_probs * (
        choice_grad - jnp.sum(router_probs * choice_grad, axis=-1, keepdims=True)
    )
    logit_low = logit_grad.astype(bf16)
    moe_in_grad = moe_in_grad + times_transposed(logit_low, full_router)
    router_grad = inner_product(act_moe, logit_low)
    upstream = cotangent.astype(f32)
    mid_norm_grad, moe_gain_grad = norm_backward(middle, inverse_moe, moe_gain, moe_in_grad)
    mid_grad = upstream + mid_norm_grad
    mid_low = mid_grad.astype(bf16)
    moe_term = lax.psum_scatter(
        all_outs.reshape(-1, model_width), "expert", scatter_dimension=0, tiled=True
    ).astype(f32)
    own_attended = lax.dynamic_slice_in_dim(attended_low, core * half_width, half_width, axis=1).T
    other_attended = move_core(
        lax.dynamic_slice_in_dim(attended_low, (1 - core) * half_width, half_width, axis=1)
    ).T
    attended_grad = (
        apply_weight(position, mid_low, pieces_vo, rows, 1, back=True)
        .astype(bf16)
        .reshape(head_shape)
    )
    probs_grad = jnp.einsum("qhd,khd->hqk", attended_grad, value_heads, preferred_element_type=f32)
    row_inner = jnp.sum(probs * probs_grad, axis=-1, keepdims=True)
    scores_grad = (probs * (probs_grad - row_inner)).astype(bf16)
    query_rot_grad = (
        jnp.einsum("hqk,khd->qhd", scores_grad, key_rot, preferred_element_type=f32) * score_scale
    )
    key_rot_grad = (
        jnp.einsum("hqk,qhd->khd", scores_grad, query_rot, preferred_element_type=f32) * score_scale
    )
    value_grad = jnp.einsum("hqk,qhd->khd", probs_low, attended_grad, preferred_element_type=f32)
    value_grad = value_grad.reshape(tokens_here, model_width).astype(bf16)
    query_back = rotate_back(query_rot_grad, cosine, sine_table).reshape(tokens_here, model_width)
    key_back = rotate_back(key_rot_grad, cosine, sine_table).reshape(tokens_here, model_width)
    query_pre_grad, query_gain_grad = norm_backward(
        query_pre, query_inverse, query_gain, query_back
    )
    key_pre_grad, key_gain_grad = norm_backward(key_pre, key_inverse, key_gain, key_back)
    query_low = query_pre_grad.astype(bf16)
    key_low = key_pre_grad.astype(bf16)
    attn_grads = []
    for low in (query_low, key_low, value_grad):
        attn_grads += [low, move_core(low)]
    weights_reduce = Reduce()
    turned = [own_act, other_act, own_attended, other_attended]
    attn_grads += [mid_low, move_core(mid_low)]
    lefts = (0, 0, 0, 1)
    first = weight_grad_parts(position, turned, attn_grads, lefts, rows, (1, 2))
    first_ways = weights_reduce.across(*first[3:])
    last = weight_grad_parts(position, turned, attn_grads, lefts, rows, (3, 0))
    last_ways = weights_reduce.across(*last[3:])
    weights_reduce.finish([1, 2], *first[:3], *first_ways)
    act_grad = (
        apply_weight(position, query_low, pieces_qk, rows, 0, back=True, waits=first_ways)
        + apply_weight(position, key_low, pieces_qk, rows, 1, back=True, waits=first_ways)
        + apply_weight(position, value_grad, pieces_vo, rows, 0, back=True, waits=first_ways)
    )
    up_grads = [chunk[2] for chunk in backward]
    own_up, other_up = column_grads(position, expert_acts, up_grads, waits=(act_grad,))
    weights_reduce.push()
    weights_reduce.finish([3, 0], *last[:3], *last_ways)
    own_down, other_down = down_grads(
        position,
        [chunk[5] for chunk in forward],
        [chunk[0] for chunk in backward],
        waits=(weights_reduce.planes[1], own_up),
    )
    weight_sums, moe_term = tie(weights_reduce.result(), moe_term)
    query_weight_grad, key_weight_grad, value_weight_grad, output_grad = jnp.split(
        weight_sums, 4, axis=0
    )
    input_norm_grad, attn_gain_grad = norm_backward(inputs_f32, inverse_attn, attn_gain, act_grad)
    input_grad = (mid_grad + input_norm_grad).astype(bf16)

    devices = 2 * owners
    small_grads = jnp.concatenate(
        [
            part.reshape(devices, -1)
            for part in (attn_gain_grad, query_gain_grad, key_gain_grad, moe_gain_grad, router_grad)
        ],
        axis=1,
    )
    small_grads = jnp.sum(
        lax.all_to_all(
            small_grads, ("dp", "expert"), split_axis=0, concat_axis=0, tiled=True
        ),
        axis=0,
    )
    attn_gain_grad, query_gain_grad, key_gain_grad, moe_gain_grad, router_grad = jnp.split(
        small_grads, [rows, 2 * rows, 3 * rows, 4 * rows]
    )

    block_out = (middle + moe_term).astype(bf16)
    down_grad = own_down + move_core(other_down).astype(f32)
    gate_weight_grad = own_gate + move_core(other_gate).astype(f32)
    up_weight_grad = own_up + move_core(other_up).astype(f32)
    return (
        block_out,
        input_grad,
        attn_gain_grad,
        query_weight_grad,
        key_weight_grad,
        value_weight_grad,
        query_gain_grad,
        key_gain_grad,
        output_grad,
        moe_gain_grad,
        router_grad.reshape(w_router.shape),
        gate_weight_grad[None],
        up_weight_grad[None],
        down_grad[None],
    )


def solution(mesh):
    body = body_dense if mesh.shape["expert"] == NZ * NY * NX else body_routed
    return jax.shard_map(
        body,
        mesh=mesh,
        in_specs=(
            P(("dp", "expert"), None),
            P(("dp", "expert"), None),
            P(("dp", "expert"), None),
            P(("dp", "expert"), None),
            P(),
            P(("dp", "expert"), None),
            P(("dp", "expert"), None),
            P(("dp", "expert"), None),
            P(),
            P(),
            P(("dp", "expert"), None),
            P(),
            P(("dp", "expert"), None),
            P("expert", None, None),
            P("expert", None, None),
            P("expert", None, None),
        ),
        out_specs=(
            P(("dp", "expert"), None),
            P(("dp", "expert"), None),
            P(("dp", "expert")),
            P(("dp", "expert"), None),
            P(("dp", "expert"), None),
            P(("dp", "expert"), None),
            P(("dp", "expert")),
            P(("dp", "expert")),
            P(("dp", "expert"), None),
            P(("dp", "expert")),
            P(("dp", "expert"), None),
            P("expert", None, "dp"),
            P("expert", None, "dp"),
            P("expert", "dp", None),
        ),
        check_vma=False,
    )
```

```python
import functools
import itertools

import jax
import jax.numpy as jnp
from jax import lax
from jax.experimental import pallas as pl
from jax.experimental.pallas import tpu as pltpu
from jax.sharding import PartitionSpec as P

HD = 128


EPSILON = 1e-05


def norm_forward(values, gain_vector):
    inverse = lax.rsqrt(jnp.mean(values * values, axis=-1, keepdims=True) + EPSILON)
    return (values * inverse * gain_vector, inverse)


def norm_backward(values, inverse, gain_vector, upstream):
    gain_grad = jnp.sum(upstream * values * inverse, axis=0)
    scaled = upstream * gain_vector
    inner_mean = jnp.mean(scaled * values, axis=-1, keepdims=True)
    return (inverse * (scaled - values * inner_mean * inverse * inverse), gain_grad)


def rotary_tables(length, head_dim):
    half_dim = head_dim // 2
    frequency = 10000.0 ** (-jnp.arange(half_dim, dtype=jnp.float32) * 2.0 / head_dim)
    angles = jnp.arange(length, dtype=jnp.float32)[:, None] * frequency[None, :]
    angles = jnp.concatenate([angles, angles], axis=1)
    return (jnp.cos(angles)[:, None, :], jnp.sin(angles)[:, None, :])


def rotate(values, cosine, sine_table):
    half_dim = values.shape[-1] // 2
    turned = jnp.concatenate([-values[..., half_dim:], values[..., :half_dim]], axis=-1)
    return values * cosine + turned * sine_table


def rotate_back(upstream, cosine, sine_table):
    half_dim = upstream.shape[-1] // 2
    with_sine = upstream * sine_table
    turned = jnp.concatenate([with_sine[..., half_dim:], -with_sine[..., :half_dim]], axis=-1)
    return upstream * cosine + turned


def times_transposed(left, right):
    return jnp.einsum("ta,ba->tb", left, right, preferred_element_type=jnp.float32)


def inner_product(left, right):
    return jnp.einsum("ta,tb->ab", left, right, preferred_element_type=jnp.float32)


def body_routed(
    hidden_in,
    cotangent,
    doc_ids,
    routes,
    attn_gain,
    w_query,
    w_key,
    w_value,
    query_gain,
    key_gain,
    w_output,
    moe_gain,
    w_router,
    w_gate,
    w_up,
    w_down,
):
    f32 = jnp.float32
    bf16 = jnp.bfloat16
    tokens_here = hidden_in.shape[0]
    model_width = hidden_in.shape[1]
    head_dim = HD
    head_count = model_width // head_dim
    top_count = routes.shape[1]
    experts_all = w_router.shape[1]
    capacity = tokens_here * top_count * 4 // (3 * experts_all)
    local_experts = w_gate.shape[0]
    owners = lax.axis_size("expert")
    full_query, full_key, full_value, full_output, full_router = (
        lax.all_gather(w_query, ("dp", "expert"), axis=0, tiled=True),
        lax.all_gather(w_key, ("dp", "expert"), axis=0, tiled=True),
        lax.all_gather(w_value, ("dp", "expert"), axis=0, tiled=True),
        lax.all_gather(w_output, ("dp", "expert"), axis=0, tiled=True),
        lax.all_gather(w_router, ("dp", "expert"), axis=0, tiled=True),
    )
    inputs_f32 = hidden_in.astype(f32)
    normed_attn, inverse_attn = norm_forward(inputs_f32, attn_gain)
    act_attn = normed_attn.astype(bf16)
    query_pre = jnp.dot(act_attn, full_query, preferred_element_type=f32)
    key_pre = jnp.dot(act_attn, full_key, preferred_element_type=f32)
    value_low = jnp.dot(act_attn, full_value, preferred_element_type=f32).astype(bf16)
    query_normed, query_inverse = norm_forward(query_pre, query_gain)
    key_normed, key_inverse = norm_forward(key_pre, key_gain)
    cosine, sine_table = rotary_tables(tokens_here, head_dim)
    head_shape = (tokens_here, head_count, head_dim)
    query_rot = rotate(query_normed.reshape(head_shape), cosine, sine_table).astype(bf16)
    key_rot = rotate(key_normed.reshape(head_shape), cosine, sine_table).astype(bf16)
    value_heads = value_low.reshape(head_shape)
    score_scale = head_dim ** (-0.5)
    position = jnp.arange(tokens_here, dtype=jnp.int32)
    allowed = (position[:, None] >= position[None, :]) & (
        doc_ids[0][:, None] == doc_ids[0][None, :]
    )

    def masked_scores():
        scores = (
            jnp.einsum("qhd,khd->hqk", query_rot, key_rot, preferred_element_type=f32) * score_scale
        )
        return jnp.where(allowed[None], scores, -1e30)

    scores = masked_scores()
    row_max = jnp.max(scores, axis=-1, keepdims=True)
    row_sum = jnp.sum(jnp.exp(scores - row_max), axis=-1, keepdims=True)
    log_total = row_max + jnp.log(row_sum)
    probs_low = jnp.exp(scores - log_total).astype(bf16)
    attended = jnp.einsum("hqk,khd->qhd", probs_low, value_heads, preferred_element_type=f32)
    attended_low = attended.reshape(tokens_here, model_width).astype(bf16)
    middle = inputs_f32 + jnp.dot(attended_low, full_output, preferred_element_type=f32)
    normed_moe, inverse_moe = norm_forward(middle, moe_gain)
    act_moe = normed_moe.astype(bf16)
    logits = jnp.dot(act_moe, full_router, preferred_element_type=f32)
    router_probs = jax.nn.softmax(logits, axis=-1)
    expert_ids = jnp.arange(experts_all, dtype=jnp.int32)
    chosen = routes[:, :, None] == expert_ids[None, None, :]
    gate_values = jnp.sum(jnp.where(chosen, router_probs[:, None, :], 0.0), axis=-1)
    flat_routes = routes.reshape(-1)
    onehot = (flat_routes[:, None] == expert_ids[None, :]).astype(jnp.int32)
    slot_of = jnp.sum((jnp.cumsum(onehot, axis=0) - 1) * onehot, axis=1)
    target_slot = flat_routes * capacity + slot_of
    pair_token = jnp.arange(tokens_here * top_count, dtype=jnp.int32) // top_count

    def to_experts(pair_rows):
        buffer = (
            jnp.zeros((experts_all * capacity, model_width), bf16).at[target_slot].set(pair_rows)
        )
        return buffer.reshape(experts_all, capacity, model_width)

    def from_experts(buffer):
        return buffer.reshape(experts_all * capacity, model_width)[target_slot]

    received = lax.all_to_all(
        to_experts(act_moe[pair_token]), "expert", split_axis=0, concat_axis=0, tiled=True
    )
    owner_rows = received.reshape(owners, local_experts, capacity, model_width)
    gate_pre = jnp.einsum("secd,edf->secf", owner_rows, w_gate, preferred_element_type=f32)
    up_pre = jnp.einsum("secd,edf->secf", owner_rows, w_up, preferred_element_type=f32)
    sigmoid = jax.nn.sigmoid(gate_pre)
    swish = gate_pre * sigmoid
    hidden_low = (swish * up_pre).astype(bf16)
    expert_out = jnp.einsum(
        "secf,efd->secd", hidden_low, w_down, preferred_element_type=f32
    ).astype(bf16)
    returned = lax.all_to_all(
        expert_out.reshape(owners * local_experts, capacity, model_width),
        "expert",
        split_axis=0,
        concat_axis=0,
        tiled=True,
    )
    pair_out = from_experts(returned).reshape(tokens_here, top_count, model_width).astype(f32)
    moe_term = jnp.sum(gate_values[:, :, None] * pair_out, axis=1)
    block_out = (middle + moe_term).astype(bf16)
    upstream = cotangent.astype(f32)
    pair_grad = (gate_values[:, :, None] * upstream[:, None, :]).astype(bf16)
    gate_grad = jnp.sum(upstream[:, None, :] * pair_out, axis=-1)
    out_grad = lax.all_to_all(
        to_experts(pair_grad.reshape(-1, model_width)),
        "expert",
        split_axis=0,
        concat_axis=0,
        tiled=True,
    )
    out_grad = out_grad.reshape(owners, local_experts, capacity, model_width)
    hidden_grad = jnp.einsum("secd,efd->secf", out_grad, w_down, preferred_element_type=f32)
    down_grad = jnp.einsum("secf,secd->efd", hidden_low, out_grad, preferred_element_type=f32)
    slope = sigmoid * (1.0 + gate_pre * (1.0 - sigmoid))
    gate_pre_grad = (hidden_grad * up_pre * slope).astype(bf16)
    up_pre_grad = (hidden_grad * swish).astype(bf16)
    row_grad = jnp.einsum("secf,edf->secd", gate_pre_grad, w_gate, preferred_element_type=f32)
    row_grad = (
        row_grad + jnp.einsum("secf,edf->secd", up_pre_grad, w_up, preferred_element_type=f32)
    ).astype(bf16)
    gate_weight_grad = jnp.einsum(
        "secd,secf->edf", owner_rows, gate_pre_grad, preferred_element_type=f32
    )
    up_weight_grad = jnp.einsum(
        "secd,secf->edf", owner_rows, up_pre_grad, preferred_element_type=f32
    )
    gate_weight_grad, up_weight_grad, down_grad = (
        lax.psum_scatter(
            gate_weight_grad.astype(jnp.bfloat16), "dp", scatter_dimension=2, tiled=True
        ).astype(jnp.float32),
        lax.psum_scatter(
            up_weight_grad.astype(jnp.bfloat16), "dp", scatter_dimension=2, tiled=True
        ).astype(jnp.float32),
        lax.psum_scatter(
            down_grad.astype(jnp.bfloat16), "dp", scatter_dimension=1, tiled=True
        ).astype(jnp.float32),
    )
    back_rows = lax.all_to_all(
        row_grad.reshape(owners * local_experts, capacity, model_width),
        "expert",
        split_axis=0,
        concat_axis=0,
        tiled=True,
    )
    moe_in_grad = jnp.sum(
        from_experts(back_rows).reshape(tokens_here, top_count, model_width).astype(f32), axis=1
    )
    choice_grad = jnp.sum(jnp.where(chosen, gate_grad[:, :, None], 0.0), axis=1)
    logit_grad = router_probs * (
        choice_grad - jnp.sum(router_probs * choice_grad, axis=-1, keepdims=True)
    )
    logit_low = logit_grad.astype(bf16)
    moe_in_grad = moe_in_grad + times_transposed(logit_low, full_router)
    router_grad = inner_product(act_moe, logit_low)
    mid_norm_grad, moe_gain_grad = norm_backward(middle, inverse_moe, moe_gain, moe_in_grad)
    mid_grad = upstream + mid_norm_grad
    mid_low = mid_grad.astype(bf16)
    output_grad = inner_product(attended_low, mid_low)
    attended_grad = times_transposed(mid_low, full_output).astype(bf16).reshape(head_shape)
    probs = jnp.exp(masked_scores() - log_total)
    probs_grad = jnp.einsum("qhd,khd->hqk", attended_grad, value_heads, preferred_element_type=f32)
    row_inner = jnp.sum(probs * probs_grad, axis=-1, keepdims=True)
    scores_grad = (probs * (probs_grad - row_inner)).astype(bf16)
    query_rot_grad = (
        jnp.einsum("hqk,khd->qhd", scores_grad, key_rot, preferred_element_type=f32) * score_scale
    )
    key_rot_grad = (
        jnp.einsum("hqk,qhd->khd", scores_grad, query_rot, preferred_element_type=f32) * score_scale
    )
    value_grad = jnp.einsum("hqk,qhd->khd", probs_low, attended_grad, preferred_element_type=f32)
    value_grad = value_grad.reshape(tokens_here, model_width).astype(bf16)
    query_back = rotate_back(query_rot_grad, cosine, sine_table).reshape(tokens_here, model_width)
    key_back = rotate_back(key_rot_grad, cosine, sine_table).reshape(tokens_here, model_width)
    query_pre_grad, query_gain_grad = norm_backward(
        query_pre, query_inverse, query_gain, query_back
    )
    key_pre_grad, key_gain_grad = norm_backward(key_pre, key_inverse, key_gain, key_back)
    query_low = query_pre_grad.astype(bf16)
    key_low = key_pre_grad.astype(bf16)
    act_grad = (
        times_transposed(query_low, full_query)
        + times_transposed(key_low, full_key)
        + times_transposed(value_grad, full_value)
    )
    query_weight_grad = inner_product(act_attn, query_low)
    key_weight_grad = inner_product(act_attn, key_low)
    value_weight_grad = inner_product(act_attn, value_grad)
    input_norm_grad, attn_gain_grad = norm_backward(inputs_f32, inverse_attn, attn_gain, act_grad)
    input_grad = (mid_grad + input_norm_grad).astype(bf16)
    sharded_grads = (
        lax.psum_scatter(attn_gain_grad, ("dp", "expert"), scatter_dimension=0, tiled=True),
        lax.psum_scatter(query_weight_grad, ("dp", "expert"), scatter_dimension=0, tiled=True),
        lax.psum_scatter(key_weight_grad, ("dp", "expert"), scatter_dimension=0, tiled=True),
        lax.psum_scatter(value_weight_grad, ("dp", "expert"), scatter_dimension=0, tiled=True),
        lax.psum_scatter(query_gain_grad, ("dp", "expert"), scatter_dimension=0, tiled=True),
        lax.psum_scatter(key_gain_grad, ("dp", "expert"), scatter_dimension=0, tiled=True),
        lax.psum_scatter(output_grad, ("dp", "expert"), scatter_dimension=0, tiled=True),
        lax.psum_scatter(moe_gain_grad, ("dp", "expert"), scatter_dimension=0, tiled=True),
        lax.psum_scatter(router_grad, ("dp", "expert"), scatter_dimension=0, tiled=True),
    )
    return (
        block_out,
        input_grad,
        sharded_grads[0],
        sharded_grads[1],
        sharded_grads[2],
        sharded_grads[3],
        sharded_grads[4],
        sharded_grads[5],
        sharded_grads[6],
        sharded_grads[7],
        sharded_grads[8],
        gate_weight_grad,
        up_weight_grad,
        down_grad,
    )


NZ, NY, NX = 4, 2, 2
VMEM_LIMIT = 48 * 1024 * 1024
EXPERT_VMEM = 60 * 1024 * 1024


def chip(z, y, x):
    return (z * NY + y) * NX + x


GRID = [(z, y, x) for z in range(NZ) for y in range(NY) for x in range(NX)]
X_PAIRS = [(chip(z, y, x), chip(z, y, 1 - x)) for z, y, x in GRID]
Y_PAIRS = [(chip(z, y, x), chip(z, 1 - y, x)) for z, y, x in GRID]
Z_PAIRS = [(chip(z, y, x), chip((z + 1) % NZ, y, x)) for z, y, x in GRID]
CORE_PAIRS = [(0, 1), (1, 0)]


def move_x(values):
    return lax.ppermute(values, "expert", X_PAIRS)


def move_y(values):
    return lax.ppermute(values, "expert", Y_PAIRS)


def move_z(values):
    return lax.ppermute(values, "expert", Z_PAIRS)


def move_core(values):
    return lax.ppermute(values, "dp", CORE_PAIRS)


def split_row(rows):
    return (rows // 2 + 15) // 16 * 16


def tie(*values):
    return lax.optimization_barrier(values)


def without(kernel, start, count):
    return lambda *refs: kernel(*refs[:start], *refs[start + count :])


def gather_z(block):
    ring = [block]
    for _ in range(1, NZ):
        ring.append(move_z(ring[-1]))
    return ring


def gather_plane(block):
    cut = split_row(block.shape[0])
    from_x = move_x(block)
    from_y = move_y(block)
    across = jnp.concatenate([move_x(from_y[:cut]), move_y(from_x[cut:])], axis=0)
    return [block, from_x, from_y, across]


def gather_chips(block):
    return [gather_plane(part) for part in gather_z(block)]


def add_f32(left, right):
    return left.astype(jnp.float32) + right.astype(jnp.float32)


class Reduce:
    def __init__(self):
        self.planes, self.steps, self.total = {}, 0, None

    def across(self, low, high):
        return move_x(low), move_y(high)

    def finish(self, steps, own, for_x, for_y, by_x, by_y, chained=False):
        low = own.dtype
        cut = by_x.shape[0]
        for_y = jnp.concatenate([add_f32(for_y[:cut], by_x).astype(low), for_y[cut:]], axis=0)
        for_x = jnp.concatenate([for_x[:cut], add_f32(for_x[cut:], by_y).astype(low)], axis=0)
        from_x, from_y = move_x(for_x), move_y(for_y)
        if chained:
            from_x, from_y, self.total = tie(from_x, from_y, self.total)
        total = add_f32(own, from_x) + from_y.astype(jnp.float32)
        for step, part in zip(steps, jnp.split(total, len(steps), axis=0), strict=True):
            self.planes[step] = part

    def push(self):
        while self.steps + 1 < NZ and self.steps + 1 in self.planes:
            self.steps += 1
            total = self.planes[self.steps]
            if self.total is not None:
                total = add_f32(self.total, total)
            self.total = move_z(total.astype(jnp.bfloat16))

    def result(self):
        self.push()
        return add_f32(self.total, self.planes[0])


def place_of(position, k):
    return (position[2] ^ (k >> 1)) * NX + (position[3] ^ (k & 1))


def weight_copies(position, pieces, rows, slot, held, sems, other):
    out = []
    for step in range(NZ):
        z_of = (position[1] + NZ - step) % NZ
        for k in range(NY * NX):
            place = pl.multiple_of((z_of * NY * NX + place_of(position, k)) * rows, rows)
            out.append(
                pltpu.make_async_copy(
                    pieces[other * NZ + step].at[k, pl.ds(slot * rows, rows)],
                    held.at[other, pl.ds(place, rows)],
                    sems.at[other * NZ + step, k],
                )
            )
    return out


def apply_kernel(position, acts, *refs, rows, slot, tile):
    pieces, (out, held, sems) = refs[: 2 * NZ], refs[2 * NZ :]
    for other in range(2):
        for copy in weight_copies(position, pieces, rows, slot, held, sems, other):
            copy.start()
    span = held.shape[1]
    for other in range(2):
        for copy in weight_copies(position, pieces, rows, slot, held, sems, other):
            copy.wait()
        left = acts[:, pl.ds(pl.multiple_of((position[0] ^ other) * span, span), span)]

        @pl.loop(0, out.shape[1] // tile)
        def _(i):
            columns = pl.ds(pl.multiple_of(i * tile, tile), tile)
            part = jnp.dot(left, held[other, :, columns], preferred_element_type=jnp.float32)
            if other == 0:
                out[:, columns] = part
            else:
                out[:, columns] += part


def apply_back_kernel(position, grads, *refs, rows, slot, tile):
    pieces, (out, held, sems) = refs[: 2 * NZ], refs[2 * NZ :]
    for other in range(2):
        for copy in weight_copies(position, pieces, rows, slot, held, sems, other):
            copy.start()
    span = held.shape[1]
    for other in range(2):
        for copy in weight_copies(position, pieces, rows, slot, held, sems, other):
            copy.wait()

        @pl.loop(0, span // tile)
        def _(i):
            lines = pl.ds(pl.multiple_of(i * tile, tile), tile)
            low = pl.multiple_of((position[0] ^ other) * span + i * tile, tile)
            out[:, pl.ds(low, tile)] = lax.dot_general(
                grads[...],
                held[other, lines, :],
                (((1,), (1,)), ((), ())),
                preferred_element_type=jnp.float32,
            )


def apply_weight(position, values, pieces, rows, slot, back=False, waits=()):
    tokens, width = values.shape
    return pl.pallas_call(
        without(
            functools.partial(
                apply_back_kernel if back else apply_kernel, rows=rows, slot=slot, tile=512
            ),
            2 + len(pieces),
            len(waits),
        ),
        out_shape=jax.ShapeDtypeStruct((tokens, width), jnp.float32),
        in_specs=[pl.BlockSpec(memory_space=pltpu.SMEM), pl.BlockSpec(memory_space=pltpu.VMEM)]
        + [pl.BlockSpec(memory_space=pl.ANY)] * (len(pieces) + len(waits)),
        out_specs=pl.BlockSpec(memory_space=pltpu.VMEM),
        scratch_shapes=[
            pltpu.VMEM((2, width // 2, width), jnp.bfloat16),
            pltpu.SemaphoreType.DMA((2 * NZ, NY * NX)),
        ],
        compiler_params=pltpu.CompilerParams(vmem_limit_bytes=VMEM_LIMIT),
        cost_estimate=pl.CostEstimate(
            flops=2 * tokens * width * width,
            bytes_accessed=2 * width * width + 6 * tokens * width,
            transcendentals=0,
        ),
    )(position, values, *pieces, *waits)


def weight_grad_kernel(position, *refs, rows, lefts, steps, tile):
    count = len(lefts)
    turned, grads = refs[: 2 * max(lefts) + 2], refs[2 * max(lefts) + 2 :]
    grads, (own, for_x, for_y, *across, stage) = grads[: 2 * count], grads[2 * count :]
    span = NY * NX * rows
    for p, step in enumerate(steps):
        z_of = (position[1] + NZ - step) % NZ
        lines = pl.ds(pl.multiple_of(z_of * span, span), span)
        for i, left in enumerate(lefts):
            low = p * count * rows + i * rows
            targets = [(own, low), (for_x, low), (for_y, low), (across[p], i * rows)]

            @pl.loop(0, grads[0].shape[1] // tile)
            def _(j):
                part = pl.ds(pl.multiple_of(j * tile, tile), tile)
                product = jnp.dot(
                    turned[2 * left][lines, :],
                    grads[2 * i][:, part],
                    preferred_element_type=jnp.float32,
                ) + jnp.dot(
                    turned[2 * left + 1][lines, :],
                    grads[2 * i + 1][:, part],
                    preferred_element_type=jnp.float32,
                )
                stage[...] = product.astype(stage.dtype)
                for k, (target, at) in enumerate(targets):
                    place = pl.multiple_of(place_of(position, k) * rows, rows)
                    target[pl.ds(at, rows), part] = stage[pl.ds(place, rows), :]


def weight_grad_parts(position, turned, grads, lefts, rows, steps, waits=()):
    count, width = len(lefts), grads[0].shape[1]
    tokens, tile = turned[0].shape[1], 512
    vmem_spec = pl.BlockSpec(memory_space=pltpu.VMEM)
    both = jax.ShapeDtypeStruct((2 * count * rows, width), jnp.bfloat16)
    one = jax.ShapeDtypeStruct((count * rows, width), jnp.bfloat16)
    operands = [*turned, *grads]
    return pl.pallas_call(
        without(
            functools.partial(weight_grad_kernel, rows=rows, lefts=lefts, steps=steps, tile=tile),
            1 + len(operands),
            len(waits),
        ),
        out_shape=[both] * 3 + [one] * 2,
        in_specs=[pl.BlockSpec(memory_space=pltpu.SMEM)]
        + [vmem_spec] * len(operands)
        + [pl.BlockSpec(memory_space=pl.ANY)] * len(waits),
        out_specs=[vmem_spec] * 5,
        scratch_shapes=[pltpu.VMEM((NY * NX * rows, tile), jnp.bfloat16)],
        compiler_params=pltpu.CompilerParams(vmem_limit_bytes=VMEM_LIMIT),
        cost_estimate=pl.CostEstimate(
            flops=8 * count * tokens * NY * NX * rows * width,
            bytes_accessed=4 * count * NY * NX * rows * width + 4 * tokens * width * (count + 1),
            transcendentals=0,
        ),
    )(position, *operands, *waits)


def column_grad_kernel(position, *refs):
    parts = (len(refs) - 2) // 2
    acts, grads, outs = refs[:parts], refs[parts:-2], refs[-2:]
    half = outs[0].shape[1]
    turned = [act[...].T for act in acts]
    for side, out in enumerate(outs):
        columns = pl.ds(pl.multiple_of((position[0] ^ side) * half, half), half)
        total = None
        for act, grad in zip(turned, grads, strict=True):
            more = jnp.dot(act, grad[:, columns], preferred_element_type=jnp.float32)
            total = more if total is None else total + more
        out[...] = total.astype(out.dtype)


def column_grads(position, acts, grads, waits=()):
    parts = len(acts)
    count, width = acts[0].shape
    units = grads[0].shape[1]
    tile = 256
    whole = pl.BlockSpec((count, units), lambda i: (0, 0), pipeline_mode=pl.Buffered(1))
    out = pl.BlockSpec((tile, units // 2), lambda i: (i, 0))
    return pl.pallas_call(
        without(column_grad_kernel, 1 + 2 * parts, len(waits)),
        grid=(width // tile,),
        out_shape=[jax.ShapeDtypeStruct((width, units // 2), t) for t in (jnp.float32, jnp.bfloat16)],
        in_specs=[pl.BlockSpec(memory_space=pltpu.SMEM)]
        + [pl.BlockSpec((count, tile), lambda i: (0, i))] * parts
        + [whole] * parts
        + [pl.BlockSpec(memory_space=pl.ANY)] * len(waits),
        out_specs=[out] * 2,
        compiler_params=pltpu.CompilerParams(vmem_limit_bytes=EXPERT_VMEM),
        cost_estimate=pl.CostEstimate(
            flops=2 * parts * count * width * units,
            bytes_accessed=2 * parts * count * (width + units) + 3 * width * units,
            transcendentals=0,
        ),
    )(position, *acts, *grads, *waits)


def down_grad_kernel(position, *refs):
    parts = (len(refs) - 3) // 2
    hiddens, grads, (own, other, turned) = refs[:parts], refs[parts:-3], refs[-3:]
    tile = 512
    for s, hidden in enumerate(hiddens):
        turned[s] = hidden[...].T

    def part_of(j):
        columns = pl.ds(pl.multiple_of(j * tile, tile), tile)
        total = None
        for s, grad in enumerate(grads):
            more = jnp.dot(turned[s], grad[:, columns], preferred_element_type=jnp.float32)
            total = more if total is None else total + more
        return columns, total

    steps = grads[0].shape[1] // tile

    @pl.when(pl.program_id(0) < pl.num_programs(0) // 2)
    def _():
        @pl.loop(0, steps)
        def _(j):
            columns, total = part_of(j)
            own[:, columns] = total

    @pl.when(pl.program_id(0) >= pl.num_programs(0) // 2)
    def _():
        @pl.loop(0, steps)
        def _(j):
            columns, total = part_of(j)
            other[:, columns] = total.astype(other.dtype)


def down_grads(position, hiddens, grads, waits=()):
    parts = len(hiddens)
    count, units = hiddens[0].shape
    width = grads[0].shape[1]
    tile = 256
    half = units // 2 // tile
    whole = pl.BlockSpec((count, width), lambda i, at: (0, 0), pipeline_mode=pl.Buffered(1))
    return pl.pallas_call(
        without(down_grad_kernel, 1 + 2 * parts, len(waits)),
        grid_spec=pltpu.PrefetchScalarGridSpec(
            num_scalar_prefetch=1,
            grid=(2 * half,),
            in_specs=[
                pl.BlockSpec((count, tile), lambda i, at: (0, (i + at[0] * half) % (2 * half)))
            ]
            * parts
            + [whole] * parts
            + [pl.BlockSpec(memory_space=pl.ANY)] * len(waits),
            out_specs=[
                pl.BlockSpec((tile, width), lambda i, at: (jnp.minimum(i, half - 1), 0)),
                pl.BlockSpec((tile, width), lambda i, at: (jnp.maximum(i - half, 0), 0)),
            ],
            scratch_shapes=[pltpu.VMEM((parts, tile, count), jnp.bfloat16)],
        ),
        out_shape=[
            jax.ShapeDtypeStruct((units // 2, width), jnp.float32),
            jax.ShapeDtypeStruct((units // 2, width), jnp.bfloat16),
        ],
        compiler_params=pltpu.CompilerParams(vmem_limit_bytes=EXPERT_VMEM),
        cost_estimate=pl.CostEstimate(
            flops=2 * parts * count * width * units,
            bytes_accessed=2 * parts * count * (width + units) + 3 * width * units,
            transcendentals=0,
        ),
    )(position, *hiddens, *grads, *waits)


def gather_weights(blocks):
    ring = [jnp.stack(part) for part in gather_chips(jnp.concatenate(blocks, axis=0))]
    return ring + [move_core(part) for part in ring]


def body_dense(
    hidden_in,
    cotangent,
    doc_ids,
    routes,
    attn_gain,
    w_query,
    w_key,
    w_value,
    query_gain,
    key_gain,
    w_output,
    moe_gain,
    w_router,
    w_gate,
    w_up,
    w_down,
):
    f32 = jnp.float32
    bf16 = jnp.bfloat16
    tokens_here, model_width = hidden_in.shape
    head_dim = HD
    head_count = model_width // head_dim
    rows = w_query.shape[0]
    experts_all = w_router.shape[1]
    owners = lax.axis_size("expert")
    core = lax.axis_index("dp")
    here = lax.axis_index("expert")
    z_at, y_at, x_at = here // (NY * NX), here // NX % NY, here % NX
    position = jnp.stack([core, z_at, y_at, x_at, here]).astype(jnp.int32)
    half_width = model_width // 2
    plane = NY * NX
    places = [(y_at ^ (k >> 1)) * NX + (x_at ^ (k & 1)) for k in range(plane)]
    planes = [(z_at + NZ - s) % NZ for s in range(NZ)]

    pieces_qk = gather_weights([w_query, w_key])
    pieces_vo = gather_weights([w_value, w_output])
    upstream, pieces_vo[0] = tie(cotangent, pieces_vo[0])
    upstream_all = lax.all_gather(
        upstream, "expert", axis=0, tiled=True
    ).reshape(NZ, plane * tokens_here, model_width)

    expert_ids = jnp.arange(experts_all, dtype=jnp.int32)
    chosen = routes[:, :, None] == expert_ids[None, None, :]
    uses = jnp.any(chosen, axis=1).astype(f32)
    router_block = jnp.broadcast_to(w_router.astype(f32).reshape(1, -1), (owners, w_router.size))
    small = jnp.concatenate([uses.T, router_block], axis=1)
    small = lax.all_to_all(
        small, "expert", split_axis=0, concat_axis=0, tiled=True
    )
    used_here = small[:, :tokens_here].reshape(NZ, plane * tokens_here, 1)
    own_router = small[:, tokens_here:].reshape(-1, experts_all)
    other_router = move_core(own_router)
    full_router = jnp.where(
        core == 0,
        jnp.concatenate([own_router, other_router], axis=0),
        jnp.concatenate([other_router, own_router], axis=0),
    ).astype(bf16)

    inputs_f32 = hidden_in.astype(f32)
    normed_attn, inverse_attn = norm_forward(inputs_f32, attn_gain)
    act_attn = normed_attn.astype(bf16)
    own_act = lax.dynamic_slice_in_dim(act_attn, core * half_width, half_width, axis=1).T
    other_act = move_core(
        lax.dynamic_slice_in_dim(act_attn, (1 - core) * half_width, half_width, axis=1)
    ).T
    query_pre = apply_weight(position, act_attn, pieces_qk, rows, 0)
    key_pre = apply_weight(position, act_attn, pieces_qk, rows, 1)
    value_low = apply_weight(
        position, act_attn, pieces_vo, rows, 0, waits=(small,)
    ).astype(bf16)
    query_normed, query_inverse = norm_forward(query_pre, query_gain)
    key_normed, key_inverse = norm_forward(key_pre, key_gain)
    cosine, sine_table = rotary_tables(tokens_here, head_dim)
    head_shape = (tokens_here, head_count, head_dim)
    query_rot = rotate(query_normed.reshape(head_shape), cosine, sine_table).astype(bf16)
    key_rot = rotate(key_normed.reshape(head_shape), cosine, sine_table).astype(bf16)
    value_heads = value_low.reshape(head_shape)
    score_scale = head_dim ** (-0.5)
    token_at = jnp.arange(tokens_here, dtype=jnp.int32)
    allowed = (token_at[:, None] >= token_at[None, :]) & (
        doc_ids[0][:, None] == doc_ids[0][None, :]
    )
    scores = (
        jnp.einsum("qhd,khd->hqk", query_rot, key_rot, preferred_element_type=f32) * score_scale
    )
    scores = jnp.where(allowed[None], scores, -1e30)
    row_max = jnp.max(scores, axis=-1, keepdims=True)
    row_sum = jnp.sum(jnp.exp(scores - row_max), axis=-1, keepdims=True)
    log_total = row_max + jnp.log(row_sum)
    probs = jnp.exp(scores - log_total)
    probs_low = probs.astype(bf16)
    attended = jnp.einsum("hqk,khd->qhd", probs_low, value_heads, preferred_element_type=f32)
    attended_low = attended.reshape(tokens_here, model_width).astype(bf16)
    middle = inputs_f32 + apply_weight(position, attended_low, pieces_vo, rows, 1)
    normed_moe, inverse_moe = norm_forward(middle, moe_gain)
    act_moe = normed_moe.astype(bf16)

    logits = jnp.dot(act_moe, full_router, preferred_element_type=f32)
    router_probs = jax.nn.softmax(logits, axis=-1)

    gate_w, up_w, down_w = w_gate[0], w_up[0], w_down[0]
    mine = (expert_ids == here).astype(f32)
    forward, backward = [], []
    for s, pieces in enumerate(gather_chips(act_moe)):
        act_rows = jnp.zeros((plane, tokens_here, model_width), bf16)
        for k in range(plane):
            act_rows = lax.dynamic_update_slice(act_rows, pieces[k][None], (places[k], 0, 0))
        act_rows = act_rows.reshape(plane * tokens_here, model_width)
        used = lax.dynamic_index_in_dim(used_here, planes[s], axis=0, keepdims=False)
        probs_rows = jax.nn.softmax(
            jnp.dot(act_rows, full_router, preferred_element_type=f32), axis=-1
        )
        gate_rows = jnp.sum(probs_rows * mine[None, :], axis=-1, keepdims=True) * used
        gate_pre = jnp.dot(act_rows, gate_w, preferred_element_type=f32)
        up_pre = jnp.dot(act_rows, up_w, preferred_element_type=f32)
        sigmoid = jax.nn.sigmoid(gate_pre)
        swish = gate_pre * sigmoid
        hidden_low = (swish * up_pre).astype(bf16)
        expert_out = jnp.dot(hidden_low, down_w, preferred_element_type=f32).astype(bf16)
        out_low = (gate_rows * expert_out.astype(f32)).astype(bf16)
        forward.append((act_rows, used, gate_rows, gate_pre, up_pre, hidden_low, expert_out, out_low))
    rows_reduce = Reduce()
    choice_rows = jnp.zeros((NZ, plane * tokens_here, 1), f32)
    for s in range(NZ):
        act_rows, used, gate_rows, gate_pre, up_pre, hidden_low, expert_out, _ = forward[s]
        upstream_rows = lax.dynamic_index_in_dim(upstream_all, planes[s], axis=0, keepdims=False)
        if s == NZ - 1:
            upstream_rows, rows_reduce.planes[0] = tie(upstream_rows, rows_reduce.planes[0])
        upstream_f32 = upstream_rows.astype(f32)
        dots = jnp.sum(upstream_f32 * expert_out.astype(f32), axis=-1, keepdims=True) * used
        choice_rows = lax.dynamic_update_slice(choice_rows, dots[None], (planes[s], 0, 0))
        out_grad = (gate_rows * upstream_f32).astype(bf16)
        hidden_grad = times_transposed(out_grad, down_w)
        sigmoid = jax.nn.sigmoid(gate_pre)
        slope = sigmoid * (1.0 + gate_pre * (1.0 - sigmoid))
        gate_pre_grad = (hidden_grad * up_pre * slope).astype(bf16)
        up_pre_grad = (hidden_grad * (gate_pre * sigmoid)).astype(bf16)
        row_grad = (
            times_transposed(gate_pre_grad, gate_w) + times_transposed(up_pre_grad, up_w)
        ).astype(bf16)
        blocks = row_grad.reshape(plane, tokens_here, model_width)
        own, for_x, for_y, across = [
            lax.dynamic_index_in_dim(blocks, places[k], axis=0, keepdims=False)
            for k in range(plane)
        ]
        cut = split_row(tokens_here)
        backward.append((out_grad, gate_pre_grad, up_pre_grad))
        ways = rows_reduce.across(across[:cut], across[cut:])
        if s:
            rows_reduce.finish([s - 1], *opened)
        opened = (own, for_x, for_y, *ways)
    rows_reduce.finish([NZ - 1], *opened)
    choice_grad = lax.all_to_all(
        choice_rows.reshape(owners, tokens_here), "expert", split_axis=0, concat_axis=0, tiled=True
    ).T
    all_outs = jnp.zeros((NZ, plane * tokens_here, model_width), bf16)
    for s in range(NZ):
        all_outs = lax.dynamic_update_slice(all_outs, forward[s][7][None], (planes[s], 0, 0))
    expert_acts = [chunk[0] for chunk in forward]
    gate_grads = [chunk[1] for chunk in backward]
    moe_in_grad = rows_reduce.result()
    own_gate, other_gate = column_grads(
        position, expert_acts, gate_grads, waits=(rows_reduce.planes[3],)
    )
    moe_in_grad, own_gate, all_outs = tie(moe_in_grad, own_gate, all_outs)

    logit_grad = router_probs * (
        choice_grad - jnp.sum(router_probs * choice_grad, axis=-1, keepdims=True)
    )
    logit_low = logit_grad.astype(bf16)
    moe_in_grad = moe_in_grad + times_transposed(logit_low, full_router)
    router_grad = inner_product(act_moe, logit_low)
    upstream = cotangent.astype(f32)
    mid_norm_grad, moe_gain_grad = norm_backward(middle, inverse_moe, moe_gain, moe_in_grad)
    mid_grad = upstream + mid_norm_grad
    mid_low = mid_grad.astype(bf16)
    moe_term = lax.psum_scatter(
        all_outs.reshape(-1, model_width), "expert", scatter_dimension=0, tiled=True
    ).astype(f32)
    own_attended = lax.dynamic_slice_in_dim(attended_low, core * half_width, half_width, axis=1).T
    other_attended = move_core(
        lax.dynamic_slice_in_dim(attended_low, (1 - core) * half_width, half_width, axis=1)
    ).T
    attended_grad = (
        apply_weight(position, mid_low, pieces_vo, rows, 1, back=True)
        .astype(bf16)
        .reshape(head_shape)
    )
    probs_grad = jnp.einsum("qhd,khd->hqk", attended_grad, value_heads, preferred_element_type=f32)
    row_inner = jnp.sum(probs * probs_grad, axis=-1, keepdims=True)
    scores_grad = (probs * (probs_grad - row_inner)).astype(bf16)
    query_rot_grad = (
        jnp.einsum("hqk,khd->qhd", scores_grad, key_rot, preferred_element_type=f32) * score_scale
    )
    key_rot_grad = (
        jnp.einsum("hqk,qhd->khd", scores_grad, query_rot, preferred_element_type=f32) * score_scale
    )
    value_grad = jnp.einsum("hqk,qhd->khd", probs_low, attended_grad, preferred_element_type=f32)
    value_grad = value_grad.reshape(tokens_here, model_width).astype(bf16)
    query_back = rotate_back(query_rot_grad, cosine, sine_table).reshape(tokens_here, model_width)
    key_back = rotate_back(key_rot_grad, cosine, sine_table).reshape(tokens_here, model_width)
    query_pre_grad, query_gain_grad = norm_backward(
        query_pre, query_inverse, query_gain, query_back
    )
    key_pre_grad, key_gain_grad = norm_backward(key_pre, key_inverse, key_gain, key_back)
    query_low = query_pre_grad.astype(bf16)
    key_low = key_pre_grad.astype(bf16)
    attn_grads = []
    for low in (query_low, key_low, value_grad):
        attn_grads += [low, move_core(low)]
    weights_reduce = Reduce()
    turned = [own_act, other_act, own_attended, other_attended]
    attn_grads += [mid_low, move_core(mid_low)]
    lefts = (0, 0, 0, 1)
    first = weight_grad_parts(position, turned, attn_grads, lefts, rows, (1, 2))
    first_ways = weights_reduce.across(*first[3:])
    last = weight_grad_parts(position, turned, attn_grads, lefts, rows, (3, 0))
    last_ways = weights_reduce.across(*last[3:])
    weights_reduce.finish([1, 2], *first[:3], *first_ways)
    act_grad = (
        apply_weight(position, query_low, pieces_qk, rows, 0, back=True, waits=first_ways)
        + apply_weight(position, key_low, pieces_qk, rows, 1, back=True, waits=first_ways)
        + apply_weight(position, value_grad, pieces_vo, rows, 0, back=True, waits=first_ways)
    )
    up_grads = [chunk[2] for chunk in backward]
    own_up, other_up = column_grads(position, expert_acts, up_grads, waits=(act_grad,))
    weights_reduce.push()
    weights_reduce.finish([3, 0], *last[:3], *last_ways, chained=True)
    own_down, other_down = down_grads(
        position,
        [chunk[5] for chunk in forward],
        [chunk[0] for chunk in backward],
        waits=(weights_reduce.planes[1], own_up),
    )
    weight_sums, moe_term = tie(weights_reduce.result(), moe_term)
    query_weight_grad, key_weight_grad, value_weight_grad, output_grad = jnp.split(
        weight_sums, 4, axis=0
    )
    input_norm_grad, attn_gain_grad = norm_backward(inputs_f32, inverse_attn, attn_gain, act_grad)
    input_grad = (mid_grad + input_norm_grad).astype(bf16)

    devices = 2 * owners
    small_grads = jnp.concatenate(
        [
            part.reshape(devices, -1)
            for part in (attn_gain_grad, query_gain_grad, key_gain_grad, moe_gain_grad, router_grad)
        ],
        axis=1,
    )
    small_grads = jnp.sum(
        lax.all_to_all(
            small_grads, ("dp", "expert"), split_axis=0, concat_axis=0, tiled=True
        ),
        axis=0,
    )
    attn_gain_grad, query_gain_grad, key_gain_grad, moe_gain_grad, router_grad = jnp.split(
        small_grads, [rows, 2 * rows, 3 * rows, 4 * rows]
    )

    block_out = (middle + moe_term).astype(bf16)
    down_grad = own_down + move_core(other_down).astype(f32)
    gate_weight_grad = own_gate + move_core(other_gate).astype(f32)
    up_weight_grad = own_up + move_core(other_up).astype(f32)
    return (
        block_out,
        input_grad,
        attn_gain_grad,
        query_weight_grad,
        key_weight_grad,
        value_weight_grad,
        query_gain_grad,
        key_gain_grad,
        output_grad,
        moe_gain_grad,
        router_grad.reshape(w_router.shape),
        gate_weight_grad[None],
        up_weight_grad[None],
        down_grad[None],
    )


def solution(mesh):
    body = body_dense if mesh.shape["expert"] == NZ * NY * NX else body_routed
    return jax.shard_map(
        body,
        mesh=mesh,
        in_specs=(
            P(("dp", "expert"), None),
            P(("dp", "expert"), None),
            P(("dp", "expert"), None),
            P(("dp", "expert"), None),
            P(),
            P(("dp", "expert"), None),
            P(("dp", "expert"), None),
            P(("dp", "expert"), None),
            P(),
            P(),
            P(("dp", "expert"), None),
            P(),
            P(("dp", "expert"), None),
            P("expert", None, None),
            P("expert", None, None),
            P("expert", None, None),
        ),
        out_specs=(
            P(("dp", "expert"), None),
            P(("dp", "expert"), None),
            P(("dp", "expert")),
            P(("dp", "expert"), None),
            P(("dp", "expert"), None),
            P(("dp", "expert"), None),
            P(("dp", "expert")),
            P(("dp", "expert")),
            P(("dp", "expert"), None),
            P(("dp", "expert")),
            P(("dp", "expert"), None),
            P("expert", None, "dp"),
            P("expert", None, "dp"),
            P("expert", "dp", None),
        ),
        check_vma=False,
    )
```

```python
import functools
import itertools

import jax
import jax.numpy as jnp
from jax import lax
from jax.experimental import pallas as pl
from jax.experimental.pallas import tpu as pltpu
from jax.sharding import PartitionSpec as P

HD = 128


EPSILON = 1e-05


def norm_forward(values, gain_vector):
    inverse = lax.rsqrt(jnp.mean(values * values, axis=-1, keepdims=True) + EPSILON)
    return (values * inverse * gain_vector, inverse)


def norm_backward(values, inverse, gain_vector, upstream):
    gain_grad = jnp.sum(upstream * values * inverse, axis=0)
    scaled = upstream * gain_vector
    inner_mean = jnp.mean(scaled * values, axis=-1, keepdims=True)
    return (inverse * (scaled - values * inner_mean * inverse * inverse), gain_grad)


def rotary_tables(length, head_dim):
    half_dim = head_dim // 2
    frequency = 10000.0 ** (-jnp.arange(half_dim, dtype=jnp.float32) * 2.0 / head_dim)
    angles = jnp.arange(length, dtype=jnp.float32)[:, None] * frequency[None, :]
    angles = jnp.concatenate([angles, angles], axis=1)
    return (jnp.cos(angles)[:, None, :], jnp.sin(angles)[:, None, :])


def rotate(values, cosine, sine_table):
    half_dim = values.shape[-1] // 2
    turned = jnp.concatenate([-values[..., half_dim:], values[..., :half_dim]], axis=-1)
    return values * cosine + turned * sine_table


def rotate_back(upstream, cosine, sine_table):
    half_dim = upstream.shape[-1] // 2
    with_sine = upstream * sine_table
    turned = jnp.concatenate([with_sine[..., half_dim:], -with_sine[..., :half_dim]], axis=-1)
    return upstream * cosine + turned


def times_transposed(left, right):
    return jnp.einsum("ta,ba->tb", left, right, preferred_element_type=jnp.float32)


def inner_product(left, right):
    return jnp.einsum("ta,tb->ab", left, right, preferred_element_type=jnp.float32)


def body_routed(
    hidden_in,
    cotangent,
    doc_ids,
    routes,
    attn_gain,
    w_query,
    w_key,
    w_value,
    query_gain,
    key_gain,
    w_output,
    moe_gain,
    w_router,
    w_gate,
    w_up,
    w_down,
):
    f32 = jnp.float32
    bf16 = jnp.bfloat16
    tokens_here = hidden_in.shape[0]
    model_width = hidden_in.shape[1]
    head_dim = HD
    head_count = model_width // head_dim
    top_count = routes.shape[1]
    experts_all = w_router.shape[1]
    capacity = tokens_here * top_count * 4 // (3 * experts_all)
    local_experts = w_gate.shape[0]
    owners = lax.axis_size("expert")
    full_query, full_key, full_value, full_output, full_router = (
        lax.all_gather(w_query, ("dp", "expert"), axis=0, tiled=True),
        lax.all_gather(w_key, ("dp", "expert"), axis=0, tiled=True),
        lax.all_gather(w_value, ("dp", "expert"), axis=0, tiled=True),
        lax.all_gather(w_output, ("dp", "expert"), axis=0, tiled=True),
        lax.all_gather(w_router, ("dp", "expert"), axis=0, tiled=True),
    )
    inputs_f32 = hidden_in.astype(f32)
    normed_attn, inverse_attn = norm_forward(inputs_f32, attn_gain)
    act_attn = normed_attn.astype(bf16)
    query_pre = jnp.dot(act_attn, full_query, preferred_element_type=f32)
    key_pre = jnp.dot(act_attn, full_key, preferred_element_type=f32)
    value_low = jnp.dot(act_attn, full_value, preferred_element_type=f32).astype(bf16)
    query_normed, query_inverse = norm_forward(query_pre, query_gain)
    key_normed, key_inverse = norm_forward(key_pre, key_gain)
    cosine, sine_table = rotary_tables(tokens_here, head_dim)
    head_shape = (tokens_here, head_count, head_dim)
    query_rot = rotate(query_normed.reshape(head_shape), cosine, sine_table).astype(bf16)
    key_rot = rotate(key_normed.reshape(head_shape), cosine, sine_table).astype(bf16)
    value_heads = value_low.reshape(head_shape)
    score_scale = head_dim ** (-0.5)
    position = jnp.arange(tokens_here, dtype=jnp.int32)
    allowed = (position[:, None] >= position[None, :]) & (
        doc_ids[0][:, None] == doc_ids[0][None, :]
    )

    def masked_scores():
        scores = (
            jnp.einsum("qhd,khd->hqk", query_rot, key_rot, preferred_element_type=f32) * score_scale
        )
        return jnp.where(allowed[None], scores, -1e30)

    scores = masked_scores()
    row_max = jnp.max(scores, axis=-1, keepdims=True)
    row_sum = jnp.sum(jnp.exp(scores - row_max), axis=-1, keepdims=True)
    log_total = row_max + jnp.log(row_sum)
    probs_low = jnp.exp(scores - log_total).astype(bf16)
    attended = jnp.einsum("hqk,khd->qhd", probs_low, value_heads, preferred_element_type=f32)
    attended_low = attended.reshape(tokens_here, model_width).astype(bf16)
    middle = inputs_f32 + jnp.dot(attended_low, full_output, preferred_element_type=f32)
    normed_moe, inverse_moe = norm_forward(middle, moe_gain)
    act_moe = normed_moe.astype(bf16)
    logits = jnp.dot(act_moe, full_router, preferred_element_type=f32)
    router_probs = jax.nn.softmax(logits, axis=-1)
    expert_ids = jnp.arange(experts_all, dtype=jnp.int32)
    chosen = routes[:, :, None] == expert_ids[None, None, :]
    gate_values = jnp.sum(jnp.where(chosen, router_probs[:, None, :], 0.0), axis=-1)
    flat_routes = routes.reshape(-1)
    onehot = (flat_routes[:, None] == expert_ids[None, :]).astype(jnp.int32)
    slot_of = jnp.sum((jnp.cumsum(onehot, axis=0) - 1) * onehot, axis=1)
    target_slot = flat_routes * capacity + slot_of
    pair_token = jnp.arange(tokens_here * top_count, dtype=jnp.int32) // top_count

    def to_experts(pair_rows):
        buffer = (
            jnp.zeros((experts_all * capacity, model_width), bf16).at[target_slot].set(pair_rows)
        )
        return buffer.reshape(experts_all, capacity, model_width)

    def from_experts(buffer):
        return buffer.reshape(experts_all * capacity, model_width)[target_slot]

    received = lax.all_to_all(
        to_experts(act_moe[pair_token]), "expert", split_axis=0, concat_axis=0, tiled=True
    )
    owner_rows = received.reshape(owners, local_experts, capacity, model_width)
    gate_pre = jnp.einsum("secd,edf->secf", owner_rows, w_gate, preferred_element_type=f32)
    up_pre = jnp.einsum("secd,edf->secf", owner_rows, w_up, preferred_element_type=f32)
    sigmoid = jax.nn.sigmoid(gate_pre)
    swish = gate_pre * sigmoid
    hidden_low = (swish * up_pre).astype(bf16)
    expert_out = jnp.einsum(
        "secf,efd->secd", hidden_low, w_down, preferred_element_type=f32
    ).astype(bf16)
    returned = lax.all_to_all(
        expert_out.reshape(owners * local_experts, capacity, model_width),
        "expert",
        split_axis=0,
        concat_axis=0,
        tiled=True,
    )
    pair_out = from_experts(returned).reshape(tokens_here, top_count, model_width).astype(f32)
    moe_term = jnp.sum(gate_values[:, :, None] * pair_out, axis=1)
    block_out = (middle + moe_term).astype(bf16)
    upstream = cotangent.astype(f32)
    pair_grad = (gate_values[:, :, None] * upstream[:, None, :]).astype(bf16)
    gate_grad = jnp.sum(upstream[:, None, :] * pair_out, axis=-1)
    out_grad = lax.all_to_all(
        to_experts(pair_grad.reshape(-1, model_width)),
        "expert",
        split_axis=0,
        concat_axis=0,
        tiled=True,
    )
    out_grad = out_grad.reshape(owners, local_experts, capacity, model_width)
    hidden_grad = jnp.einsum("secd,efd->secf", out_grad, w_down, preferred_element_type=f32)
    down_grad = jnp.einsum("secf,secd->efd", hidden_low, out_grad, preferred_element_type=f32)
    slope = sigmoid * (1.0 + gate_pre * (1.0 - sigmoid))
    gate_pre_grad = (hidden_grad * up_pre * slope).astype(bf16)
    up_pre_grad = (hidden_grad * swish).astype(bf16)
    row_grad = jnp.einsum("secf,edf->secd", gate_pre_grad, w_gate, preferred_element_type=f32)
    row_grad = (
        row_grad + jnp.einsum("secf,edf->secd", up_pre_grad, w_up, preferred_element_type=f32)
    ).astype(bf16)
    gate_weight_grad = jnp.einsum(
        "secd,secf->edf", owner_rows, gate_pre_grad, preferred_element_type=f32
    )
    up_weight_grad = jnp.einsum(
        "secd,secf->edf", owner_rows, up_pre_grad, preferred_element_type=f32
    )
    gate_weight_grad, up_weight_grad, down_grad = (
        lax.psum_scatter(
            gate_weight_grad.astype(jnp.bfloat16), "dp", scatter_dimension=2, tiled=True
        ).astype(jnp.float32),
        lax.psum_scatter(
            up_weight_grad.astype(jnp.bfloat16), "dp", scatter_dimension=2, tiled=True
        ).astype(jnp.float32),
        lax.psum_scatter(
            down_grad.astype(jnp.bfloat16), "dp", scatter_dimension=1, tiled=True
        ).astype(jnp.float32),
    )
    back_rows = lax.all_to_all(
        row_grad.reshape(owners * local_experts, capacity, model_width),
        "expert",
        split_axis=0,
        concat_axis=0,
        tiled=True,
    )
    moe_in_grad = jnp.sum(
        from_experts(back_rows).reshape(tokens_here, top_count, model_width).astype(f32), axis=1
    )
    choice_grad = jnp.sum(jnp.where(chosen, gate_grad[:, :, None], 0.0), axis=1)
    logit_grad = router_probs * (
        choice_grad - jnp.sum(router_probs * choice_grad, axis=-1, keepdims=True)
    )
    logit_low = logit_grad.astype(bf16)
    moe_in_grad = moe_in_grad + times_transposed(logit_low, full_router)
    router_grad = inner_product(act_moe, logit_low)
    mid_norm_grad, moe_gain_grad = norm_backward(middle, inverse_moe, moe_gain, moe_in_grad)
    mid_grad = upstream + mid_norm_grad
    mid_low = mid_grad.astype(bf16)
    output_grad = inner_product(attended_low, mid_low)
    attended_grad = times_transposed(mid_low, full_output).astype(bf16).reshape(head_shape)
    probs = jnp.exp(masked_scores() - log_total)
    probs_grad = jnp.einsum("qhd,khd->hqk", attended_grad, value_heads, preferred_element_type=f32)
    row_inner = jnp.sum(probs * probs_grad, axis=-1, keepdims=True)
    scores_grad = (probs * (probs_grad - row_inner)).astype(bf16)
    query_rot_grad = (
        jnp.einsum("hqk,khd->qhd", scores_grad, key_rot, preferred_element_type=f32) * score_scale
    )
    key_rot_grad = (
        jnp.einsum("hqk,qhd->khd", scores_grad, query_rot, preferred_element_type=f32) * score_scale
    )
    value_grad = jnp.einsum("hqk,qhd->khd", probs_low, attended_grad, preferred_element_type=f32)
    value_grad = value_grad.reshape(tokens_here, model_width).astype(bf16)
    query_back = rotate_back(query_rot_grad, cosine, sine_table).reshape(tokens_here, model_width)
    key_back = rotate_back(key_rot_grad, cosine, sine_table).reshape(tokens_here, model_width)
    query_pre_grad, query_gain_grad = norm_backward(
        query_pre, query_inverse, query_gain, query_back
    )
    key_pre_grad, key_gain_grad = norm_backward(key_pre, key_inverse, key_gain, key_back)
    query_low = query_pre_grad.astype(bf16)
    key_low = key_pre_grad.astype(bf16)
    act_grad = (
        times_transposed(query_low, full_query)
        + times_transposed(key_low, full_key)
        + times_transposed(value_grad, full_value)
    )
    query_weight_grad = inner_product(act_attn, query_low)
    key_weight_grad = inner_product(act_attn, key_low)
    value_weight_grad = inner_product(act_attn, value_grad)
    input_norm_grad, attn_gain_grad = norm_backward(inputs_f32, inverse_attn, attn_gain, act_grad)
    input_grad = (mid_grad + input_norm_grad).astype(bf16)
    sharded_grads = (
        lax.psum_scatter(attn_gain_grad, ("dp", "expert"), scatter_dimension=0, tiled=True),
        lax.psum_scatter(query_weight_grad, ("dp", "expert"), scatter_dimension=0, tiled=True),
        lax.psum_scatter(key_weight_grad, ("dp", "expert"), scatter_dimension=0, tiled=True),
        lax.psum_scatter(value_weight_grad, ("dp", "expert"), scatter_dimension=0, tiled=True),
        lax.psum_scatter(query_gain_grad, ("dp", "expert"), scatter_dimension=0, tiled=True),
        lax.psum_scatter(key_gain_grad, ("dp", "expert"), scatter_dimension=0, tiled=True),
        lax.psum_scatter(output_grad, ("dp", "expert"), scatter_dimension=0, tiled=True),
        lax.psum_scatter(moe_gain_grad, ("dp", "expert"), scatter_dimension=0, tiled=True),
        lax.psum_scatter(router_grad, ("dp", "expert"), scatter_dimension=0, tiled=True),
    )
    return (
        block_out,
        input_grad,
        sharded_grads[0],
        sharded_grads[1],
        sharded_grads[2],
        sharded_grads[3],
        sharded_grads[4],
        sharded_grads[5],
        sharded_grads[6],
        sharded_grads[7],
        sharded_grads[8],
        gate_weight_grad,
        up_weight_grad,
        down_grad,
    )


NZ, NY, NX = 4, 2, 2
VMEM_LIMIT = 48 * 1024 * 1024
EXPERT_VMEM = 60 * 1024 * 1024


def chip(z, y, x):
    return (z * NY + y) * NX + x


GRID = [(z, y, x) for z in range(NZ) for y in range(NY) for x in range(NX)]
X_PAIRS = [(chip(z, y, x), chip(z, y, 1 - x)) for z, y, x in GRID]
Y_PAIRS = [(chip(z, y, x), chip(z, 1 - y, x)) for z, y, x in GRID]
Z_PAIRS = [(chip(z, y, x), chip((z + 1) % NZ, y, x)) for z, y, x in GRID]
CORE_PAIRS = [(0, 1), (1, 0)]


def move_x(values):
    return lax.ppermute(values, "expert", X_PAIRS)


def move_y(values):
    return lax.ppermute(values, "expert", Y_PAIRS)


def move_z(values):
    return lax.ppermute(values, "expert", Z_PAIRS)


def move_core(values):
    return lax.ppermute(values, "dp", CORE_PAIRS)


def split_row(rows):
    return (rows // 2 + 15) // 16 * 16


def tie(*values):
    return lax.optimization_barrier(values)


def without(kernel, start, count):
    return lambda *refs: kernel(*refs[:start], *refs[start + count :])


def gather_z(block):
    ring = [block]
    for _ in range(1, NZ):
        ring.append(move_z(ring[-1]))
    return ring


def gather_plane(block):
    cut = split_row(block.shape[0])
    from_x = move_x(block)
    from_y = move_y(block)
    across = jnp.concatenate([move_x(from_y[:cut]), move_y(from_x[cut:])], axis=0)
    return [block, from_x, from_y, across]


def gather_chips(block):
    return [gather_plane(part) for part in gather_z(block)]


def add_f32(left, right):
    return left.astype(jnp.float32) + right.astype(jnp.float32)


class Reduce:
    def __init__(self):
        self.planes, self.steps, self.total = {}, 0, None

    def across(self, low, high):
        return move_x(low), move_y(high)

    def finish(self, steps, own, for_x, for_y, by_x, by_y, chained=False):
        low = own.dtype
        cut = by_x.shape[0]
        for_y = jnp.concatenate([add_f32(for_y[:cut], by_x).astype(low), for_y[cut:]], axis=0)
        for_x = jnp.concatenate([for_x[:cut], add_f32(for_x[cut:], by_y).astype(low)], axis=0)
        from_x, from_y = move_x(for_x), move_y(for_y)
        if chained:
            from_x, from_y, self.total = tie(from_x, from_y, self.total)
        total = add_f32(own, from_x) + from_y.astype(jnp.float32)
        for step, part in zip(steps, jnp.split(total, len(steps), axis=0), strict=True):
            self.planes[step] = part

    def push(self, before=None):
        while self.steps + 1 < NZ and self.steps + 1 in self.planes:
            self.steps += 1
            total = self.planes[self.steps]
            if self.total is not None:
                total = add_f32(self.total, total)
            total = total.astype(jnp.bfloat16)
            if before is not None and self.steps == NZ - 1:
                total, before = tie(total, before)
            self.total = move_z(total)
        return before

    def result(self):
        self.push()
        return add_f32(self.total, self.planes[0])


def place_of(position, k):
    return (position[2] ^ (k >> 1)) * NX + (position[3] ^ (k & 1))


def weight_copies(position, pieces, rows, slot, held, sems, other):
    out = []
    for step in range(NZ):
        z_of = (position[1] + NZ - step) % NZ
        for k in range(NY * NX):
            place = pl.multiple_of((z_of * NY * NX + place_of(position, k)) * rows, rows)
            out.append(
                pltpu.make_async_copy(
                    pieces[other * NZ + step].at[k, pl.ds(slot * rows, rows)],
                    held.at[other, pl.ds(place, rows)],
                    sems.at[other * NZ + step, k],
                )
            )
    return out


def apply_kernel(position, acts, *refs, rows, slot, tile):
    pieces, (out, held, sems) = refs[: 2 * NZ], refs[2 * NZ :]
    for other in range(2):
        for copy in weight_copies(position, pieces, rows, slot, held, sems, other):
            copy.start()
    span = held.shape[1]
    for other in range(2):
        for copy in weight_copies(position, pieces, rows, slot, held, sems, other):
            copy.wait()
        left = acts[:, pl.ds(pl.multiple_of((position[0] ^ other) * span, span), span)]

        @pl.loop(0, out.shape[1] // tile)
        def _(i):
            columns = pl.ds(pl.multiple_of(i * tile, tile), tile)
            part = jnp.dot(left, held[other, :, columns], preferred_element_type=jnp.float32)
            if other == 0:
                out[:, columns] = part
            else:
                out[:, columns] += part


def apply_back_kernel(position, grads, *refs, rows, slot, tile):
    pieces, (out, held, sems) = refs[: 2 * NZ], refs[2 * NZ :]
    for other in range(2):
        for copy in weight_copies(position, pieces, rows, slot, held, sems, other):
            copy.start()
    span = held.shape[1]
    for other in range(2):
        for copy in weight_copies(position, pieces, rows, slot, held, sems, other):
            copy.wait()

        @pl.loop(0, span // tile)
        def _(i):
            lines = pl.ds(pl.multiple_of(i * tile, tile), tile)
            low = pl.multiple_of((position[0] ^ other) * span + i * tile, tile)
            out[:, pl.ds(low, tile)] = lax.dot_general(
                grads[...],
                held[other, lines, :],
                (((1,), (1,)), ((), ())),
                preferred_element_type=jnp.float32,
            )


def apply_weight(position, values, pieces, rows, slot, back=False, waits=()):
    tokens, width = values.shape
    return pl.pallas_call(
        without(
            functools.partial(
                apply_back_kernel if back else apply_kernel, rows=rows, slot=slot, tile=512
            ),
            2 + len(pieces),
            len(waits),
        ),
        out_shape=jax.ShapeDtypeStruct((tokens, width), jnp.float32),
        in_specs=[pl.BlockSpec(memory_space=pltpu.SMEM), pl.BlockSpec(memory_space=pltpu.VMEM)]
        + [pl.BlockSpec(memory_space=pl.ANY)] * (len(pieces) + len(waits)),
        out_specs=pl.BlockSpec(memory_space=pltpu.VMEM),
        scratch_shapes=[
            pltpu.VMEM((2, width // 2, width), jnp.bfloat16),
            pltpu.SemaphoreType.DMA((2 * NZ, NY * NX)),
        ],
        compiler_params=pltpu.CompilerParams(vmem_limit_bytes=VMEM_LIMIT),
        cost_estimate=pl.CostEstimate(
            flops=2 * tokens * width * width,
            bytes_accessed=2 * width * width + 6 * tokens * width,
            transcendentals=0,
        ),
    )(position, values, *pieces, *waits)


def weight_grad_kernel(position, *refs, rows, lefts, steps, tile):
    count = len(lefts)
    turned, grads = refs[: 2 * max(lefts) + 2], refs[2 * max(lefts) + 2 :]
    grads, (own, for_x, for_y, *across, stage) = grads[: 2 * count], grads[2 * count :]
    span = NY * NX * rows
    for p, step in enumerate(steps):
        z_of = (position[1] + NZ - step) % NZ
        lines = pl.ds(pl.multiple_of(z_of * span, span), span)
        for i, left in enumerate(lefts):
            low = p * count * rows + i * rows
            targets = [(own, low), (for_x, low), (for_y, low), (across[p], i * rows)]

            @pl.loop(0, grads[0].shape[1] // tile)
            def _(j):
                part = pl.ds(pl.multiple_of(j * tile, tile), tile)
                product = jnp.dot(
                    turned[2 * left][lines, :],
                    grads[2 * i][:, part],
                    preferred_element_type=jnp.float32,
                ) + jnp.dot(
                    turned[2 * left + 1][lines, :],
                    grads[2 * i + 1][:, part],
                    preferred_element_type=jnp.float32,
                )
                stage[...] = product.astype(stage.dtype)
                for k, (target, at) in enumerate(targets):
                    place = pl.multiple_of(place_of(position, k) * rows, rows)
                    target[pl.ds(at, rows), part] = stage[pl.ds(place, rows), :]


def weight_grad_parts(position, turned, grads, lefts, rows, steps, waits=()):
    count, width = len(lefts), grads[0].shape[1]
    tokens, tile = turned[0].shape[1], 512
    vmem_spec = pl.BlockSpec(memory_space=pltpu.VMEM)
    both = jax.ShapeDtypeStruct((2 * count * rows, width), jnp.bfloat16)
    one = jax.ShapeDtypeStruct((count * rows, width), jnp.bfloat16)
    operands = [*turned, *grads]
    return pl.pallas_call(
        without(
            functools.partial(weight_grad_kernel, rows=rows, lefts=lefts, steps=steps, tile=tile),
            1 + len(operands),
            len(waits),
        ),
        out_shape=[both] * 3 + [one] * 2,
        in_specs=[pl.BlockSpec(memory_space=pltpu.SMEM)]
        + [vmem_spec] * len(operands)
        + [pl.BlockSpec(memory_space=pl.ANY)] * len(waits),
        out_specs=[vmem_spec] * 5,
        scratch_shapes=[pltpu.VMEM((NY * NX * rows, tile), jnp.bfloat16)],
        compiler_params=pltpu.CompilerParams(vmem_limit_bytes=VMEM_LIMIT),
        cost_estimate=pl.CostEstimate(
            flops=8 * count * tokens * NY * NX * rows * width,
            bytes_accessed=4 * count * NY * NX * rows * width + 4 * tokens * width * (count + 1),
            transcendentals=0,
        ),
    )(position, *operands, *waits)


def column_grad_kernel(position, *refs):
    parts = (len(refs) - 2) // 2
    acts, grads, outs = refs[:parts], refs[parts:-2], refs[-2:]
    half = outs[0].shape[1]
    turned = [act[...].T for act in acts]
    for side, out in enumerate(outs):
        columns = pl.ds(pl.multiple_of((position[0] ^ side) * half, half), half)
        total = None
        for act, grad in zip(turned, grads, strict=True):
            more = jnp.dot(act, grad[:, columns], preferred_element_type=jnp.float32)
            total = more if total is None else total + more
        out[...] = total.astype(out.dtype)


def column_grads(position, acts, grads, waits=()):
    parts = len(acts)
    count, width = acts[0].shape
    units = grads[0].shape[1]
    tile = 256
    whole = pl.BlockSpec((count, units), lambda i: (0, 0), pipeline_mode=pl.Buffered(1))
    out = pl.BlockSpec((tile, units // 2), lambda i: (i, 0))
    return pl.pallas_call(
        without(column_grad_kernel, 1 + 2 * parts, len(waits)),
        grid=(width // tile,),
        out_shape=[jax.ShapeDtypeStruct((width, units // 2), t) for t in (jnp.float32, jnp.bfloat16)],
        in_specs=[pl.BlockSpec(memory_space=pltpu.SMEM)]
        + [pl.BlockSpec((count, tile), lambda i: (0, i))] * parts
        + [whole] * parts
        + [pl.BlockSpec(memory_space=pl.ANY)] * len(waits),
        out_specs=[out] * 2,
        compiler_params=pltpu.CompilerParams(vmem_limit_bytes=EXPERT_VMEM),
        cost_estimate=pl.CostEstimate(
            flops=2 * parts * count * width * units,
            bytes_accessed=2 * parts * count * (width + units) + 3 * width * units,
            transcendentals=0,
        ),
    )(position, *acts, *grads, *waits)


def down_grad_kernel(position, *refs):
    parts = (len(refs) - 3) // 2
    hiddens, grads, (own, other, turned) = refs[:parts], refs[parts:-3], refs[-3:]
    tile = 512
    for s, hidden in enumerate(hiddens):
        turned[s] = hidden[...].T

    def part_of(j):
        columns = pl.ds(pl.multiple_of(j * tile, tile), tile)
        total = None
        for s, grad in enumerate(grads):
            more = jnp.dot(turned[s], grad[:, columns], preferred_element_type=jnp.float32)
            total = more if total is None else total + more
        return columns, total

    steps = grads[0].shape[1] // tile

    @pl.when(pl.program_id(0) < pl.num_programs(0) // 2)
    def _():
        @pl.loop(0, steps)
        def _(j):
            columns, total = part_of(j)
            own[:, columns] = total

    @pl.when(pl.program_id(0) >= pl.num_programs(0) // 2)
    def _():
        @pl.loop(0, steps)
        def _(j):
            columns, total = part_of(j)
            other[:, columns] = total.astype(other.dtype)


def down_grads(position, hiddens, grads, waits=()):
    parts = len(hiddens)
    count, units = hiddens[0].shape
    width = grads[0].shape[1]
    tile = 256
    half = units // 2 // tile
    whole = pl.BlockSpec((count, width), lambda i, at: (0, 0), pipeline_mode=pl.Buffered(1))
    return pl.pallas_call(
        without(down_grad_kernel, 1 + 2 * parts, len(waits)),
        grid_spec=pltpu.PrefetchScalarGridSpec(
            num_scalar_prefetch=1,
            grid=(2 * half,),
            in_specs=[
                pl.BlockSpec((count, tile), lambda i, at: (0, (i + at[0] * half) % (2 * half)))
            ]
            * parts
            + [whole] * parts
            + [pl.BlockSpec(memory_space=pl.ANY)] * len(waits),
            out_specs=[
                pl.BlockSpec((tile, width), lambda i, at: (jnp.minimum(i, half - 1), 0)),
                pl.BlockSpec((tile, width), lambda i, at: (jnp.maximum(i - half, 0), 0)),
            ],
            scratch_shapes=[pltpu.VMEM((parts, tile, count), jnp.bfloat16)],
        ),
        out_shape=[
            jax.ShapeDtypeStruct((units // 2, width), jnp.float32),
            jax.ShapeDtypeStruct((units // 2, width), jnp.bfloat16),
        ],
        compiler_params=pltpu.CompilerParams(vmem_limit_bytes=EXPERT_VMEM),
        cost_estimate=pl.CostEstimate(
            flops=2 * parts * count * width * units,
            bytes_accessed=2 * parts * count * (width + units) + 3 * width * units,
            transcendentals=0,
        ),
    )(position, *hiddens, *grads, *waits)


def gather_weights(blocks):
    ring = [jnp.stack(part) for part in gather_chips(jnp.concatenate(blocks, axis=0))]
    return ring + [move_core(part) for part in ring]


def body_dense(
    hidden_in,
    cotangent,
    doc_ids,
    routes,
    attn_gain,
    w_query,
    w_key,
    w_value,
    query_gain,
    key_gain,
    w_output,
    moe_gain,
    w_router,
    w_gate,
    w_up,
    w_down,
):
    f32 = jnp.float32
    bf16 = jnp.bfloat16
    tokens_here, model_width = hidden_in.shape
    head_dim = HD
    head_count = model_width // head_dim
    rows = w_query.shape[0]
    experts_all = w_router.shape[1]
    owners = lax.axis_size("expert")
    core = lax.axis_index("dp")
    here = lax.axis_index("expert")
    z_at, y_at, x_at = here // (NY * NX), here // NX % NY, here % NX
    position = jnp.stack([core, z_at, y_at, x_at, here]).astype(jnp.int32)
    half_width = model_width // 2
    plane = NY * NX
    places = [(y_at ^ (k >> 1)) * NX + (x_at ^ (k & 1)) for k in range(plane)]
    planes = [(z_at + NZ - s) % NZ for s in range(NZ)]

    pieces_qk = gather_weights([w_query, w_key])
    pieces_vo = gather_weights([w_value, w_output])
    upstream, pieces_vo[0] = tie(cotangent, pieces_vo[0])
    upstream_all = lax.all_gather(
        upstream, "expert", axis=0, tiled=True
    ).reshape(NZ, plane * tokens_here, model_width)

    expert_ids = jnp.arange(experts_all, dtype=jnp.int32)
    chosen = routes[:, :, None] == expert_ids[None, None, :]
    uses = jnp.any(chosen, axis=1).astype(f32)
    router_block = jnp.broadcast_to(w_router.astype(f32).reshape(1, -1), (owners, w_router.size))
    small = jnp.concatenate([uses.T, router_block], axis=1)
    small = lax.all_to_all(
        small, "expert", split_axis=0, concat_axis=0, tiled=True
    )
    used_here = small[:, :tokens_here].reshape(NZ, plane * tokens_here, 1)
    own_router = small[:, tokens_here:].reshape(-1, experts_all)
    other_router = move_core(own_router)
    full_router = jnp.where(
        core == 0,
        jnp.concatenate([own_router, other_router], axis=0),
        jnp.concatenate([other_router, own_router], axis=0),
    ).astype(bf16)

    inputs_f32 = hidden_in.astype(f32)
    normed_attn, inverse_attn = norm_forward(inputs_f32, attn_gain)
    act_attn = normed_attn.astype(bf16)
    own_act = lax.dynamic_slice_in_dim(act_attn, core * half_width, half_width, axis=1).T
    other_act = move_core(
        lax.dynamic_slice_in_dim(act_attn, (1 - core) * half_width, half_width, axis=1)
    ).T
    query_pre = apply_weight(position, act_attn, pieces_qk, rows, 0)
    key_pre = apply_weight(position, act_attn, pieces_qk, rows, 1)
    value_low = apply_weight(
        position, act_attn, pieces_vo, rows, 0, waits=(small,)
    ).astype(bf16)
    query_normed, query_inverse = norm_forward(query_pre, query_gain)
    key_normed, key_inverse = norm_forward(key_pre, key_gain)
    cosine, sine_table = rotary_tables(tokens_here, head_dim)
    head_shape = (tokens_here, head_count, head_dim)
    query_rot = rotate(query_normed.reshape(head_shape), cosine, sine_table).astype(bf16)
    key_rot = rotate(key_normed.reshape(head_shape), cosine, sine_table).astype(bf16)
    value_heads = value_low.reshape(head_shape)
    score_scale = head_dim ** (-0.5)
    token_at = jnp.arange(tokens_here, dtype=jnp.int32)
    allowed = (token_at[:, None] >= token_at[None, :]) & (
        doc_ids[0][:, None] == doc_ids[0][None, :]
    )
    scores = (
        jnp.einsum("qhd,khd->hqk", query_rot, key_rot, preferred_element_type=f32) * score_scale
    )
    scores = jnp.where(allowed[None], scores, -1e30)
    row_max = jnp.max(scores, axis=-1, keepdims=True)
    row_sum = jnp.sum(jnp.exp(scores - row_max), axis=-1, keepdims=True)
    log_total = row_max + jnp.log(row_sum)
    probs = jnp.exp(scores - log_total)
    probs_low = probs.astype(bf16)
    attended = jnp.einsum("hqk,khd->qhd", probs_low, value_heads, preferred_element_type=f32)
    attended_low = attended.reshape(tokens_here, model_width).astype(bf16)
    middle = inputs_f32 + apply_weight(position, attended_low, pieces_vo, rows, 1)
    normed_moe, inverse_moe = norm_forward(middle, moe_gain)
    act_moe = normed_moe.astype(bf16)

    logits = jnp.dot(act_moe, full_router, preferred_element_type=f32)
    router_probs = jax.nn.softmax(logits, axis=-1)

    gate_w, up_w, down_w = w_gate[0], w_up[0], w_down[0]
    mine = (expert_ids == here).astype(f32)
    forward, backward = [], []
    for s, pieces in enumerate(gather_chips(act_moe)):
        act_rows = jnp.zeros((plane, tokens_here, model_width), bf16)
        for k in range(plane):
            act_rows = lax.dynamic_update_slice(act_rows, pieces[k][None], (places[k], 0, 0))
        act_rows = act_rows.reshape(plane * tokens_here, model_width)
        used = lax.dynamic_index_in_dim(used_here, planes[s], axis=0, keepdims=False)
        probs_rows = jax.nn.softmax(
            jnp.dot(act_rows, full_router, preferred_element_type=f32), axis=-1
        )
        gate_rows = jnp.sum(probs_rows * mine[None, :], axis=-1, keepdims=True) * used
        gate_pre = jnp.dot(act_rows, gate_w, preferred_element_type=f32)
        up_pre = jnp.dot(act_rows, up_w, preferred_element_type=f32)
        sigmoid = jax.nn.sigmoid(gate_pre)
        swish = gate_pre * sigmoid
        hidden_low = (swish * up_pre).astype(bf16)
        expert_out = jnp.dot(hidden_low, down_w, preferred_element_type=f32).astype(bf16)
        out_low = (gate_rows * expert_out.astype(f32)).astype(bf16)
        forward.append((act_rows, used, gate_rows, gate_pre, up_pre, hidden_low, expert_out, out_low))
    rows_reduce = Reduce()
    choice_rows = jnp.zeros((NZ, plane * tokens_here, 1), f32)
    for s in range(NZ):
        act_rows, used, gate_rows, gate_pre, up_pre, hidden_low, expert_out, _ = forward[s]
        upstream_rows = lax.dynamic_index_in_dim(upstream_all, planes[s], axis=0, keepdims=False)
        if s == NZ - 1:
            upstream_rows, rows_reduce.planes[0] = tie(upstream_rows, rows_reduce.planes[0])
        upstream_f32 = upstream_rows.astype(f32)
        dots = jnp.sum(upstream_f32 * expert_out.astype(f32), axis=-1, keepdims=True) * used
        choice_rows = lax.dynamic_update_slice(choice_rows, dots[None], (planes[s], 0, 0))
        out_grad = (gate_rows * upstream_f32).astype(bf16)
        hidden_grad = times_transposed(out_grad, down_w)
        sigmoid = jax.nn.sigmoid(gate_pre)
        slope = sigmoid * (1.0 + gate_pre * (1.0 - sigmoid))
        gate_pre_grad = (hidden_grad * up_pre * slope).astype(bf16)
        up_pre_grad = (hidden_grad * (gate_pre * sigmoid)).astype(bf16)
        row_grad = (
            times_transposed(gate_pre_grad, gate_w) + times_transposed(up_pre_grad, up_w)
        ).astype(bf16)
        blocks = row_grad.reshape(plane, tokens_here, model_width)
        own, for_x, for_y, across = [
            lax.dynamic_index_in_dim(blocks, places[k], axis=0, keepdims=False)
            for k in range(plane)
        ]
        cut = split_row(tokens_here)
        backward.append((out_grad, gate_pre_grad, up_pre_grad))
        ways = rows_reduce.across(across[:cut], across[cut:])
        if s:
            rows_reduce.finish([s - 1], *opened)
        opened = (own, for_x, for_y, *ways)
    rows_reduce.finish([NZ - 1], *opened)
    choice_grad = lax.all_to_all(
        choice_rows.reshape(owners, tokens_here), "expert", split_axis=0, concat_axis=0, tiled=True
    ).T
    all_outs = jnp.zeros((NZ, plane * tokens_here, model_width), bf16)
    for s in range(NZ):
        all_outs = lax.dynamic_update_slice(all_outs, forward[s][7][None], (planes[s], 0, 0))
    expert_acts = [chunk[0] for chunk in forward]
    gate_grads = [chunk[1] for chunk in backward]
    choice_grad = rows_reduce.push(choice_grad)
    moe_in_grad = rows_reduce.result()
    own_gate, other_gate = column_grads(
        position, expert_acts, gate_grads, waits=(rows_reduce.planes[3],)
    )
    moe_in_grad, own_gate, all_outs = tie(moe_in_grad, own_gate, all_outs)

    logit_grad = router_probs * (
        choice_grad - jnp.sum(router_probs * choice_grad, axis=-1, keepdims=True)
    )
    logit_low = logit_grad.astype(bf16)
    moe_in_grad = moe_in_grad + times_transposed(logit_low, full_router)
    router_grad = inner_product(act_moe, logit_low)
    upstream = cotangent.astype(f32)
    mid_norm_grad, moe_gain_grad = norm_backward(middle, inverse_moe, moe_gain, moe_in_grad)
    mid_grad = upstream + mid_norm_grad
    mid_low = mid_grad.astype(bf16)
    moe_term = lax.psum_scatter(
        all_outs.reshape(-1, model_width), "expert", scatter_dimension=0, tiled=True
    ).astype(f32)
    own_attended = lax.dynamic_slice_in_dim(attended_low, core * half_width, half_width, axis=1).T
    other_attended = move_core(
        lax.dynamic_slice_in_dim(attended_low, (1 - core) * half_width, half_width, axis=1)
    ).T
    attended_grad = (
        apply_weight(position, mid_low, pieces_vo, rows, 1, back=True)
        .astype(bf16)
        .reshape(head_shape)
    )
    probs_grad = jnp.einsum("qhd,khd->hqk", attended_grad, value_heads, preferred_element_type=f32)
    row_inner = jnp.sum(probs * probs_grad, axis=-1, keepdims=True)
    scores_grad = (probs * (probs_grad - row_inner)).astype(bf16)
    query_rot_grad = (
        jnp.einsum("hqk,khd->qhd", scores_grad, key_rot, preferred_element_type=f32) * score_scale
    )
    key_rot_grad = (
        jnp.einsum("hqk,qhd->khd", scores_grad, query_rot, preferred_element_type=f32) * score_scale
    )
    value_grad = jnp.einsum("hqk,qhd->khd", probs_low, attended_grad, preferred_element_type=f32)
    value_grad = value_grad.reshape(tokens_here, model_width).astype(bf16)
    query_back = rotate_back(query_rot_grad, cosine, sine_table).reshape(tokens_here, model_width)
    key_back = rotate_back(key_rot_grad, cosine, sine_table).reshape(tokens_here, model_width)
    query_pre_grad, query_gain_grad = norm_backward(
        query_pre, query_inverse, query_gain, query_back
    )
    key_pre_grad, key_gain_grad = norm_backward(key_pre, key_inverse, key_gain, key_back)
    query_low = query_pre_grad.astype(bf16)
    key_low = key_pre_grad.astype(bf16)
    attn_grads = []
    for low in (query_low, key_low, value_grad):
        attn_grads += [low, move_core(low)]
    weights_reduce = Reduce()
    turned = [own_act, other_act, own_attended, other_attended]
    attn_grads += [mid_low, move_core(mid_low)]
    lefts = (0, 0, 0, 1)
    first = weight_grad_parts(position, turned, attn_grads, lefts, rows, (1, 2))
    first_ways = weights_reduce.across(*first[3:])
    last = weight_grad_parts(position, turned, attn_grads, lefts, rows, (3, 0))
    last_ways = weights_reduce.across(*last[3:])
    weights_reduce.finish([1, 2], *first[:3], *first_ways)
    act_grad = (
        apply_weight(position, query_low, pieces_qk, rows, 0, back=True, waits=first_ways)
        + apply_weight(position, key_low, pieces_qk, rows, 1, back=True, waits=first_ways)
        + apply_weight(position, value_grad, pieces_vo, rows, 0, back=True, waits=first_ways)
    )
    up_grads = [chunk[2] for chunk in backward]
    own_up, other_up = column_grads(position, expert_acts, up_grads, waits=(act_grad,))
    weights_reduce.push()
    weights_reduce.finish([3, 0], *last[:3], *last_ways, chained=True)
    own_down, other_down = down_grads(
        position,
        [chunk[5] for chunk in forward],
        [chunk[0] for chunk in backward],
        waits=(weights_reduce.planes[1], own_up),
    )
    weight_sums, moe_term = tie(weights_reduce.result(), moe_term)
    query_weight_grad, key_weight_grad, value_weight_grad, output_grad = jnp.split(
        weight_sums, 4, axis=0
    )
    input_norm_grad, attn_gain_grad = norm_backward(inputs_f32, inverse_attn, attn_gain, act_grad)
    input_grad = (mid_grad + input_norm_grad).astype(bf16)

    devices = 2 * owners
    small_grads = jnp.concatenate(
        [
            part.reshape(devices, -1)
            for part in (attn_gain_grad, query_gain_grad, key_gain_grad, moe_gain_grad, router_grad)
        ],
        axis=1,
    )
    small_grads = jnp.sum(
        lax.all_to_all(
            small_grads, ("dp", "expert"), split_axis=0, concat_axis=0, tiled=True
        ),
        axis=0,
    )
    attn_gain_grad, query_gain_grad, key_gain_grad, moe_gain_grad, router_grad = jnp.split(
        small_grads, [rows, 2 * rows, 3 * rows, 4 * rows]
    )

    block_out = (middle + moe_term).astype(bf16)
    down_grad = own_down + move_core(other_down).astype(f32)
    gate_weight_grad = own_gate + move_core(other_gate).astype(f32)
    up_weight_grad = own_up + move_core(other_up).astype(f32)
    return (
        block_out,
        input_grad,
        attn_gain_grad,
        query_weight_grad,
        key_weight_grad,
        value_weight_grad,
        query_gain_grad,
        key_gain_grad,
        output_grad,
        moe_gain_grad,
        router_grad.reshape(w_router.shape),
        gate_weight_grad[None],
        up_weight_grad[None],
        down_grad[None],
    )


def solution(mesh):
    body = body_dense if mesh.shape["expert"] == NZ * NY * NX else body_routed
    return jax.shard_map(
        body,
        mesh=mesh,
        in_specs=(
            P(("dp", "expert"), None),
            P(("dp", "expert"), None),
            P(("dp", "expert"), None),
            P(("dp", "expert"), None),
            P(),
            P(("dp", "expert"), None),
            P(("dp", "expert"), None),
            P(("dp", "expert"), None),
            P(),
            P(),
            P(("dp", "expert"), None),
            P(),
            P(("dp", "expert"), None),
            P("expert", None, None),
            P("expert", None, None),
            P("expert", None, None),
        ),
        out_specs=(
            P(("dp", "expert"), None),
            P(("dp", "expert"), None),
            P(("dp", "expert")),
            P(("dp", "expert"), None),
            P(("dp", "expert"), None),
            P(("dp", "expert"), None),
            P(("dp", "expert")),
            P(("dp", "expert")),
            P(("dp", "expert"), None),
            P(("dp", "expert")),
            P(("dp", "expert"), None),
            P("expert", None, "dp"),
            P("expert", None, "dp"),
            P("expert", "dp", None),
        ),
        check_vma=False,
    )
```
